512 devices in a mesh: dp: 32 (over x, z_lo, core), tensor: 16 (over y, z_hi).
Axes of the slice: x: 4, y: 4, z: 16 (z_hi: 4, z_lo: 4; z = z_hi * 4 + z_lo), core: 2. Of those that a mesh axis runs over, the one named last changes fastest.
Arguments:
- gate_logits: bfloat16 [16384, 14336], P('dp', 'tensor'), may hold values from -6 to 6
- up_projected: bfloat16 [16384, 14336], P('dp', 'tensor'), may hold values from -6 to 6
- output_gradient: bfloat16 [16384, 4096], P('dp', 'tensor'), may hold values from -6 to 6
- down_matrix: bfloat16 [14336, 4096], P('tensor', 'dp'), may hold values from -0.046875 to 0.046875
- adapter_input_factors: float32 [32, 16, 14336], P('dp', None, 'tensor'), may hold values from -0.046875 to 0.046875
- adapter_output_factors: float32 [32, 16, 4096], P('dp', None, 'tensor'), may hold values from -0.375 to 0.375
- input_moments: float32 [2, 32, 16, 14336], P(None, 'dp', None, 'tensor'), as said below
- output_moments: float32 [2, 32, 16, 4096], P(None, 'dp', None, 'tensor'), as said below
- batch_tenants: int32 [16384], P('dp'), may hold values from 0 to 15, as said below
- tenant_owner_slots: int32 [16], replicated, may hold values from 0 to 31, as said below
Outputs:
- grad_gate: bfloat16 [16384, 14336], P('dp', 'tensor')
- grad_up: bfloat16 [16384, 14336], P('dp', 'tensor')
- new_moments_a: float32 [2, 32, 16, 14336], P(None, 'dp', None, 'tensor')
- new_moments_b: float32 [2, 32, 16, 4096], P(None, 'dp', None, 'tensor')
- step_a: float32 [32, 16, 14336], P('dp', None, 'tensor')
- step_b: float32 [32, 16, 4096], P('dp', None, 'tensor')
The draws below stay inside these ranges and needn't reach their ends.
Inputs may be any that keep to these rules, and one draw needn't show every extreme that they name: `tenant_owner_slots`: distinct slots; 16 slots own no tenant. `batch_tenants`: each micro-batch (the 512 tokens of one index of dp) is a run of one tenant followed by a run of a tenant that may differ, each run one token or more. `input_moments`: the second row (second moments) is positive. `output_moments`: the second row (second moments) is positive.
All inputs are finite; a program needn't handle non-finite values.
Results may differ from the reference program's by a relative error of at most 0.0041.
Values may be sent and summed in bfloat16 or wider, within the bound.
No kernel may reach another device: no remote copies, remote signals or barrier semaphores. Data moves between devices by JAX's collectives and lax.ppermute only.
A program may use at most 64 MiB of HBM per device.

```python
import jax
import jax.numpy as jnp
from jax import lax

OUTPUT_WIDTH = 4096
HIDDEN_UNITS = 14336
ADAPTER_RANK = 16
TOK_DEV = 512
ADAM_STEP = 10
MICRO = 32
OWNER_SLOTS = 32
TENANTS = 16
TOKENS = 16384


def moment_stack(first_unit, key, spread, shape):
    second = spread * spread * jnp.exp(jax.random.uniform(key, shape, minval=-1.4, maxval=1.4))
    return jnp.stack([spread * first_unit, second]).astype(jnp.float32)


def draw_tenant_owner_slots(key, part):
    key = jax.random.fold_in(key, 11)
    inner_key, order_key = jax.random.split(key)
    inner = jax.random.permutation(inner_key, OWNER_SLOTS - 2)[:TENANTS - 2].astype(jnp.int32) + 1
    ends = jnp.array([0, OWNER_SLOTS - 1], jnp.int32)
    return jax.random.permutation(order_key, jnp.concatenate([ends, inner])).astype(jnp.int32)


def draw_batch_tenants(key, part):
    key = jax.random.fold_in(key, 14)
    lead_key, tail_key, cut_key = jax.random.split(key, 3)
    leading = jax.random.randint(lead_key, (MICRO,), 0, TENANTS).astype(jnp.int32)
    trailing = jax.random.randint(tail_key, (MICRO,), 0, TENANTS).astype(jnp.int32)
    cuts = jax.random.randint(cut_key, (MICRO,), 1, TOK_DEV).astype(jnp.int32)
    position = jnp.arange(TOK_DEV, dtype=jnp.int32)
    tenants = jnp.where(position[None, :] < cuts[:, None], leading[:, None], trailing[:, None])
    return tenants.reshape(TOKENS).astype(jnp.int32)


def draw_input_moments(key, part):
    key = jax.random.fold_in(key, 12)
    first_key, second_key = jax.random.split(key)
    shape = (OWNER_SLOTS, ADAPTER_RANK, HIDDEN_UNITS)
    first_unit = jax.random.normal(first_key, shape)
    return moment_stack(first_unit, second_key, 0.15, shape)


def draw_output_moments(key, part):
    key = jax.random.fold_in(key, 13)
    first_key, second_key = jax.random.split(key)
    shape = (OWNER_SLOTS, ADAPTER_RANK, OUTPUT_WIDTH)
    first_unit = jax.random.normal(first_key, shape)
    return moment_stack(first_unit, second_key, 0.04, shape)


def shard_levels(key, shape, cuts, smallest, largest):
    factor_of, own = 1.0, jax.random.fold_in(key, 6)
    for dim, blocks in cuts:
        heights = jnp.exp(jax.random.uniform(jax.random.fold_in(own, dim), (blocks,), jnp.float32, smallest / len(cuts), largest / len(cuts)))
        factor_of = factor_of * jnp.repeat(heights, shape[dim] // blocks).reshape([-1 if axis == dim else 1 for axis in range(len(shape))])
    return factor_of


def noise(own_key, shape, width, reach, cuts=(), kind=jnp.bfloat16):
    drawn = jax.random.normal(own_key, shape, jnp.float32) * width
    if len(cuts) > 0:
        drawn = shard_levels(own_key, shape, cuts, -0.22, 0.18) * drawn
    return jnp.clip(drawn, min=-reach, max=reach).astype(kind)


def setup_inputs(seed: int = 0) -> dict:
    key_list = jax.random.split(jax.random.key(seed), 11)
    return {
        "gate_logits": noise(key_list[0], (TOKENS, HIDDEN_UNITS), 1.0, 6.0, ((0, 32), (1, 16))),
        "up_projected": noise(key_list[1], (TOKENS, HIDDEN_UNITS), 1.0, 6.0, ((0, 32), (1, 16))),
        "output_gradient": noise(key_list[2], (TOKENS, OUTPUT_WIDTH), 1.0, 6.0, ((0, 32), (1, 16))),
        "down_matrix": noise(key_list[3], (HIDDEN_UNITS, OUTPUT_WIDTH), HIDDEN_UNITS ** -0.5, 0.046875, ((0, 16), (1, 32))),
        "adapter_input_factors": noise(key_list[4], (OWNER_SLOTS, ADAPTER_RANK, HIDDEN_UNITS), HIDDEN_UNITS ** -0.5, 0.046875, ((0, 32), (2, 16)), jnp.float32),
        "adapter_output_factors": noise(key_list[5], (OWNER_SLOTS, ADAPTER_RANK, OUTPUT_WIDTH), (OUTPUT_WIDTH // 16) ** -0.5, 0.375, ((0, 32), (2, 16)), jnp.float32),
        "input_moments": draw_input_moments(jax.random.fold_in(key_list[10], 71), 0),
        "output_moments": draw_output_moments(jax.random.fold_in(key_list[10], 71), 0),
        "batch_tenants": draw_batch_tenants(jax.random.fold_in(key_list[10], 71), 0),
        "tenant_owner_slots": draw_tenant_owner_slots(jax.random.fold_in(key_list[10], 71), 0),
    }


ADAPTER_SCALE = 2.0
BETA_ONE = 0.9
BETA_TWO = 0.95
ADAM_EPS = 1e-08

def adam_update(sums, counts, moments):
    grad = sums / jnp.maximum(counts, 1.0)[:, None, None]
    active = (counts > 0.5)[:, None, None]
    first = jnp.where(active, BETA_ONE * moments[0] + (1.0 - BETA_ONE) * grad, moments[0])
    second = jnp.where(active, BETA_TWO * moments[1] + (1.0 - BETA_TWO) * grad * grad, moments[1])
    corr_one = 1.0 - BETA_ONE ** ADAM_STEP
    corr_two = 1.0 - BETA_TWO ** ADAM_STEP
    update = first / corr_one / (jnp.sqrt(second / corr_two) + ADAM_EPS)
    update = jnp.where(active, update, jnp.zeros_like(update))
    return (jnp.stack([first, second]), update)

def reference(gate_logits, up_projected, output_gradient, down_matrix, adapter_input_factors, adapter_output_factors, input_moments, output_moments, batch_tenants, tenant_owner_slots):
    one_hot = (batch_tenants[:, None] == jnp.arange(TENANTS, dtype=jnp.int32)[None, :]).astype(jnp.int32)
    slot_of_token = lax.optimization_barrier(jnp.sum(one_hot * tenant_owner_slots[None, :], axis=1)).astype(jnp.int32)
    gate_blocks = gate_logits.reshape(MICRO, TOK_DEV, HIDDEN_UNITS)
    up_blocks = up_projected.reshape(MICRO, TOK_DEV, HIDDEN_UNITS)
    cot_blocks = output_gradient.reshape(MICRO, TOK_DEV, OUTPUT_WIDTH)
    slot_blocks = slot_of_token.reshape(MICRO, TOK_DEV)
    factors_a = adapter_input_factors.astype(jnp.bfloat16).reshape(OWNER_SLOTS * ADAPTER_RANK, HIDDEN_UNITS)
    factors_b = adapter_output_factors.astype(jnp.bfloat16).reshape(OWNER_SLOTS * ADAPTER_RANK, OUTPUT_WIDTH)

    def one_batch(carry, item):
        sum_a, sum_b, counts = carry
        gate_in, up_in, hidden_cotangent, token_slots = item
        select = (token_slots[:, None] == jnp.arange(OWNER_SLOTS, dtype=jnp.int32)[None, :]).astype(jnp.float32)
        gate_f = gate_in.astype(jnp.float32)
        up_f = up_in.astype(jnp.float32)
        sigmoid_gate = jax.nn.sigmoid(gate_f)
        activated = gate_f * sigmoid_gate
        hidden = (activated * up_f).astype(jnp.bfloat16)
        proj_all = jnp.dot(hidden, factors_a.T, preferred_element_type=jnp.float32).reshape(TOK_DEV, OWNER_SLOTS, ADAPTER_RANK)
        rank_projection = lax.optimization_barrier(jnp.sum(select[:, :, None] * proj_all, axis=1)).astype(jnp.bfloat16)
        grad_all = jnp.dot(hidden_cotangent, factors_b.T, preferred_element_type=jnp.float32).reshape(TOK_DEV, OWNER_SLOTS, ADAPTER_RANK)
        rank_gradient = (ADAPTER_SCALE * lax.optimization_barrier(jnp.sum(select[:, :, None] * grad_all, axis=1))).astype(jnp.bfloat16)
        spread_grad = (select[:, :, None] * rank_gradient.astype(jnp.float32)[:, None, :]).astype(jnp.bfloat16).reshape(TOK_DEV, OWNER_SLOTS * ADAPTER_RANK)
        spread_proj = (select[:, :, None] * rank_projection.astype(jnp.float32)[:, None, :]).astype(jnp.bfloat16).reshape(TOK_DEV, OWNER_SLOTS * ADAPTER_RANK)
        hidden_grad = jnp.dot(hidden_cotangent, down_matrix.T, preferred_element_type=jnp.float32)
        hidden_grad = hidden_grad + jnp.dot(spread_grad, factors_a, preferred_element_type=jnp.float32)
        grad_gate_blk = (hidden_grad * up_f * sigmoid_gate * (1.0 + gate_f * (1.0 - sigmoid_gate))).astype(jnp.bfloat16)
        grad_up_blk = (hidden_grad * activated).astype(jnp.bfloat16)
        term_a = jnp.dot(spread_grad.T, hidden, preferred_element_type=jnp.float32).reshape(OWNER_SLOTS, ADAPTER_RANK, HIDDEN_UNITS)
        term_b = ADAPTER_SCALE * jnp.dot(spread_proj.T, hidden_cotangent, preferred_element_type=jnp.float32).reshape(OWNER_SLOTS, ADAPTER_RANK, OUTPUT_WIDTH)
        return ((sum_a + term_a, sum_b + term_b, counts + lax.optimization_barrier(jnp.sum(select, axis=0))), (grad_gate_blk, grad_up_blk))
    start = (jnp.zeros((OWNER_SLOTS, ADAPTER_RANK, HIDDEN_UNITS), jnp.float32), jnp.zeros((OWNER_SLOTS, ADAPTER_RANK, OUTPUT_WIDTH), jnp.float32), jnp.zeros((OWNER_SLOTS,), jnp.float32))
    (sum_a, sum_b, counts), (grad_gate, grad_up) = lax.scan(one_batch, start, (gate_blocks, up_blocks, cot_blocks, slot_blocks))
    new_moments_a, step_a = adam_update(sum_a, counts, input_moments)
    new_moments_b, step_b = adam_update(sum_b, counts, output_moments)
    return (grad_gate.reshape(TOKENS, HIDDEN_UNITS), grad_up.reshape(TOKENS, HIDDEN_UNITS), new_moments_a, new_moments_b, step_a, step_b)
```

```python
import jax
import jax.numpy as jnp
from jax import lax
from jax.sharding import PartitionSpec as P

ADAM_STEP = 10


ADAPTER_SCALE = 2.0
BETA_ONE = 0.9
BETA_TWO = 0.95
ADAM_EPS = 1e-08
Y, Z_HI = 4, 4
COUNT_BASE = 32


def adam_update(sums, count, moments):
    grad = sums / jnp.maximum(count, 1.0)
    active = count > 0.5
    first = jnp.where(active, BETA_ONE * moments[0] + (1.0 - BETA_ONE) * grad, moments[0])
    second = jnp.where(active, BETA_TWO * moments[1] + (1.0 - BETA_TWO) * grad * grad, moments[1])
    corr_one = 1.0 - BETA_ONE**ADAM_STEP
    corr_two = 1.0 - BETA_TWO**ADAM_STEP
    update = first / corr_one / (jnp.sqrt(second / corr_two) + ADAM_EPS)
    update = jnp.where(active, update, jnp.zeros_like(update))
    return (jnp.stack([first, second]), update)


def gather_by_exchange(block, axis, groups=None, size=None):
    size = lax.axis_size(axis) if size is None else size
    copies = jnp.broadcast_to(block[None], (size,) + block.shape)
    return lax.all_to_all(copies, axis, 0, 0, axis_index_groups=groups)


def nt_dot(left, right):
    return lax.dot_general(
        left, right, (((1,), (1,)), ((), ())), preferred_element_type=jnp.float32
    )


def shards(
    gate_logits,
    up_projected,
    output_gradient,
    down_matrix,
    adapter_input_factors,
    adapter_output_factors,
    input_moments,
    output_moments,
    batch_tenants,
    tenant_owner_slots,
):
    slot_count = lax.axis_size("dp")
    me = lax.axis_index("dp")
    rank, hid = adapter_input_factors.shape[1:]
    feat = adapter_output_factors.shape[2]
    tok = gate_logits.shape[0]
    cot_full = lax.all_gather(output_gradient, "tensor", axis=1, tiled=True)
    down_full = lax.all_gather(down_matrix, "dp", axis=1, tiled=True)

    tenant_ids = jnp.arange(tenant_owner_slots.shape[0], dtype=jnp.int32)
    slot_first = jnp.sum(jnp.where(tenant_ids == batch_tenants[0], tenant_owner_slots, 0))
    slot_last = jnp.sum(jnp.where(tenant_ids == batch_tenants[-1], tenant_owner_slots, 0))
    in_first = (batch_tenants == batch_tenants[0])[None, :]
    count_first = jnp.sum(in_first.astype(jnp.int32))
    count_last = tok - count_first
    slots = jnp.arange(slot_count, dtype=jnp.int32)
    hot_first = slots == slot_first
    hot_last = slots == slot_last
    run_counts = jnp.where(hot_first, count_first, 0) + jnp.where(hot_last, count_last, 0)
    digits = jnp.stack([run_counts // COUNT_BASE, run_counts % COUNT_BASE]).astype(jnp.bfloat16)
    digits = jnp.pad(digits, ((0, rank - 2), (0, 128 - slot_count)))

    packed = jnp.concatenate(
        [
            adapter_input_factors[0].astype(jnp.bfloat16),
            adapter_output_factors[0].astype(jnp.bfloat16),
            digits,
        ],
        axis=1,
    )
    gathered = gather_by_exchange(packed, "dp")
    mine = lax.dynamic_index_in_dim(gathered[:, :2, hid + feat :], me, axis=2, keepdims=False)
    count_parts = jnp.sum(mine.astype(jnp.float32), axis=0)
    count = COUNT_BASE * count_parts[0] + count_parts[1]
    pair = jnp.concatenate(
        [
            lax.dynamic_index_in_dim(gathered, slot_first, 0, keepdims=False),
            lax.dynamic_index_in_dim(gathered, slot_last, 0, keepdims=False),
        ],
        axis=0,
    )
    pair_a, pair_b = pair[:, :hid], pair[:, hid : hid + feat]

    gate_f = gate_logits.astype(jnp.float32)
    up_f = up_projected.astype(jnp.float32)
    sigmoid_gate = jax.nn.sigmoid(gate_f)
    activated = gate_f * sigmoid_gate
    hidden = (activated * up_f).astype(jnp.bfloat16)

    proj_pair = nt_dot(pair_a, hidden)
    grad_pair = nt_dot(pair_b, output_gradient)
    part = jnp.concatenate(
        [
            jnp.where(in_first, proj_pair[:rank], proj_pair[rank:]),
            jnp.where(in_first, grad_pair[:rank], grad_pair[rank:]),
        ],
        axis=0,
    )
    along_y = [[y * Z_HI + h for y in range(Y)] for h in range(Z_HI)]
    along_z = [[y * Z_HI + h for h in range(Z_HI)] for y in range(Y)]
    chunks = part.reshape(2 * rank, Y, tok // Y).transpose(1, 0, 2)
    chunk = jnp.sum(lax.all_to_all(chunks, "tensor", 0, 0, axis_index_groups=along_y), axis=0)
    chunk = jnp.sum(lax.all_gather(chunk, "tensor", axis_index_groups=along_z), axis=0)
    scale = jnp.where(jnp.arange(2 * rank)[:, None] < rank, 1.0, ADAPTER_SCALE)
    rounded = (scale * chunk).astype(jnp.bfloat16)
    whole = lax.all_gather(rounded, "tensor", axis_index_groups=along_y)
    whole = whole.transpose(1, 0, 2).reshape(2 * rank, tok)
    rank_projection, rank_gradient = whole[:rank], whole[rank:]
    zero = jnp.zeros((), jnp.bfloat16)
    spread_grad = jnp.concatenate(
        [jnp.where(in_first, rank_gradient, zero), jnp.where(in_first, zero, rank_gradient)]
    )
    spread_proj = jnp.concatenate(
        [jnp.where(in_first, rank_projection, zero), jnp.where(in_first, zero, rank_projection)]
    )
    term_a = jnp.dot(spread_grad, hidden, preferred_element_type=jnp.float32)
    term_b = ADAPTER_SCALE * jnp.dot(
        spread_proj, output_gradient, preferred_element_type=jnp.float32
    )
    term = jnp.concatenate([term_a, term_b], axis=1)
    outgoing = jnp.where(hot_first[:, None, None], term[:rank][None], 0.0) + jnp.where(
        hot_last[:, None, None], term[rank:][None], 0.0
    )
    incoming = lax.all_to_all(outgoing.astype(jnp.bfloat16), "dp", 0, 0)
    sums = jnp.sum(incoming.astype(jnp.float32), axis=0)
    new_moments_a, step_a = adam_update(sums[None, :, :hid], count, input_moments)
    new_moments_b, step_b = adam_update(sums[None, :, hid:], count, output_moments)

    hidden_grad = nt_dot(cot_full, down_full)
    hidden_grad = hidden_grad + lax.dot_general(
        spread_grad, pair_a, (((0,), (0,)), ((), ())), preferred_element_type=jnp.float32
    )
    grad_gate = (hidden_grad * up_f * sigmoid_gate * (1.0 + gate_f * (1.0 - sigmoid_gate))).astype(
        jnp.bfloat16
    )
    grad_up = (hidden_grad * activated).astype(jnp.bfloat16)
    return (grad_gate, grad_up, new_moments_a, new_moments_b, step_a, step_b)


def solution(mesh):
    placed = (
        P("dp", "tensor"),
        P("dp", "tensor"),
        P("dp", "tensor"),
        P("tensor", "dp"),
        P("dp", None, "tensor"),
        P("dp", None, "tensor"),
        P(None, "dp", None, "tensor"),
        P(None, "dp", None, "tensor"),
        P("dp"),
        P(),
    )
    return jax.shard_map(
        shards,
        mesh=mesh,
        in_specs=placed,
        out_specs=(
            P("dp", "tensor"),
            P("dp", "tensor"),
            P(None, "dp", None, "tensor"),
            P(None, "dp", None, "tensor"),
            P("dp", None, "tensor"),
            P("dp", None, "tensor"),
        ),
        check_vma=False,
    )
```

```python
import functools

import jax
import jax.numpy as jnp
from jax import lax
from jax.experimental import pallas as pl
from jax.experimental.pallas import tpu as pltpu
from jax.sharding import PartitionSpec as P

ADAM_STEP = 10


ADAPTER_SCALE = 2.0
BETA_ONE = 0.9
BETA_TWO = 0.95
ADAM_EPS = 1e-08
X, Z_LO, CORES = 4, 4, 2
Y, Z_HI = 4, 4
COUNT_BASE = 32
LANES = 128
INFO_FIRST, INFO_LAST, INFO_CUT = 0, 1, 2

ALONG_X = [[(x * Z_LO + z) * CORES + c for x in range(X)] for z in range(Z_LO) for c in range(CORES)]
ALONG_Z_LO = [[(x * Z_LO + z) * CORES + c for z in range(Z_LO)] for x in range(X) for c in range(CORES)]
ALONG_Y = [[y * Z_HI + h for y in range(Y)] for h in range(Z_HI)]
ALONG_Z_HI = [[y * Z_HI + h for h in range(Z_HI)] for y in range(Y)]
OTHER_CORE = [(d, d ^ 1) for d in range(X * Z_LO * CORES)]
NEXT_Z = [(y * Z_HI + h, y * Z_HI + (h + 1) % Z_HI) for y in range(Y) for h in range(Z_HI)]
LAST_Z = [(y * Z_HI + h, y * Z_HI + (h - 1) % Z_HI) for y in range(Y) for h in range(Z_HI)]
NEXT_Y = [(y * Z_HI + h, (y + 1) % Y * Z_HI + h) for y in range(Y) for h in range(Z_HI)]
LAST_Y = [(y * Z_HI + h, (y - 1) % Y * Z_HI + h) for y in range(Y) for h in range(Z_HI)]

VMEM = pl.BlockSpec(memory_space=pltpu.VMEM)
SMEM = pl.BlockSpec(memory_space=pltpu.SMEM)


def params(mib=40):
    return pltpu.CompilerParams(vmem_limit_bytes=mib * 1024 * 1024)


def nt_dot(left, right):
    return lax.dot_general(
        left, right, (((1,), (1,)), ((), ())), preferred_element_type=jnp.float32
    )


def tn_dot(left, right):
    return lax.dot_general(
        left, right, (((0,), (0,)), ((), ())), preferred_element_type=jnp.float32
    )


def spread(copies, block):
    return jnp.broadcast_to(block[None], (copies,) + block.shape)


def prepare(tenants_s, owners_s, tenants_v, factor_a, factor_b, packed, info_v):
    tok = tenants_s.shape[0]
    rank, hid = factor_a.shape
    feat = factor_b.shape[1]
    first, last = tenants_s[0], tenants_s[tok - 1]
    slot_first, slot_last = owners_s[first], owners_s[last]
    cut = jnp.sum((tenants_v[...] == first).astype(jnp.int32))
    lane = lax.broadcasted_iota(jnp.int32, (rank, LANES), 1)
    row = lax.broadcasted_iota(jnp.int32, (rank, LANES), 0)
    counts = jnp.where(lane == slot_first, cut, 0) + jnp.where(lane == slot_last, tok - cut, 0)
    high = lax.shift_right_logical(counts, 5)
    digits = jnp.where(row == 0, high, jnp.where(row == 1, counts - COUNT_BASE * high, 0))
    digits = digits.astype(jnp.float32).astype(jnp.bfloat16)
    a = factor_a[...].astype(jnp.bfloat16)
    b = factor_b[...].astype(jnp.bfloat16)
    for copy in range(packed.shape[0]):
        packed[copy, :, :hid] = a
        packed[copy, :, hid : hid + feat] = b
        packed[copy, :, hid + feat :] = digits
    lane_i = lax.broadcasted_iota(jnp.int32, info_v.shape, 1)
    info_v[...] = jnp.where(
        lane_i == INFO_FIRST, slot_first, jnp.where(lane_i == INFO_LAST, slot_last, cut)
    )


def low_rank(info_s, core_s, own, other, hidden, cot, part, pair, totals):
    core = core_s[0]
    rank = own.shape[1]
    hid, feat = hidden.shape[1], cot.shape[1]
    for run, place in enumerate((INFO_FIRST, INFO_LAST)):
        slot = info_s[place]
        chip = lax.shift_right_logical(slot, 1)
        here = (slot & 1) == core
        rows = pl.ds(run * rank, rank)

        @pl.when(here)
        def _():
            pair[rows, :] = own[chip, :, : hid + feat]

        @pl.when(jnp.logical_not(here))
        def _():
            pair[rows, :] = other[chip, :, : hid + feat]

    tok = hidden.shape[0]
    in_first = lax.broadcasted_iota(jnp.int32, (rank, tok), 1) < info_s[INFO_CUT]
    proj = nt_dot(pair[:, :hid], hidden[...])
    grad = nt_dot(pair[:, hid:], cot[...])
    proj = jnp.where(in_first, proj[:rank], proj[rank:])
    grad = jnp.where(in_first, grad[:rank], grad[rank:])
    width = tok // Y
    for y in range(Y):
        part[y, :rank, :] = proj[:, y * width : (y + 1) * width]
        part[y, rank:, :] = grad[:, y * width : (y + 1) * width]
    digits = own[:, :, hid + feat :].astype(jnp.float32)
    digits = digits + other[:, :, hid + feat :].astype(jnp.float32)
    totals[...] = jnp.sum(digits, axis=0)


def terms(info_s, whole, hidden, cot, grad_rows, term):
    rank = whole.shape[1] // 2
    hid = hidden.shape[1]
    tok = hidden.shape[0]
    rows = jnp.concatenate([whole[y] for y in range(Y)], axis=1)
    in_first = lax.broadcasted_iota(jnp.int32, (rank, tok), 1) < info_s[INFO_CUT]
    proj = rows[:rank].astype(jnp.float32)
    grad = rows[rank:].astype(jnp.float32)
    zero = jnp.zeros_like(proj)

    def by_run(values):
        both = [jnp.where(in_first, values, zero), jnp.where(in_first, zero, values)]
        return jnp.concatenate(both, axis=0).astype(jnp.bfloat16)

    proj, grad = by_run(proj), by_run(grad)
    grad_rows[...] = grad
    term[:, :hid] = jnp.dot(grad, hidden[...], preferred_element_type=jnp.float32)
    term[:, hid:] = ADAPTER_SCALE * jnp.dot(proj, cot[...], preferred_element_type=jnp.float32)


def dense(info_s, info_other_s, core_s, term, term_other, outgoing, total):
    core = core_s[0]
    rank = outgoing.shape[1]
    total[...] = jnp.zeros_like(total)
    for info, source in ((info_s, term), (info_other_s, term_other)):
        for run, place in enumerate((INFO_FIRST, INFO_LAST)):
            slot = info[place]
            chip = lax.shift_right_logical(slot, 1)

            @pl.when((slot & 1) == core)
            def _():
                total[chip] += source[run * rank : (run + 1) * rank, :]

    outgoing[...] = total[...].astype(jnp.bfloat16)


def adam(me_s, totals, incoming, moments_a, moments_b, new_a, new_b, step_a, step_b):
    lane = lax.broadcasted_iota(jnp.int32, (1, LANES), 1)
    digit = COUNT_BASE * totals[0:1, :] + totals[1:2, :]
    count = jnp.sum(jnp.where(lane == me_s[0], digit, 0.0))
    active = count > 0.5
    divisor = jnp.maximum(count, 1.0)
    corr_one = 1.0 - BETA_ONE**ADAM_STEP
    corr_two = 1.0 - BETA_TWO**ADAM_STEP
    sums = jnp.sum(incoming[...].astype(jnp.float32), axis=0)
    hid = moments_a.shape[-1]
    for part, moments, new, step in (
        (sums[:, :hid], moments_a, new_a, step_a),
        (sums[:, hid:], moments_b, new_b, step_b),
    ):
        grad = part / divisor
        old_one, old_two = moments[0, 0], moments[1, 0]
        first = jnp.where(active, BETA_ONE * old_one + (1.0 - BETA_ONE) * grad, old_one)
        second = jnp.where(active, BETA_TWO * old_two + (1.0 - BETA_TWO) * grad * grad, old_two)
        update = first / corr_one / (jnp.sqrt(second / corr_two) + ADAM_EPS)
        new[0, 0] = first
        new[1, 0] = second
        step[0] = jnp.where(active, update, 0.0)


def finish(
    y_s, own, back, ahead, far_top, far_low, down, grad_rows, pair_a, gate, up, out_gate, out_up, total
):
    place, turn = pl.program_id(0), pl.program_id(1)
    half = far_top.shape[1]
    weights = down[...]

    @pl.when((place == 0) & (turn == 0))
    def _():
        total[...] = tn_dot(grad_rows[...], pair_a[...])

    @pl.when(turn == 0)
    def _():
        total[...] += nt_dot(own[0], weights)

    @pl.when(turn == 1)
    def _():
        total[...] += nt_dot(back[0], weights)

    @pl.when(turn == 2)
    def _():
        total[...] += nt_dot(ahead[0], weights)

    @pl.when(turn == 3)
    def _():
        total[:half, :] += nt_dot(far_top[0], weights)
        total[half:, :] += nt_dot(far_low[0], weights)

    @pl.when((place == pl.num_programs(0) - 1) & (turn == pl.num_programs(1) - 1))
    def _():
        gate_f = gate[...].astype(jnp.float32)
        up_f = up[...].astype(jnp.float32)
        sigmoid_gate = jax.nn.sigmoid(gate_f)
        grad = total[...]
        out_gate[...] = (
            grad * up_f * sigmoid_gate * (1.0 + gate_f * (1.0 - sigmoid_gate))
        ).astype(jnp.bfloat16)
        out_up[...] = (grad * (gate_f * sigmoid_gate)).astype(jnp.bfloat16)


def shards(
    gate_logits,
    up_projected,
    output_gradient,
    down_matrix,
    adapter_input_factors,
    adapter_output_factors,
    input_moments,
    output_moments,
    batch_tenants,
    tenant_owner_slots,
):
    me = lax.axis_index("dp").astype(jnp.int32)
    core_s = (me & (CORES - 1)).reshape(1)
    tensor = lax.axis_index("tensor").astype(jnp.int32)
    y_s = jnp.stack([lax.shift_right_logical(tensor, 2), tensor & (Z_HI - 1)])
    rank, hid = adapter_input_factors.shape[1:]
    feat = adapter_output_factors.shape[2]
    tok = gate_logits.shape[0]
    wide = hid + feat
    bf16, f32 = jnp.bfloat16, jnp.float32
    shape = jax.ShapeDtypeStruct

    down_full = lax.all_gather(down_matrix, "dp", axis=1, tiled=True)

    packed, info_v = pl.pallas_call(
        prepare,
        out_shape=(shape((Z_LO, rank, wide + LANES), bf16), shape((8, LANES), jnp.int32)),
        in_specs=[SMEM, SMEM, VMEM, VMEM, VMEM],
        out_specs=(VMEM, VMEM),
        compiler_params=params(),
        name="prepare",
    )(
        batch_tenants,
        tenant_owner_slots,
        batch_tenants.reshape(-1, LANES),
        adapter_input_factors[0],
        adapter_output_factors[0],
    )
    column = lax.all_to_all(packed, "dp", 0, 0, axis_index_groups=ALONG_Z_LO)
    info_other_v = lax.ppermute(info_v, "dp", OTHER_CORE)
    info_s, info_other_s = info_v[0, :8], info_other_v[0, :8]
    half = tok // 2
    z_back = lax.ppermute(output_gradient, "tensor", NEXT_Z)
    z_ahead = lax.ppermute(output_gradient, "tensor", LAST_Z)
    hidden = (
        jax.nn.silu(gate_logits.astype(f32)) * up_projected.astype(f32)
    ).astype(bf16)
    plane = lax.all_to_all(spread(X, column), "dp", 0, 0, axis_index_groups=ALONG_X)
    own = plane.reshape(X * Z_LO, rank, wide + LANES)
    other = lax.ppermute(own, "dp", OTHER_CORE)

    part, pair, totals = pl.pallas_call(
        low_rank,
        out_shape=(
            shape((Y, 2 * rank, tok // Y), f32),
            shape((2 * rank, wide), bf16),
            shape((rank, LANES), f32),
        ),
        in_specs=[SMEM, SMEM, VMEM, VMEM, VMEM, VMEM],
        out_specs=(VMEM, VMEM, VMEM),
        compiler_params=params(),
        name="low_rank",
    )(info_s, core_s, own, other, hidden, output_gradient)

    z_back, z_ahead, part = lax.optimization_barrier((z_back, z_ahead, part))
    z_far_top = lax.ppermute(z_back[:half], "tensor", NEXT_Z)
    z_far_low = lax.ppermute(z_ahead[half:], "tensor", LAST_Z)

    chunk = jnp.sum(lax.all_to_all(part, "tensor", 0, 0, axis_index_groups=ALONG_Y), axis=0)
    chunk = jnp.sum(lax.all_gather(chunk, "tensor", axis_index_groups=ALONG_Z_HI), axis=0)
    scale = jnp.where(jnp.arange(2 * rank)[:, None] < rank, 1.0, ADAPTER_SCALE)
    rounded = (scale * chunk).astype(bf16)
    whole = lax.all_to_all(spread(Y, rounded), "tensor", 0, 0, axis_index_groups=ALONG_Y)

    z_far_top, z_far_low, whole = lax.optimization_barrier((z_far_top, z_far_low, whole))
    z_far = jnp.concatenate([z_far_top, z_far_low])
    cot_z = jnp.stack([output_gradient, z_back, z_ahead, z_far])
    back = lax.ppermute(cot_z, "tensor", NEXT_Y)
    ahead = lax.ppermute(cot_z, "tensor", LAST_Y)

    grad_rows, term = pl.pallas_call(
        terms,
        out_shape=(shape((2 * rank, tok), bf16), shape((2 * rank, wide), f32)),
        in_specs=[SMEM, VMEM, VMEM, VMEM],
        out_specs=(VMEM, VMEM),
        compiler_params=params(),
        name="terms",
    )(info_s, whole, hidden, output_gradient)

    term_other = lax.ppermute(term, "dp", OTHER_CORE)
    outgoing = pl.pallas_call(
        dense,
        out_shape=shape((X * Z_LO, rank, wide), bf16),
        in_specs=[SMEM, SMEM, SMEM, VMEM, VMEM],
        out_specs=VMEM,
        scratch_shapes=[pltpu.VMEM((X * Z_LO, rank, wide), f32)],
        compiler_params=params(),
        name="dense",
    )(info_s, info_other_s, core_s, term, term_other)
    outgoing = outgoing.reshape(X, Z_LO, rank, wide)
    by_x = lax.all_to_all(outgoing, "dp", 0, 0, axis_index_groups=ALONG_X)
    by_x = jnp.sum(by_x.astype(f32), axis=0).astype(bf16)
    incoming = lax.all_to_all(by_x, "dp", 0, 0, axis_index_groups=ALONG_Z_LO)

    new_moments_a, new_moments_b, step_a, step_b = pl.pallas_call(
        adam,
        out_shape=(
            shape(input_moments.shape, f32),
            shape(output_moments.shape, f32),
            shape(adapter_input_factors.shape, f32),
            shape(adapter_output_factors.shape, f32),
        ),
        in_specs=[SMEM, VMEM, VMEM, VMEM, VMEM],
        out_specs=(VMEM,) * 4,
        compiler_params=params(),
        name="adam",
    )(me.reshape(1), totals, incoming, input_moments, output_moments)

    far_top = lax.ppermute(back[:, :half], "tensor", NEXT_Y)
    far_low = lax.ppermute(ahead[:, half:], "tensor", LAST_Y)

    def down_block(place, turn, y_ref):
        y_off = jnp.where(turn == 1, Y - 1, jnp.where(turn == 2, 1, jnp.where(turn == 3, 2, 0)))
        z_off = jnp.where(place == 1, Z_HI - 1, jnp.where(place == 2, 1, jnp.where(place == 3, 2, 0)))
        return 0, lax.rem(y_ref[0] + y_off, Y) * Z_HI + lax.rem(y_ref[1] + z_off, Z_HI)

    def by_place(rows):
        return pl.BlockSpec((1, rows, feat), lambda place, turn, y_ref: (place, 0, 0))

    def whole_of(rows, columns):
        return pl.BlockSpec((rows, columns), lambda place, turn, y_ref: (0, 0))

    grad_gate, grad_up = pl.pallas_call(
        finish,
        out_shape=(shape((tok, hid), bf16), shape((tok, hid), bf16)),
        grid_spec=pltpu.PrefetchScalarGridSpec(
            num_scalar_prefetch=1,
            grid=(Z_HI, Y),
            in_specs=[
                by_place(tok),
                by_place(tok),
                by_place(tok),
                by_place(half),
                by_place(half),
                pl.BlockSpec((hid, feat), down_block),
                whole_of(2 * rank, tok),
                whole_of(2 * rank, hid),
                whole_of(tok, hid),
                whole_of(tok, hid),
            ],
            out_specs=[whole_of(tok, hid), whole_of(tok, hid)],
            scratch_shapes=[pltpu.VMEM((tok, hid), f32)],
        ),
        compiler_params=params(),
        name="finish",
    )(
        y_s,
        cot_z,
        back,
        ahead,
        far_top,
        far_low,
        down_full,
        grad_rows,
        pair[:, :hid],
        gate_logits,
        up_projected,
    )
    return (grad_gate, grad_up, new_moments_a, new_moments_b, step_a, step_b)


def solution(mesh):
    placed = (
        P("dp", "tensor"),
        P("dp", "tensor"),
        P("dp", "tensor"),
        P("tensor", "dp"),
        P("dp", None, "tensor"),
        P("dp", None, "tensor"),
        P(None, "dp", None, "tensor"),
        P(None, "dp", None, "tensor"),
        P("dp"),
        P(),
    )
    return jax.shard_map(
        shards,
        mesh=mesh,
        in_specs=placed,
        out_specs=(
            P("dp", "tensor"),
            P("dp", "tensor"),
            P(None, "dp", None, "tensor"),
            P(None, "dp", None, "tensor"),
            P("dp", None, "tensor"),
            P("dp", None, "tensor"),
        ),
        check_vma=False,
    )
```

```python
import functools

import jax
import jax.numpy as jnp
from jax import lax
from jax.experimental import pallas as pl
from jax.experimental.pallas import tpu as pltpu
from jax.sharding import PartitionSpec as P

ADAM_STEP = 10


ADAPTER_SCALE = 2.0
BETA_ONE = 0.9
BETA_TWO = 0.95
ADAM_EPS = 1e-08
X, Z_LO, CORES = 4, 4, 2
Y, Z_HI = 4, 4
COUNT_BASE = 32
LANES = 128
INFO_FIRST, INFO_LAST, INFO_CUT = 0, 1, 2

ALONG_X = [[(x * Z_LO + z) * CORES + c for x in range(X)] for z in range(Z_LO) for c in range(CORES)]
ALONG_Z_LO = [[(x * Z_LO + z) * CORES + c for z in range(Z_LO)] for x in range(X) for c in range(CORES)]
ALONG_Y = [[y * Z_HI + h for y in range(Y)] for h in range(Z_HI)]
ALONG_Z_HI = [[y * Z_HI + h for h in range(Z_HI)] for y in range(Y)]
OTHER_CORE = [(d, d ^ 1) for d in range(X * Z_LO * CORES)]
NEXT_Y = [(y * Z_HI + h, (y + 1) % Y * Z_HI + h) for y in range(Y) for h in range(Z_HI)]
LAST_Y = [(y * Z_HI + h, (y - 1) % Y * Z_HI + h) for y in range(Y) for h in range(Z_HI)]

VMEM = pl.BlockSpec(memory_space=pltpu.VMEM)
WHOLE = pl.BlockSpec()
SMEM = pl.BlockSpec(memory_space=pltpu.SMEM)


def params(mib=40):
    return pltpu.CompilerParams(vmem_limit_bytes=mib * 1024 * 1024)


def nt_dot(left, right):
    return lax.dot_general(
        left, right, (((1,), (1,)), ((), ())), preferred_element_type=jnp.float32
    )


def tn_dot(left, right):
    return lax.dot_general(
        left, right, (((0,), (0,)), ((), ())), preferred_element_type=jnp.float32
    )


def spread(copies, block):
    return jnp.broadcast_to(block[None], (copies,) + block.shape)


def prepare(tenants_s, owners_s, tenants_v, factor_a, factor_b, packed, info_v):
    tok = tenants_s.shape[0]
    rank, hid = factor_a.shape
    feat = factor_b.shape[1]
    first, last = tenants_s[0], tenants_s[tok - 1]
    slot_first, slot_last = owners_s[first], owners_s[last]
    cut = jnp.sum((tenants_v[...] == first).astype(jnp.int32))
    lane = lax.broadcasted_iota(jnp.int32, (rank, LANES), 1)
    row = lax.broadcasted_iota(jnp.int32, (rank, LANES), 0)
    counts = jnp.where(lane == slot_first, cut, 0) + jnp.where(lane == slot_last, tok - cut, 0)
    high = lax.shift_right_logical(counts, 5)
    digits = jnp.where(row == 0, high, jnp.where(row == 1, counts - COUNT_BASE * high, 0))
    digits = digits.astype(jnp.float32).astype(jnp.bfloat16)
    a = factor_a[...].astype(jnp.bfloat16)
    b = factor_b[...].astype(jnp.bfloat16)
    packed[:, :hid] = a
    packed[:, hid : hid + feat] = b
    packed[:, hid + feat :] = digits
    lane_i = lax.broadcasted_iota(jnp.int32, info_v.shape, 1)
    info_v[...] = jnp.where(
        lane_i == INFO_FIRST, slot_first, jnp.where(lane_i == INFO_LAST, slot_last, cut)
    )


def low_rank(info_s, core_s, own, other, hidden, cot, part, pair, totals):
    core = core_s[0]
    rank = own.shape[1]
    hid, feat = hidden.shape[1], cot.shape[1]
    for run, place in enumerate((INFO_FIRST, INFO_LAST)):
        slot = info_s[place]
        chip = lax.shift_right_logical(slot, 1)
        here = (slot & 1) == core
        rows = pl.ds(run * rank, rank)

        @pl.when(here)
        def _():
            pair[rows, :] = own[chip, :, : hid + feat]

        @pl.when(jnp.logical_not(here))
        def _():
            pair[rows, :] = other[chip, :, : hid + feat]

    tok = hidden.shape[0]
    in_first = lax.broadcasted_iota(jnp.int32, (rank, tok), 1) < info_s[INFO_CUT]
    proj = nt_dot(pair[:, :hid], hidden[...])
    grad = nt_dot(pair[:, hid:], cot[...])
    proj = jnp.where(in_first, proj[:rank], proj[rank:])
    grad = jnp.where(in_first, grad[:rank], grad[rank:])
    for y in range(Y):
        part[y, :rank, :] = proj
        part[y, rank:, :] = grad
    digits = own[:, :, hid + feat :].astype(jnp.float32)
    digits = digits + other[:, :, hid + feat :].astype(jnp.float32)
    totals[...] = jnp.sum(digits, axis=0)


def terms(info_s, sums, hidden, cot, grad_rows, term):
    rank = sums.shape[1] // 2
    hid = hidden.shape[1]
    tok = hidden.shape[0]
    rows = jnp.sum(sums[...], axis=0)
    in_first = lax.broadcasted_iota(jnp.int32, (rank, tok), 1) < info_s[INFO_CUT]
    proj = rows[:rank]
    grad = ADAPTER_SCALE * rows[rank:]
    zero = jnp.zeros_like(proj)

    def by_run(values):
        both = [jnp.where(in_first, values, zero), jnp.where(in_first, zero, values)]
        return jnp.concatenate(both, axis=0).astype(jnp.bfloat16)

    proj, grad = by_run(proj), by_run(grad)
    grad_rows[...] = grad
    term[:, :hid] = jnp.dot(grad, hidden[...], preferred_element_type=jnp.float32)
    term[:, hid:] = ADAPTER_SCALE * jnp.dot(proj, cot[...], preferred_element_type=jnp.float32)


def dense(info_s, info_other_s, core_s, term, term_other, outgoing, total):
    core = core_s[0]
    rank = outgoing.shape[1]
    total[...] = jnp.zeros_like(total)
    for info, source in ((info_s, term), (info_other_s, term_other)):
        for run, place in enumerate((INFO_FIRST, INFO_LAST)):
            slot = info[place]
            chip = lax.shift_right_logical(slot, 1)

            @pl.when((slot & 1) == core)
            def _():
                total[chip] += source[run * rank : (run + 1) * rank, :]

    outgoing[...] = total[...].astype(jnp.bfloat16)


def adam(me_s, totals, incoming, moments_a, moments_b, new_a, new_b, step_a, step_b):
    lane = lax.broadcasted_iota(jnp.int32, (1, LANES), 1)
    digit = COUNT_BASE * totals[0:1, :] + totals[1:2, :]
    count = jnp.sum(jnp.where(lane == me_s[0], digit, 0.0))
    active = count > 0.5
    divisor = jnp.maximum(count, 1.0)
    corr_one = 1.0 - BETA_ONE**ADAM_STEP
    corr_two = 1.0 - BETA_TWO**ADAM_STEP
    sums = jnp.sum(incoming[...].astype(jnp.float32), axis=0)
    hid = moments_a.shape[-1]
    for part, moments, new, step in (
        (sums[:, :hid], moments_a, new_a, step_a),
        (sums[:, hid:], moments_b, new_b, step_b),
    ):
        grad = part / divisor
        old_one, old_two = moments[0, 0], moments[1, 0]
        first = jnp.where(active, BETA_ONE * old_one + (1.0 - BETA_ONE) * grad, old_one)
        second = jnp.where(active, BETA_TWO * old_two + (1.0 - BETA_TWO) * grad * grad, old_two)
        update = first / corr_one / (jnp.sqrt(second / corr_two) + ADAM_EPS)
        new[0, 0] = first
        new[1, 0] = second
        step[0] = jnp.where(active, update, 0.0)


def finish(
    place_s, own, back, ahead, far_low, far_high, down_own, down_back, down_ahead, down_far,
    grad_rows, pair_a, gate, up, out_gate, out_up, total, far
):
    place = pl.program_id(0)

    @pl.when(place == 0)
    def _():
        total[...] = tn_dot(grad_rows[...], pair_a[...])

    @pl.when(place < 2)
    def _():
        far[...] = far_low[0]

    @pl.when(place >= 2)
    def _():
        far[...] = far_high[0]

    total[...] += (
        nt_dot(own[0], down_own[...])
        + nt_dot(back[0], down_back[...])
        + nt_dot(ahead[0], down_ahead[...])
        + nt_dot(far[...], down_far[...])
    )

    @pl.when(place == pl.num_programs(0) - 1)
    def _():
        gate_f = gate[...].astype(jnp.float32)
        up_f = up[...].astype(jnp.float32)
        sigmoid_gate = jax.nn.sigmoid(gate_f)
        grad = total[...]
        out_gate[...] = (
            grad * up_f * sigmoid_gate * (1.0 + gate_f * (1.0 - sigmoid_gate))
        ).astype(jnp.bfloat16)
        out_up[...] = (grad * (gate_f * sigmoid_gate)).astype(jnp.bfloat16)


def shards(
    gate_logits,
    up_projected,
    output_gradient,
    down_matrix,
    adapter_input_factors,
    adapter_output_factors,
    input_moments,
    output_moments,
    batch_tenants,
    tenant_owner_slots,
):
    me = lax.axis_index("dp").astype(jnp.int32)
    core_s = (me & (CORES - 1)).reshape(1)
    y_s = lax.shift_right_logical(lax.axis_index("tensor").astype(jnp.int32), 2).reshape(1)
    rank, hid = adapter_input_factors.shape[1:]
    feat = adapter_output_factors.shape[2]
    tok = gate_logits.shape[0]
    wide = hid + feat
    bf16, f32 = jnp.bfloat16, jnp.float32
    shape = jax.ShapeDtypeStruct

    down_full = lax.all_gather(down_matrix, "dp", axis=1, tiled=True)

    packed, info_v = pl.pallas_call(
        prepare,
        out_shape=(shape((rank, wide + LANES), bf16), shape((8, LANES), jnp.int32)),
        in_specs=[SMEM, SMEM, WHOLE, WHOLE, WHOLE],
        out_specs=(WHOLE, WHOLE),
        compiler_params=params(56),
        name="prepare",
    )(
        batch_tenants,
        tenant_owner_slots,
        batch_tenants.reshape(-1, LANES),
        adapter_input_factors[0],
        adapter_output_factors[0],
    )
    cot_z = lax.all_to_all(
        spread(Z_HI, output_gradient), "tensor", 0, 0, axis_index_groups=ALONG_Z_HI
    )
    info_other_v = lax.ppermute(info_v, "dp", OTHER_CORE)
    info_s, info_other_s = info_v[0, :8], info_other_v[0, :8]
    hidden = (
        jax.nn.silu(gate_logits.astype(f32)) * up_projected.astype(f32)
    ).astype(bf16)
    column = lax.all_gather(packed, "dp", axis_index_groups=ALONG_Z_LO)
    plane = lax.all_gather(column, "dp", axis_index_groups=ALONG_X)
    own = plane.reshape(X * Z_LO, rank, wide + LANES)
    other = lax.ppermute(own, "dp", OTHER_CORE)

    part, pair, totals = pl.pallas_call(
        low_rank,
        out_shape=(
            shape((Y, 2 * rank, tok), f32),
            shape((2 * rank, wide), bf16),
            shape((rank, LANES), f32),
        ),
        in_specs=[SMEM, SMEM, VMEM, VMEM, VMEM, VMEM],
        out_specs=(VMEM, VMEM, VMEM),
        compiler_params=params(),
        name="low_rank",
    )(info_s, core_s, own, other, hidden, output_gradient)

    cot_z, part = lax.optimization_barrier((cot_z, part))
    back = lax.ppermute(cot_z, "tensor", NEXT_Y)
    ahead = lax.ppermute(cot_z, "tensor", LAST_Y)

    sums = jnp.sum(lax.all_to_all(part, "tensor", 0, 0, axis_index_groups=ALONG_Y), axis=0)
    sums = lax.all_gather(sums, "tensor", axis_index_groups=ALONG_Z_HI)
    back, ahead, sums = lax.optimization_barrier((back, ahead, sums))
    half = Z_HI // 2
    far_low = lax.ppermute(back[:half], "tensor", NEXT_Y)
    far_high = lax.ppermute(ahead[half:], "tensor", LAST_Y)

    grad_rows, term = pl.pallas_call(
        terms,
        out_shape=(shape((2 * rank, tok), bf16), shape((2 * rank, wide), f32)),
        in_specs=[SMEM, VMEM, VMEM, VMEM],
        out_specs=(VMEM, VMEM),
        compiler_params=params(),
        name="terms",
    )(info_s, sums, hidden, output_gradient)

    term_other = lax.ppermute(term, "dp", OTHER_CORE)
    outgoing = pl.pallas_call(
        dense,
        out_shape=shape((X * Z_LO, rank, wide), bf16),
        in_specs=[SMEM, SMEM, SMEM, VMEM, VMEM],
        out_specs=VMEM,
        scratch_shapes=[pltpu.VMEM((X * Z_LO, rank, wide), f32)],
        compiler_params=params(),
        name="dense",
    )(info_s, info_other_s, core_s, term, term_other)
    outgoing = outgoing.reshape(X, Z_LO, rank, wide)
    by_x = lax.all_to_all(outgoing, "dp", 0, 0, axis_index_groups=ALONG_X)
    by_x = jnp.sum(by_x.astype(f32), axis=0).astype(bf16)
    incoming = lax.all_to_all(by_x, "dp", 0, 0, axis_index_groups=ALONG_Z_LO)

    new_moments_a, new_moments_b, step_a, step_b = pl.pallas_call(
        adam,
        out_shape=(
            shape(input_moments.shape, f32),
            shape(output_moments.shape, f32),
            shape(adapter_input_factors.shape, f32),
            shape(adapter_output_factors.shape, f32),
        ),
        in_specs=[SMEM, WHOLE, WHOLE, WHOLE, WHOLE],
        out_specs=(WHOLE,) * 4,
        compiler_params=params(56),
        name="adam",
    )(me.reshape(1), totals, incoming, input_moments, output_moments)

    def down_block(ahead_by):
        return pl.BlockSpec(
            (hid, feat),
            lambda place, y_ref: (0, lax.rem(y_ref[0] + ahead_by, Y) * Z_HI + place),
        )

    def by_place(index):
        return pl.BlockSpec((1, tok, feat), lambda place, y_ref: (index(place), 0, 0))

    def whole_of(rows, columns):
        return pl.BlockSpec((rows, columns), lambda place, y_ref: (0, 0))

    grad_gate, grad_up = pl.pallas_call(
        finish,
        out_shape=(shape((tok, hid), bf16), shape((tok, hid), bf16)),
        grid_spec=pltpu.PrefetchScalarGridSpec(
            num_scalar_prefetch=1,
            grid=(Z_HI,),
            in_specs=[
                by_place(lambda place: place),
                by_place(lambda place: place),
                by_place(lambda place: place),
                by_place(lambda place: jnp.minimum(place, half - 1)),
                by_place(lambda place: jnp.maximum(place - half, 0)),
                down_block(0),
                down_block(Y - 1),
                down_block(1),
                down_block(2),
                whole_of(2 * rank, tok),
                whole_of(2 * rank, hid),
                whole_of(tok, hid),
                whole_of(tok, hid),
            ],
            out_specs=[whole_of(tok, hid), whole_of(tok, hid)],
            scratch_shapes=[pltpu.VMEM((tok, hid), f32), pltpu.VMEM((tok, feat), bf16)],
        ),
        compiler_params=params(56),
        name="finish",
    )(
        y_s,
        cot_z,
        back,
        ahead,
        far_low,
        far_high,
        down_full,
        down_full,
        down_full,
        down_full,
        grad_rows,
        pair[:, :hid],
        gate_logits,
        up_projected,
    )
    return (grad_gate, grad_up, new_moments_a, new_moments_b, step_a, step_b)


def solution(mesh):
    placed = (
        P("dp", "tensor"),
        P("dp", "tensor"),
        P("dp", "tensor"),
        P("tensor", "dp"),
        P("dp", None, "tensor"),
        P("dp", None, "tensor"),
        P(None, "dp", None, "tensor"),
        P(None, "dp", None, "tensor"),
        P("dp"),
        P(),
    )
    return jax.shard_map(
        shards,
        mesh=mesh,
        in_specs=placed,
        out_specs=(
            P("dp", "tensor"),
            P("dp", "tensor"),
            P(None, "dp", None, "tensor"),
            P(None, "dp", None, "tensor"),
            P("dp", None, "tensor"),
            P("dp", None, "tensor"),
        ),
        check_vma=False,
    )
```

```python
import functools

import jax
import jax.numpy as jnp
from jax import lax
from jax.experimental import pallas as pl
from jax.experimental.pallas import tpu as pltpu
from jax.sharding import PartitionSpec as P

ADAM_STEP = 10


ADAPTER_SCALE = 2.0
BETA_ONE = 0.9
BETA_TWO = 0.95
ADAM_EPS = 1e-08
X, Z_LO, CORES = 4, 4, 2
Y, Z_HI = 4, 4
COUNT_BASE = 32
LANES = 128
INFO_FIRST, INFO_LAST, INFO_CUT = 0, 1, 2

ALONG_X = [[(x * Z_LO + z) * CORES + c for x in range(X)] for z in range(Z_LO) for c in range(CORES)]
ALONG_Z_LO = [[(x * Z_LO + z) * CORES + c for z in range(Z_LO)] for x in range(X) for c in range(CORES)]
ALONG_Y = [[y * Z_HI + h for y in range(Y)] for h in range(Z_HI)]
ALONG_Z_HI = [[y * Z_HI + h for h in range(Z_HI)] for y in range(Y)]
OTHER_CORE = [(d, d ^ 1) for d in range(X * Z_LO * CORES)]
NEXT_Y = [(y * Z_HI + h, (y + 1) % Y * Z_HI + h) for y in range(Y) for h in range(Z_HI)]
LAST_Y = [(y * Z_HI + h, (y - 1) % Y * Z_HI + h) for y in range(Y) for h in range(Z_HI)]

VMEM = pl.BlockSpec(memory_space=pltpu.VMEM)
WHOLE = pl.BlockSpec()
SMEM = pl.BlockSpec(memory_space=pltpu.SMEM)


def params(mib=40):
    return pltpu.CompilerParams(vmem_limit_bytes=mib * 1024 * 1024)


def nt_dot(left, right):
    return lax.dot_general(
        left, right, (((1,), (1,)), ((), ())), preferred_element_type=jnp.float32
    )


def tn_dot(left, right):
    return lax.dot_general(
        left, right, (((0,), (0,)), ((), ())), preferred_element_type=jnp.float32
    )


def spread(copies, block):
    return jnp.broadcast_to(block[None], (copies,) + block.shape)


def prepare(tenants_s, owners_s, tenants_v, factor_a, factor_b, packed, info_v):
    tok = tenants_s.shape[0]
    rank, hid = factor_a.shape
    feat = factor_b.shape[1]
    first, last = tenants_s[0], tenants_s[tok - 1]
    slot_first, slot_last = owners_s[first], owners_s[last]
    cut = jnp.sum((tenants_v[...] == first).astype(jnp.int32))
    lane = lax.broadcasted_iota(jnp.int32, (rank, LANES), 1)
    row = lax.broadcasted_iota(jnp.int32, (rank, LANES), 0)
    counts = jnp.where(lane == slot_first, cut, 0) + jnp.where(lane == slot_last, tok - cut, 0)
    high = lax.shift_right_logical(counts, 5)
    digits = jnp.where(row == 0, high, jnp.where(row == 1, counts - COUNT_BASE * high, 0))
    digits = digits.astype(jnp.float32).astype(jnp.bfloat16)
    a = factor_a[...].astype(jnp.bfloat16)
    b = factor_b[...].astype(jnp.bfloat16)
    for copy in range(packed.shape[0]):
        packed[copy, :, :hid] = a
        packed[copy, :, hid : hid + feat] = b
        packed[copy, :, hid + feat :] = digits
    lane_i = lax.broadcasted_iota(jnp.int32, info_v.shape, 1)
    info_v[...] = jnp.where(
        lane_i == INFO_FIRST, slot_first, jnp.where(lane_i == INFO_LAST, slot_last, cut)
    )


def low_rank(info_s, core_s, own, other, hidden, cot, part, pair, totals):
    core = core_s[0]
    rank = own.shape[1]
    hid, feat = hidden.shape[1], cot.shape[1]
    for run, place in enumerate((INFO_FIRST, INFO_LAST)):
        slot = info_s[place]
        chip = lax.shift_right_logical(slot, 1)
        here = (slot & 1) == core
        rows = pl.ds(run * rank, rank)

        @pl.when(here)
        def _():
            pair[rows, :] = own[chip, :, : hid + feat]

        @pl.when(jnp.logical_not(here))
        def _():
            pair[rows, :] = other[chip, :, : hid + feat]

    tok = hidden.shape[0]
    in_first = lax.broadcasted_iota(jnp.int32, (rank, tok), 1) < info_s[INFO_CUT]
    proj = nt_dot(pair[:, :hid], hidden[...])
    grad = nt_dot(pair[:, hid:], cot[...])
    proj = jnp.where(in_first, proj[:rank], proj[rank:])
    grad = jnp.where(in_first, grad[:rank], grad[rank:])
    part[:rank, :] = proj
    part[rank:, :] = grad
    digits = own[:, :, hid + feat :].astype(jnp.float32)
    digits = digits + other[:, :, hid + feat :].astype(jnp.float32)
    totals[...] = jnp.sum(digits, axis=0)


def terms(info_s, sums, hidden, cot, grad_rows, term):
    rank = sums.shape[1] // 2
    hid = hidden.shape[1]
    tok = hidden.shape[0]
    rows = jnp.sum(sums[...], axis=0)
    in_first = lax.broadcasted_iota(jnp.int32, (rank, tok), 1) < info_s[INFO_CUT]
    proj = rows[:rank]
    grad = ADAPTER_SCALE * rows[rank:]
    zero = jnp.zeros_like(proj)

    def by_run(values):
        both = [jnp.where(in_first, values, zero), jnp.where(in_first, zero, values)]
        return jnp.concatenate(both, axis=0).astype(jnp.bfloat16)

    proj, grad = by_run(proj), by_run(grad)
    grad_rows[...] = grad
    term[:, :hid] = jnp.dot(grad, hidden[...], preferred_element_type=jnp.float32)
    wide = hid + cot.shape[1]
    term[:, hid:wide] = ADAPTER_SCALE * jnp.dot(
        proj, cot[...], preferred_element_type=jnp.float32
    )
    term[:rank, wide:] = jnp.full((rank, LANES), info_s[INFO_FIRST], jnp.int32).astype(jnp.float32)
    term[rank:, wide:] = jnp.full((rank, LANES), info_s[INFO_LAST], jnp.int32).astype(jnp.float32)


def dense(core_s, term, term_other, outgoing, total):
    core = core_s[0]
    rank, wide = outgoing.shape[1:]
    total[...] = jnp.zeros_like(total)
    for source in (term, term_other):
        for run in range(2):
            slot = jnp.max(source[run * rank : run * rank + 8, wide:]).astype(jnp.int32)
            chip = lax.shift_right_logical(slot, 1)

            @pl.when((slot & 1) == core)
            def _():
                total[chip] += source[run * rank : (run + 1) * rank, :wide]

    outgoing[...] = total[...].astype(jnp.bfloat16)


def adam(me_s, totals, incoming, moments_a, moments_b, new_a, new_b, step_a, step_b):
    lane = lax.broadcasted_iota(jnp.int32, (1, LANES), 1)
    digit = COUNT_BASE * totals[0:1, :] + totals[1:2, :]
    count = jnp.sum(jnp.where(lane == me_s[0], digit, 0.0))
    active = count > 0.5
    divisor = jnp.maximum(count, 1.0)
    corr_one = 1.0 - BETA_ONE**ADAM_STEP
    corr_two = 1.0 - BETA_TWO**ADAM_STEP
    sums = jnp.sum(incoming[...].astype(jnp.float32), axis=0)
    hid = moments_a.shape[-1]
    for part, moments, new, step in (
        (sums[:, :hid], moments_a, new_a, step_a),
        (sums[:, hid:], moments_b, new_b, step_b),
    ):
        grad = part / divisor
        old_one, old_two = moments[0, 0], moments[1, 0]
        first = jnp.where(active, BETA_ONE * old_one + (1.0 - BETA_ONE) * grad, old_one)
        second = jnp.where(active, BETA_TWO * old_two + (1.0 - BETA_TWO) * grad * grad, old_two)
        update = first / corr_one / (jnp.sqrt(second / corr_two) + ADAM_EPS)
        new[0, 0] = first
        new[1, 0] = second
        step[0] = jnp.where(active, update, 0.0)


def finish(
    place_s, own, back, ahead, far_low, far_high, down_own, down_back, down_ahead, down_far,
    grad_rows, pair_a, gate, up, out_gate, out_up, total, far
):
    place = pl.program_id(0)

    @pl.when(place == 0)
    def _():
        total[...] = tn_dot(grad_rows[...], pair_a[...])

    @pl.when(place < 2)
    def _():
        far[...] = far_low[0]

    @pl.when(place >= 2)
    def _():
        far[...] = far_high[0]

    total[...] += (
        nt_dot(own[0], down_own[...])
        + nt_dot(back[0], down_back[...])
        + nt_dot(ahead[0], down_ahead[...])
        + nt_dot(far[...], down_far[...])
    )

    @pl.when(place == pl.num_programs(0) - 1)
    def _():
        gate_f = gate[...].astype(jnp.float32)
        up_f = up[...].astype(jnp.float32)
        sigmoid_gate = jax.nn.sigmoid(gate_f)
        grad = total[...]
        out_gate[...] = (
            grad * up_f * sigmoid_gate * (1.0 + gate_f * (1.0 - sigmoid_gate))
        ).astype(jnp.bfloat16)
        out_up[...] = (grad * (gate_f * sigmoid_gate)).astype(jnp.bfloat16)


def shards(
    gate_logits,
    up_projected,
    output_gradient,
    down_matrix,
    adapter_input_factors,
    adapter_output_factors,
    input_moments,
    output_moments,
    batch_tenants,
    tenant_owner_slots,
):
    me = lax.axis_index("dp").astype(jnp.int32)
    core_s = (me & (CORES - 1)).reshape(1)
    y_s = lax.shift_right_logical(lax.axis_index("tensor").astype(jnp.int32), 2).reshape(1)
    rank, hid = adapter_input_factors.shape[1:]
    feat = adapter_output_factors.shape[2]
    tok = gate_logits.shape[0]
    wide = hid + feat
    bf16, f32 = jnp.bfloat16, jnp.float32
    shape = jax.ShapeDtypeStruct

    down_full = lax.all_gather(down_matrix, "dp", axis=1, tiled=True)

    packed, info_v = pl.pallas_call(
        prepare,
        out_shape=(shape((Z_LO, rank, wide + LANES), bf16), shape((8, LANES), jnp.int32)),
        in_specs=[SMEM, SMEM, WHOLE, WHOLE, WHOLE],
        out_specs=(WHOLE, WHOLE),
        compiler_params=params(56),
        name="prepare",
    )(
        batch_tenants,
        tenant_owner_slots,
        batch_tenants.reshape(-1, LANES),
        adapter_input_factors[0],
        adapter_output_factors[0],
    )
    column = lax.all_to_all(packed, "dp", 0, 0, axis_index_groups=ALONG_Z_LO)
    column, cot_copies = lax.optimization_barrier((column, spread(Z_HI, output_gradient)))
    cot_z = lax.all_to_all(cot_copies, "tensor", 0, 0, axis_index_groups=ALONG_Z_HI)
    info_s = info_v[0, :8]
    hidden = (
        jax.nn.silu(gate_logits.astype(f32)) * up_projected.astype(f32)
    ).astype(bf16)
    plane = lax.all_gather(column, "dp", axis_index_groups=ALONG_X)
    own = plane.reshape(X * Z_LO, rank, wide + LANES)
    other = lax.ppermute(own, "dp", OTHER_CORE)

    part, pair, totals = pl.pallas_call(
        low_rank,
        out_shape=(
            shape((2 * rank, tok), f32),
            shape((2 * rank, wide), bf16),
            shape((rank, LANES), f32),
        ),
        in_specs=[SMEM, SMEM, VMEM, VMEM, VMEM, VMEM],
        out_specs=(VMEM, VMEM, VMEM),
        compiler_params=params(),
        name="low_rank",
    )(info_s, core_s, own, other, hidden, output_gradient)

    sums = jnp.sum(lax.all_gather(part, "tensor", axis_index_groups=ALONG_Y), axis=0)
    cot_z, sums = lax.optimization_barrier((cot_z, sums))
    back = lax.ppermute(cot_z, "tensor", NEXT_Y)
    ahead = lax.ppermute(cot_z, "tensor", LAST_Y)
    sums = lax.all_gather(sums, "tensor", axis_index_groups=ALONG_Z_HI)
    half = Z_HI // 2
    far_low = lax.ppermute(back[:half], "tensor", NEXT_Y)
    far_high = lax.ppermute(ahead[half:], "tensor", LAST_Y)

    grad_rows, term = pl.pallas_call(
        terms,
        out_shape=(shape((2 * rank, tok), bf16), shape((2 * rank, wide + LANES), f32)),
        in_specs=[SMEM, VMEM, VMEM, VMEM],
        out_specs=(VMEM, VMEM),
        compiler_params=params(),
        name="terms",
    )(info_s, sums, hidden, output_gradient)

    term_other = lax.ppermute(term, "dp", OTHER_CORE)
    outgoing = pl.pallas_call(
        dense,
        out_shape=shape((X * Z_LO, rank, wide), bf16),
        in_specs=[SMEM, VMEM, VMEM],
        out_specs=VMEM,
        scratch_shapes=[pltpu.VMEM((X * Z_LO, rank, wide), f32)],
        compiler_params=params(),
        name="dense",
    )(core_s, term, term_other)
    outgoing = outgoing.reshape(X, Z_LO, rank, wide)
    by_x = lax.all_to_all(outgoing, "dp", 0, 0, axis_index_groups=ALONG_X)
    by_x = jnp.sum(by_x.astype(f32), axis=0).astype(bf16)
    incoming = lax.all_to_all(by_x, "dp", 0, 0, axis_index_groups=ALONG_Z_LO)

    new_moments_a, new_moments_b, step_a, step_b = pl.pallas_call(
        adam,
        out_shape=(
            shape(input_moments.shape, f32),
            shape(output_moments.shape, f32),
            shape(adapter_input_factors.shape, f32),
            shape(adapter_output_factors.shape, f32),
        ),
        in_specs=[SMEM, WHOLE, WHOLE, WHOLE, WHOLE],
        out_specs=(WHOLE,) * 4,
        compiler_params=params(56),
        name="adam",
    )(me.reshape(1), totals, incoming, input_moments, output_moments)

    def down_block(ahead_by):
        return pl.BlockSpec(
            (hid, feat),
            lambda place, y_ref: (0, lax.rem(y_ref[0] + ahead_by, Y) * Z_HI + place),
        )

    def by_place(index):
        return pl.BlockSpec((1, tok, feat), lambda place, y_ref: (index(place), 0, 0))

    def whole_of(rows, columns):
        return pl.BlockSpec((rows, columns), lambda place, y_ref: (0, 0))

    grad_gate, grad_up = pl.pallas_call(
        finish,
        out_shape=(shape((tok, hid), bf16), shape((tok, hid), bf16)),
        grid_spec=pltpu.PrefetchScalarGridSpec(
            num_scalar_prefetch=1,
            grid=(Z_HI,),
            in_specs=[
                by_place(lambda place: place),
                by_place(lambda place: place),
                by_place(lambda place: place),
                by_place(lambda place: jnp.minimum(place, half - 1)),
                by_place(lambda place: jnp.maximum(place - half, 0)),
                down_block(0),
                down_block(Y - 1),
                down_block(1),
                down_block(2),
                whole_of(2 * rank, tok),
                whole_of(2 * rank, hid),
                whole_of(tok, hid),
                whole_of(tok, hid),
            ],
            out_specs=[whole_of(tok, hid), whole_of(tok, hid)],
            scratch_shapes=[pltpu.VMEM((tok, hid), f32), pltpu.VMEM((tok, feat), bf16)],
        ),
        compiler_params=params(56),
        name="finish",
    )(
        y_s,
        cot_z,
        back,
        ahead,
        far_low,
        far_high,
        down_full,
        down_full,
        down_full,
        down_full,
        grad_rows,
        pair[:, :hid],
        gate_logits,
        up_projected,
    )
    return (grad_gate, grad_up, new_moments_a, new_moments_b, step_a, step_b)


def solution(mesh):
    placed = (
        P("dp", "tensor"),
        P("dp", "tensor"),
        P("dp", "tensor"),
        P("tensor", "dp"),
        P("dp", None, "tensor"),
        P("dp", None, "tensor"),
        P(None, "dp", None, "tensor"),
        P(None, "dp", None, "tensor"),
        P("dp"),
        P(),
    )
    return jax.shard_map(
        shards,
        mesh=mesh,
        in_specs=placed,
        out_specs=(
            P("dp", "tensor"),
            P("dp", "tensor"),
            P(None, "dp", None, "tensor"),
            P(None, "dp", None, "tensor"),
            P("dp", None, "tensor"),
            P("dp", None, "tensor"),
        ),
        check_vma=False,
    )
```

```python
import functools

import jax
import jax.numpy as jnp
from jax import lax
from jax.experimental import pallas as pl
from jax.experimental.pallas import tpu as pltpu
from jax.sharding import PartitionSpec as P

ADAM_STEP = 10


ADAPTER_SCALE = 2.0
BETA_ONE = 0.9
BETA_TWO = 0.95
ADAM_EPS = 1e-08
X, Z_LO, CORES = 4, 4, 2
Y, Z_HI = 4, 4
COUNT_BASE = 32
LANES = 128
INFO_FIRST, INFO_LAST, INFO_CUT = 0, 1, 2

ALONG_X = [[(x * Z_LO + z) * CORES + c for x in range(X)] for z in range(Z_LO) for c in range(CORES)]
ALONG_Z_LO = [[(x * Z_LO + z) * CORES + c for z in range(Z_LO)] for x in range(X) for c in range(CORES)]
ALONG_Y = [[y * Z_HI + h for y in range(Y)] for h in range(Z_HI)]
ALONG_Z_HI = [[y * Z_HI + h for h in range(Z_HI)] for y in range(Y)]
OTHER_CORE = [(d, d ^ 1) for d in range(X * Z_LO * CORES)]
SAME_CORE = [[(x * Z_LO + z) * CORES + c for x in range(X) for z in range(Z_LO)] for c in range(CORES)]


def shift_x(by):
    return [
        ((x * Z_LO + z) * CORES + c, ((x + by) % X * Z_LO + z) * CORES + c)
        for x in range(X)
        for z in range(Z_LO)
        for c in range(CORES)
    ]


def shift_z_lo(by):
    return [
        ((x * Z_LO + z) * CORES + c, (x * Z_LO + (z + by) % Z_LO) * CORES + c)
        for x in range(X)
        for z in range(Z_LO)
        for c in range(CORES)
    ]


VMEM = pl.BlockSpec(memory_space=pltpu.VMEM)
WHOLE = pl.BlockSpec()
SMEM = pl.BlockSpec(memory_space=pltpu.SMEM)


def params(mib=40):
    return pltpu.CompilerParams(vmem_limit_bytes=mib * 1024 * 1024)


def nt_dot(left, right):
    return lax.dot_general(
        left, right, (((1,), (1,)), ((), ())), preferred_element_type=jnp.float32
    )


def tn_dot(left, right):
    return lax.dot_general(
        left, right, (((0,), (0,)), ((), ())), preferred_element_type=jnp.float32
    )


def spread(copies, block):
    return jnp.broadcast_to(block[None], (copies,) + block.shape)


def prepare(tenants_s, owners_s, tenants_v, factor_a, factor_b, packed, info_v):
    tok = tenants_s.shape[0]
    rank, hid = factor_a.shape
    feat = factor_b.shape[1]
    first, last = tenants_s[0], tenants_s[tok - 1]
    slot_first, slot_last = owners_s[first], owners_s[last]
    cut = jnp.sum((tenants_v[...] == first).astype(jnp.int32))
    lane = lax.broadcasted_iota(jnp.int32, (rank, LANES), 1)
    row = lax.broadcasted_iota(jnp.int32, (rank, LANES), 0)
    counts = jnp.where(lane == slot_first, cut, 0) + jnp.where(lane == slot_last, tok - cut, 0)
    high = lax.shift_right_logical(counts, 5)
    digits = jnp.where(row == 0, high, jnp.where(row == 1, counts - COUNT_BASE * high, 0))
    digits = digits.astype(jnp.float32).astype(jnp.bfloat16)
    a = factor_a[...].astype(jnp.bfloat16)
    b = factor_b[...].astype(jnp.bfloat16)
    for copy in range(packed.shape[0]):
        packed[copy, :, :hid] = a
        packed[copy, :, hid : hid + feat] = b
        packed[copy, :, hid + feat :] = digits
    lane_i = lax.broadcasted_iota(jnp.int32, info_v.shape, 1)
    info_v[...] = jnp.where(
        lane_i == INFO_FIRST, slot_first, jnp.where(lane_i == INFO_LAST, slot_last, cut)
    )


def low_rank(info_s, place_s, own, other, hidden, cot, part, pair, totals):
    core = place_s[0]
    rank = own.shape[1]
    hid, feat = hidden.shape[1], cot.shape[1]
    for run, place in enumerate((INFO_FIRST, INFO_LAST)):
        slot = info_s[place]
        chip = lax.shift_right_logical(slot, 1)
        here = (slot & 1) == core
        rows = pl.ds(run * rank, rank)

        @pl.when(here)
        def _():
            pair[rows, :] = own[chip, :, : hid + feat]

        @pl.when(jnp.logical_not(here))
        def _():
            pair[rows, :] = other[chip, :, : hid + feat]

    tok = hidden.shape[0]
    in_first = lax.broadcasted_iota(jnp.int32, (rank, tok), 1) < info_s[INFO_CUT]
    proj = nt_dot(pair[:, :hid], hidden[...])
    grad = nt_dot(pair[:, hid:], cot[...])
    proj = jnp.where(in_first, proj[:rank], proj[rank:])
    grad = jnp.where(in_first, grad[:rank], grad[rank:])
    part[:rank, :] = proj
    part[rank:, :] = grad
    digits = own[:, :, hid + feat :].astype(jnp.float32)
    digits = digits + other[:, :, hid + feat :].astype(jnp.float32)
    totals[...] = jnp.sum(digits, axis=0)


def terms(info_s, sums, hidden, cot, grad_rows, term):
    rank = sums.shape[1] // 2
    hid = hidden.shape[1]
    tok = hidden.shape[0]
    rows = jnp.sum(sums[...], axis=0)
    in_first = lax.broadcasted_iota(jnp.int32, (rank, tok), 1) < info_s[INFO_CUT]
    proj = rows[:rank]
    grad = ADAPTER_SCALE * rows[rank:]
    zero = jnp.zeros_like(proj)

    def by_run(values):
        both = [jnp.where(in_first, values, zero), jnp.where(in_first, zero, values)]
        return jnp.concatenate(both, axis=0).astype(jnp.bfloat16)

    proj, grad = by_run(proj), by_run(grad)
    grad_rows[...] = grad
    term[:, :hid] = jnp.dot(grad, hidden[...], preferred_element_type=jnp.float32)
    wide = hid + cot.shape[1]
    term[:, hid:wide] = ADAPTER_SCALE * jnp.dot(
        proj, cot[...], preferred_element_type=jnp.float32
    )
    term[:rank, wide:] = jnp.full((rank, LANES), info_s[INFO_FIRST], jnp.int32).astype(jnp.float32)
    term[rank:, wide:] = jnp.full((rank, LANES), info_s[INFO_LAST], jnp.int32).astype(jnp.float32)


def dense(place_s, term, term_other, stay, next_one, next_two, next_three, total):
    core, x = place_s[0], place_s[1]
    rank, wide = stay.shape[1:]
    total[...] = jnp.zeros_like(total)
    for source in (term, term_other):
        for run in range(2):
            slot = jnp.max(source[run * rank : run * rank + 8, wide:]).astype(jnp.int32)
            chip = lax.shift_right_logical(slot, 1)

            @pl.when((slot & 1) == core)
            def _():
                total[chip] += source[run * rank : (run + 1) * rank, :wide]

    for distance, out in enumerate((stay, next_one, next_two, next_three)):
        target = (x + distance) & (X - 1)
        out[...] = total[pl.ds(target * Z_LO, Z_LO)].astype(jnp.bfloat16)


def merge(place_s, one, two, three, four, stay, next_one, next_two, next_three, total):
    z = place_s[2]
    total[...] = (
        one[...].astype(jnp.float32)
        + two[...].astype(jnp.float32)
        + three[...].astype(jnp.float32)
        + four[...].astype(jnp.float32)
    )
    for distance, out in enumerate((stay, next_one, next_two, next_three)):
        out[...] = total[(z + distance) & (Z_LO - 1)].astype(jnp.bfloat16)


def adam(place_s, totals, one, two, three, four, moments_a, moments_b, new_a, new_b, step_a, step_b):
    lane = lax.broadcasted_iota(jnp.int32, (1, LANES), 1)
    digit = COUNT_BASE * totals[0:1, :] + totals[1:2, :]
    count = jnp.sum(jnp.where(lane == place_s[3], digit, 0.0))
    active = count > 0.5
    divisor = jnp.maximum(count, 1.0)
    corr_one = 1.0 - BETA_ONE**ADAM_STEP
    corr_two = 1.0 - BETA_TWO**ADAM_STEP
    sums = (
        one[...].astype(jnp.float32)
        + two[...].astype(jnp.float32)
        + three[...].astype(jnp.float32)
        + four[...].astype(jnp.float32)
    )
    hid = moments_a.shape[-1]
    for part, moments, new, step in (
        (sums[:, :hid], moments_a, new_a, step_a),
        (sums[:, hid:], moments_b, new_b, step_b),
    ):
        grad = part / divisor
        old_one, old_two = moments[0, 0], moments[1, 0]
        first = jnp.where(active, BETA_ONE * old_one + (1.0 - BETA_ONE) * grad, old_one)
        second = jnp.where(active, BETA_TWO * old_two + (1.0 - BETA_TWO) * grad * grad, old_two)
        update = first / corr_one / (jnp.sqrt(second / corr_two) + ADAM_EPS)
        new[0, 0] = first
        new[1, 0] = second
        step[0] = jnp.where(active, update, 0.0)


def finish(
    place_s, cot, down_own, down_other, grad_rows, pair_a, gate, up, out_gate, out_up, total, weights
):
    place = pl.program_id(0)
    core = place_s[0]
    half = cot.shape[2] // CORES

    @pl.when(place == 0)
    def _():
        total[...] = tn_dot(grad_rows[...], pair_a[...])

    mine = pl.ds(pl.multiple_of(core * half, half), half)
    theirs = pl.ds(pl.multiple_of((1 - core) * half, half), half)
    for block in range(cot.shape[0]):
        weights[block, :, mine] = down_own[:, block * half : (block + 1) * half]
        weights[block, :, theirs] = down_other[:, block * half : (block + 1) * half]
    added = nt_dot(cot[0], weights[0])
    for block in range(1, cot.shape[0]):
        added += nt_dot(cot[block], weights[block])
    total[...] += added

    @pl.when(place == pl.num_programs(0) - 1)
    def _():
        gate_f = gate[...].astype(jnp.float32)
        up_f = up[...].astype(jnp.float32)
        sigmoid_gate = jax.nn.sigmoid(gate_f)
        grad = total[...]
        out_gate[...] = (
            grad * up_f * sigmoid_gate * (1.0 + gate_f * (1.0 - sigmoid_gate))
        ).astype(jnp.bfloat16)
        out_up[...] = (grad * (gate_f * sigmoid_gate)).astype(jnp.bfloat16)


def shards(
    gate_logits,
    up_projected,
    output_gradient,
    down_matrix,
    adapter_input_factors,
    adapter_output_factors,
    input_moments,
    output_moments,
    batch_tenants,
    tenant_owner_slots,
):
    me = lax.axis_index("dp").astype(jnp.int32)
    chip = lax.shift_right_logical(me, 1)
    place_s = jnp.stack([me & (CORES - 1), lax.shift_right_logical(chip, 2), chip & (Z_LO - 1), me])
    rank, hid = adapter_input_factors.shape[1:]
    feat = adapter_output_factors.shape[2]
    tok = gate_logits.shape[0]
    wide = hid + feat
    bf16, f32 = jnp.bfloat16, jnp.float32
    shape = jax.ShapeDtypeStruct

    down_own = lax.all_gather(
        down_matrix, "dp", axis=1, tiled=True, axis_index_groups=SAME_CORE
    )

    packed, info_v = pl.pallas_call(
        prepare,
        out_shape=(shape((Z_LO, rank, wide + LANES), bf16), shape((8, LANES), jnp.int32)),
        in_specs=[SMEM, SMEM, WHOLE, WHOLE, WHOLE],
        out_specs=(WHOLE, WHOLE),
        compiler_params=params(56),
        name="prepare",
    )(
        batch_tenants,
        tenant_owner_slots,
        batch_tenants.reshape(-1, LANES),
        adapter_input_factors[0],
        adapter_output_factors[0],
    )
    column = lax.all_to_all(packed, "dp", 0, 0, axis_index_groups=ALONG_Z_LO)
    column, cot_copies = lax.optimization_barrier((column, spread(Z_HI, output_gradient)))
    cot_z = lax.all_to_all(cot_copies, "tensor", 0, 0, axis_index_groups=ALONG_Z_HI)
    info_s = info_v[0, :8]
    hidden = (
        jax.nn.silu(gate_logits.astype(f32)) * up_projected.astype(f32)
    ).astype(bf16)
    plane = lax.all_gather(column, "dp", axis_index_groups=ALONG_X)
    own = plane.reshape(X * Z_LO, rank, wide + LANES)
    other = lax.ppermute(own, "dp", OTHER_CORE)

    part, pair, totals = pl.pallas_call(
        low_rank,
        out_shape=(
            shape((2 * rank, tok), f32),
            shape((2 * rank, wide), bf16),
            shape((rank, LANES), f32),
        ),
        in_specs=[SMEM, SMEM, VMEM, VMEM, VMEM, VMEM],
        out_specs=(VMEM, VMEM, VMEM),
        compiler_params=params(),
        name="low_rank",
    )(info_s, place_s, own, other, hidden, output_gradient)

    sums = jnp.sum(lax.all_gather(part, "tensor", axis_index_groups=ALONG_Y), axis=0)
    cot_z, sums = lax.optimization_barrier((cot_z, sums))
    cot_all = lax.all_to_all(spread(Y, cot_z), "tensor", 0, 0, axis_index_groups=ALONG_Y)
    sums = lax.all_gather(sums, "tensor", axis_index_groups=ALONG_Z_HI)

    grad_rows, term = pl.pallas_call(
        terms,
        out_shape=(shape((2 * rank, tok), bf16), shape((2 * rank, wide + LANES), f32)),
        in_specs=[SMEM, VMEM, VMEM, VMEM],
        out_specs=(VMEM, VMEM),
        compiler_params=params(),
        name="terms",
    )(info_s, sums, hidden, output_gradient)

    term_other = lax.ppermute(term, "dp", OTHER_CORE)
    down_own, term_other = lax.optimization_barrier((down_own, term_other))
    down_other = lax.ppermute(down_own, "dp", OTHER_CORE)
    block = shape((Z_LO, rank, wide), bf16)
    stay, *leave = pl.pallas_call(
        dense,
        out_shape=(block,) * X,
        in_specs=[SMEM, VMEM, VMEM],
        out_specs=(VMEM,) * X,
        scratch_shapes=[pltpu.VMEM((X * Z_LO, rank, wide), f32)],
        compiler_params=params(),
        name="dense",
    )(place_s, term, term_other)
    arrived = [lax.ppermute(part, "dp", shift_x(by + 1)) for by, part in enumerate(leave)]
    block = shape((rank, wide), bf16)
    stay, *leave = pl.pallas_call(
        merge,
        out_shape=(block,) * Z_LO,
        in_specs=[SMEM] + [VMEM] * X,
        out_specs=(VMEM,) * Z_LO,
        scratch_shapes=[pltpu.VMEM((Z_LO, rank, wide), f32)],
        compiler_params=params(),
        name="merge",
    )(place_s, stay, *arrived)
    arrived = [lax.ppermute(part, "dp", shift_z_lo(by + 1)) for by, part in enumerate(leave)]

    new_moments_a, new_moments_b, step_a, step_b = pl.pallas_call(
        adam,
        out_shape=(
            shape(input_moments.shape, f32),
            shape(output_moments.shape, f32),
            shape(adapter_input_factors.shape, f32),
            shape(adapter_output_factors.shape, f32),
        ),
        in_specs=[SMEM] + [WHOLE] * 7,
        out_specs=(WHOLE,) * 4,
        compiler_params=params(56),
        name="adam",
    )(place_s, totals, stay, *arrived, input_moments, output_moments)

    def whole_of(rows, columns):
        return pl.BlockSpec((rows, columns), lambda place, place_ref: (0, 0))

    def down_part():
        return pl.BlockSpec((hid, Z_HI * feat // CORES), lambda place, place_ref: (0, place))

    grad_gate, grad_up = pl.pallas_call(
        finish,
        out_shape=(shape((tok, hid), bf16), shape((tok, hid), bf16)),
        grid_spec=pltpu.PrefetchScalarGridSpec(
            num_scalar_prefetch=1,
            grid=(Y,),
            in_specs=[
                pl.BlockSpec((Z_HI, tok, feat), lambda place, place_ref: (place, 0, 0)),
                down_part(),
                down_part(),
                whole_of(2 * rank, tok),
                whole_of(2 * rank, hid),
                whole_of(tok, hid),
                whole_of(tok, hid),
            ],
            out_specs=[whole_of(tok, hid), whole_of(tok, hid)],
            scratch_shapes=[pltpu.VMEM((tok, hid), f32), pltpu.VMEM((Z_HI, hid, feat), bf16)],
        ),
        compiler_params=params(56),
        name="finish",
    )(
        place_s,
        cot_all.reshape(Y * Z_HI, tok, feat),
        down_own,
        down_other,
        grad_rows,
        pair[:, :hid],
        gate_logits,
        up_projected,
    )
    return (grad_gate, grad_up, new_moments_a, new_moments_b, step_a, step_b)


def solution(mesh):
    placed = (
        P("dp", "tensor"),
        P("dp", "tensor"),
        P("dp", "tensor"),
        P("tensor", "dp"),
        P("dp", None, "tensor"),
        P("dp", None, "tensor"),
        P(None, "dp", None, "tensor"),
        P(None, "dp", None, "tensor"),
        P("dp"),
        P(),
    )
    return jax.shard_map(
        shards,
        mesh=mesh,
        in_specs=placed,
        out_specs=(
            P("dp", "tensor"),
            P("dp", "tensor"),
            P(None, "dp", None, "tensor"),
            P(None, "dp", None, "tensor"),
            P("dp", None, "tensor"),
            P("dp", None, "tensor"),
        ),
        check_vma=False,
    )
```

```python
import functools

import jax
import jax.numpy as jnp
from jax import lax
from jax.experimental import pallas as pl
from jax.experimental.pallas import tpu as pltpu
from jax.sharding import PartitionSpec as P

ADAM_STEP = 10


ADAPTER_SCALE = 2.0
BETA_ONE = 0.9
BETA_TWO = 0.95
ADAM_EPS = 1e-08
X, Z_LO, CORES = 4, 4, 2
Y, Z_HI = 4, 4
COUNT_BASE = 32
LANES = 128
INFO_FIRST, INFO_LAST, INFO_CUT = 0, 1, 2

ALONG_X = [[(x * Z_LO + z) * CORES + c for x in range(X)] for z in range(Z_LO) for c in range(CORES)]
ALONG_Z_LO = [[(x * Z_LO + z) * CORES + c for z in range(Z_LO)] for x in range(X) for c in range(CORES)]
ALONG_Y = [[y * Z_HI + h for y in range(Y)] for h in range(Z_HI)]
ALONG_Z_HI = [[y * Z_HI + h for h in range(Z_HI)] for y in range(Y)]
OTHER_CORE = [(d, d ^ 1) for d in range(X * Z_LO * CORES)]
NEXT_Y = [(y * Z_HI + h, (y + 1) % Y * Z_HI + h) for y in range(Y) for h in range(Z_HI)]
LAST_Y = [(y * Z_HI + h, (y - 1) % Y * Z_HI + h) for y in range(Y) for h in range(Z_HI)]

VMEM = pl.BlockSpec(memory_space=pltpu.VMEM)
WHOLE = pl.BlockSpec()
SMEM = pl.BlockSpec(memory_space=pltpu.SMEM)


def params(mib=40):
    return pltpu.CompilerParams(vmem_limit_bytes=mib * 1024 * 1024)


def nt_dot(left, right):
    return lax.dot_general(
        left, right, (((1,), (1,)), ((), ())), preferred_element_type=jnp.float32
    )


def tn_dot(left, right):
    return lax.dot_general(
        left, right, (((0,), (0,)), ((), ())), preferred_element_type=jnp.float32
    )


def spread(copies, block):
    return jnp.broadcast_to(block[None], (copies,) + block.shape)


def prepare(tenants_s, owners_s, tenants_v, factor_a, factor_b, packed, info_v):
    tok = tenants_s.shape[0]
    rank, hid = factor_a.shape
    feat = factor_b.shape[1]
    first, last = tenants_s[0], tenants_s[tok - 1]
    slot_first, slot_last = owners_s[first], owners_s[last]
    cut = jnp.sum((tenants_v[...] == first).astype(jnp.int32))
    lane = lax.broadcasted_iota(jnp.int32, (rank, LANES), 1)
    row = lax.broadcasted_iota(jnp.int32, (rank, LANES), 0)
    counts = jnp.where(lane == slot_first, cut, 0) + jnp.where(lane == slot_last, tok - cut, 0)
    high = lax.shift_right_logical(counts, 5)
    digits = jnp.where(row == 0, high, jnp.where(row == 1, counts - COUNT_BASE * high, 0))
    digits = digits.astype(jnp.float32).astype(jnp.bfloat16)
    a = factor_a[...].astype(jnp.bfloat16)
    b = factor_b[...].astype(jnp.bfloat16)
    for copy in range(packed.shape[0]):
        packed[copy, :, :hid] = a
        packed[copy, :, hid : hid + feat] = b
        packed[copy, :, hid + feat :] = digits
    lane_i = lax.broadcasted_iota(jnp.int32, info_v.shape, 1)
    info_v[...] = jnp.where(
        lane_i == INFO_FIRST, slot_first, jnp.where(lane_i == INFO_LAST, slot_last, cut)
    )


def low_rank(info_s, core_s, own, other, hidden, cot, part, pair, totals):
    core = core_s[0]
    rank = own.shape[1]
    hid, feat = hidden.shape[1], cot.shape[1]
    for run, place in enumerate((INFO_FIRST, INFO_LAST)):
        slot = info_s[place]
        chip = lax.shift_right_logical(slot, 1)
        here = (slot & 1) == core
        rows = pl.ds(run * rank, rank)

        @pl.when(here)
        def _():
            pair[rows, :] = own[chip, :, : hid + feat]

        @pl.when(jnp.logical_not(here))
        def _():
            pair[rows, :] = other[chip, :, : hid + feat]

    tok = hidden.shape[0]
    in_first = lax.broadcasted_iota(jnp.int32, (rank, tok), 1) < info_s[INFO_CUT]
    proj = nt_dot(pair[:, :hid], hidden[...])
    grad = nt_dot(pair[:, hid:], cot[...])
    proj = jnp.where(in_first, proj[:rank], proj[rank:])
    grad = jnp.where(in_first, grad[:rank], grad[rank:])
    part[:rank, :] = proj
    part[rank:, :] = grad
    digits = own[:, :, hid + feat :].astype(jnp.float32)
    digits = digits + other[:, :, hid + feat :].astype(jnp.float32)
    totals[...] = jnp.sum(digits, axis=0)


def terms(info_s, sums, hidden, cot, grad_rows, term):
    rank = sums.shape[1] // 4
    hid = hidden.shape[1]
    tok = hidden.shape[0]
    rows = jnp.sum(sums[...].astype(jnp.float32), axis=0)
    rows = rows[: 2 * rank] + rows[2 * rank :]
    in_first = lax.broadcasted_iota(jnp.int32, (rank, tok), 1) < info_s[INFO_CUT]
    proj = rows[:rank]
    grad = ADAPTER_SCALE * rows[rank:]
    zero = jnp.zeros_like(proj)

    def by_run(values):
        both = [jnp.where(in_first, values, zero), jnp.where(in_first, zero, values)]
        return jnp.concatenate(both, axis=0).astype(jnp.bfloat16)

    proj, grad = by_run(proj), by_run(grad)
    grad_rows[...] = grad
    term[:, :hid] = jnp.dot(grad, hidden[...], preferred_element_type=jnp.float32)
    wide = hid + cot.shape[1]
    term[:, hid:wide] = ADAPTER_SCALE * jnp.dot(
        proj, cot[...], preferred_element_type=jnp.float32
    )
    term[:rank, wide:] = jnp.full((rank, LANES), info_s[INFO_FIRST], jnp.int32).astype(jnp.float32)
    term[rank:, wide:] = jnp.full((rank, LANES), info_s[INFO_LAST], jnp.int32).astype(jnp.float32)


def dense(core_s, term, term_other, outgoing, total):
    core = core_s[0]
    rank, wide = outgoing.shape[1:]
    total[...] = jnp.zeros_like(total)
    for source in (term, term_other):
        for run in range(2):
            slot = jnp.max(source[run * rank : run * rank + 8, wide:]).astype(jnp.int32)
            chip = lax.shift_right_logical(slot, 1)

            @pl.when((slot & 1) == core)
            def _():
                total[chip] += source[run * rank : (run + 1) * rank, :wide]

    outgoing[...] = total[...].astype(jnp.bfloat16)


def adam(me_s, totals, incoming, moments_a, moments_b, new_a, new_b, step_a, step_b):
    lane = lax.broadcasted_iota(jnp.int32, (1, LANES), 1)
    digit = COUNT_BASE * totals[0:1, :] + totals[1:2, :]
    count = jnp.sum(jnp.where(lane == me_s[0], digit, 0.0))
    active = count > 0.5
    divisor = jnp.maximum(count, 1.0)
    corr_one = 1.0 - BETA_ONE**ADAM_STEP
    corr_two = 1.0 - BETA_TWO**ADAM_STEP
    sums = jnp.sum(incoming[...].astype(jnp.float32), axis=0)
    hid = moments_a.shape[-1]
    for part, moments, new, step in (
        (sums[:, :hid], moments_a, new_a, step_a),
        (sums[:, hid:], moments_b, new_b, step_b),
    ):
        grad = part / divisor
        old_one, old_two = moments[0, 0], moments[1, 0]
        first = jnp.where(active, BETA_ONE * old_one + (1.0 - BETA_ONE) * grad, old_one)
        second = jnp.where(active, BETA_TWO * old_two + (1.0 - BETA_TWO) * grad * grad, old_two)
        update = first / corr_one / (jnp.sqrt(second / corr_two) + ADAM_EPS)
        new[0, 0] = first
        new[1, 0] = second
        step[0] = jnp.where(active, update, 0.0)


def finish(place_s, *refs):
    halves, refs = (refs[0:5], refs[5:10]), refs[10:]
    down, refs = refs[:4], refs[4:]
    grad_rows, pair_a, gate, up, out_gate, out_up, total, far = refs
    place = pl.program_id(0)
    rows = far.shape[0]

    @pl.when(place == 0)
    def _():
        total[...] = tn_dot(grad_rows[...], pair_a[...])

    for half, (own, back, ahead, far_low, far_high) in enumerate(halves):

        @pl.when(place < 2)
        def _():
            far[...] = far_low[0]

        @pl.when(place >= 2)
        def _():
            far[...] = far_high[0]

        total[half * rows : (half + 1) * rows, :] += (
            nt_dot(own[0], down[0][...])
            + nt_dot(back[0], down[1][...])
            + nt_dot(ahead[0], down[2][...])
            + nt_dot(far[...], down[3][...])
        )

    @pl.when(place == pl.num_programs(0) - 1)
    def _():
        gate_f = gate[...].astype(jnp.float32)
        up_f = up[...].astype(jnp.float32)
        sigmoid_gate = jax.nn.sigmoid(gate_f)
        grad = total[...]
        out_gate[...] = (
            grad * up_f * sigmoid_gate * (1.0 + gate_f * (1.0 - sigmoid_gate))
        ).astype(jnp.bfloat16)
        out_up[...] = (grad * (gate_f * sigmoid_gate)).astype(jnp.bfloat16)


def shards(
    gate_logits,
    up_projected,
    output_gradient,
    down_matrix,
    adapter_input_factors,
    adapter_output_factors,
    input_moments,
    output_moments,
    batch_tenants,
    tenant_owner_slots,
):
    me = lax.axis_index("dp").astype(jnp.int32)
    core_s = (me & (CORES - 1)).reshape(1)
    y_s = lax.shift_right_logical(lax.axis_index("tensor").astype(jnp.int32), 2).reshape(1)
    rank, hid = adapter_input_factors.shape[1:]
    feat = adapter_output_factors.shape[2]
    tok = gate_logits.shape[0]
    wide = hid + feat
    bf16, f32 = jnp.bfloat16, jnp.float32
    shape = jax.ShapeDtypeStruct

    packed, info_v = pl.pallas_call(
        prepare,
        out_shape=(shape((Z_LO, rank, wide + LANES), bf16), shape((8, LANES), jnp.int32)),
        in_specs=[SMEM, SMEM, WHOLE, WHOLE, WHOLE],
        out_specs=(WHOLE, WHOLE),
        compiler_params=params(56),
        name="prepare",
    )(
        batch_tenants,
        tenant_owner_slots,
        batch_tenants.reshape(-1, LANES),
        adapter_input_factors[0],
        adapter_output_factors[0],
    )
    column = lax.all_to_all(packed, "dp", 0, 0, axis_index_groups=ALONG_Z_LO)
    half = tok // 2
    column, first_half, down = lax.optimization_barrier(
        (column, spread(Z_HI, output_gradient[:half]), down_matrix)
    )
    cot_first = lax.all_to_all(first_half, "tensor", 0, 0, axis_index_groups=ALONG_Z_HI)
    info_s = info_v[0, :8]
    gate_f = gate_logits.astype(f32)
    hidden = (jax.nn.silu(gate_f) * up_projected.astype(f32)).astype(bf16)
    plane = lax.all_gather(column, "dp", axis_index_groups=ALONG_X)
    own = plane.reshape(X * Z_LO, rank, wide + LANES)
    down_full = lax.all_gather(down, "dp", axis=1, tiled=True)
    other = lax.ppermute(own, "dp", OTHER_CORE)

    part, pair, totals = pl.pallas_call(
        low_rank,
        out_shape=(
            shape((2 * rank, tok), f32),
            shape((2 * rank, wide), bf16),
            shape((rank, LANES), f32),
        ),
        in_specs=[SMEM, SMEM, VMEM, VMEM, VMEM, VMEM],
        out_specs=(VMEM, VMEM, VMEM),
        compiler_params=params(),
        name="low_rank",
    )(info_s, core_s, own, other, hidden, output_gradient)

    sums = jnp.sum(lax.all_gather(part, "tensor", axis_index_groups=ALONG_Y), axis=0)
    value = sums.astype(bf16)
    remainder = (sums - value.astype(f32)).astype(bf16)
    packed_sums = jnp.concatenate([value, remainder]).reshape(-1, feat)
    second_half = jnp.concatenate([output_gradient[half:], packed_sums])
    cot_first, second_half = lax.optimization_barrier((cot_first, second_half))
    arrived = lax.all_to_all(
        spread(Z_HI, second_half), "tensor", 0, 0, axis_index_groups=ALONG_Z_HI
    )
    cot_second = arrived[:, :half]
    sums = arrived[:, half:].reshape(Z_HI, 4 * rank, tok)

    def near_y(blocks):
        return lax.ppermute(blocks, "tensor", NEXT_Y), lax.ppermute(blocks, "tensor", LAST_Y)

    def far_y(back, ahead):
        low = lax.ppermute(back[: Z_HI // 2], "tensor", NEXT_Y)
        high = lax.ppermute(ahead[Z_HI // 2 :], "tensor", LAST_Y)
        return low, high

    near_first, sums = lax.optimization_barrier((near_y(cot_first), sums))
    far_first = far_y(*near_first)
    near_second = near_y(cot_second)
    far_second = far_y(*near_second)

    grad_rows, term = pl.pallas_call(
        terms,
        out_shape=(shape((2 * rank, tok), bf16), shape((2 * rank, wide + LANES), f32)),
        in_specs=[SMEM, VMEM, VMEM, VMEM],
        out_specs=(VMEM, VMEM),
        compiler_params=params(),
        name="terms",
    )(info_s, sums, hidden, output_gradient)

    term_other = lax.ppermute(term, "dp", OTHER_CORE)
    outgoing = pl.pallas_call(
        dense,
        out_shape=shape((X * Z_LO, rank, wide), bf16),
        in_specs=[SMEM, VMEM, VMEM],
        out_specs=VMEM,
        scratch_shapes=[pltpu.VMEM((X * Z_LO, rank, wide), f32)],
        compiler_params=params(),
        name="dense",
    )(core_s, term, term_other)
    outgoing = outgoing.reshape(X, Z_LO, rank, wide)
    by_x = lax.all_to_all(outgoing, "dp", 0, 0, axis_index_groups=ALONG_X)
    by_x = jnp.sum(by_x.astype(f32), axis=0).astype(bf16)
    far_first, by_x = lax.optimization_barrier((far_first, by_x))
    incoming = lax.all_to_all(by_x, "dp", 0, 0, axis_index_groups=ALONG_Z_LO)

    new_moments_a, new_moments_b, step_a, step_b = pl.pallas_call(
        adam,
        out_shape=(
            shape(input_moments.shape, f32),
            shape(output_moments.shape, f32),
            shape(adapter_input_factors.shape, f32),
            shape(adapter_output_factors.shape, f32),
        ),
        in_specs=[SMEM, WHOLE, WHOLE, WHOLE, WHOLE],
        out_specs=(WHOLE,) * 4,
        compiler_params=params(56),
        name="adam",
    )(me.reshape(1), totals, incoming, input_moments, output_moments)

    def down_block(ahead_by):
        return pl.BlockSpec(
            (hid, feat),
            lambda place, y_ref: (0, lax.rem(y_ref[0] + ahead_by, Y) * Z_HI + place),
        )

    def by_place(index):
        return pl.BlockSpec((1, half, feat), lambda place, y_ref: (index(place), 0, 0))

    half_specs = [
        by_place(lambda place: place),
        by_place(lambda place: place),
        by_place(lambda place: place),
        by_place(lambda place: jnp.minimum(place, Z_HI // 2 - 1)),
        by_place(lambda place: jnp.maximum(place - Z_HI // 2, 0)),
    ]

    def whole_of(rows, columns):
        return pl.BlockSpec((rows, columns), lambda place, y_ref: (0, 0))

    grad_gate, grad_up = pl.pallas_call(
        finish,
        out_shape=(shape((tok, hid), bf16), shape((tok, hid), bf16)),
        grid_spec=pltpu.PrefetchScalarGridSpec(
            num_scalar_prefetch=1,
            grid=(Z_HI,),
            in_specs=[
                *half_specs,
                *half_specs,
                down_block(0),
                down_block(Y - 1),
                down_block(1),
                down_block(2),
                whole_of(2 * rank, tok),
                whole_of(2 * rank, hid),
                whole_of(tok, hid),
                whole_of(tok, hid),
            ],
            out_specs=[whole_of(tok, hid), whole_of(tok, hid)],
            scratch_shapes=[pltpu.VMEM((tok, hid), f32), pltpu.VMEM((half, feat), bf16)],
        ),
        compiler_params=params(56),
        name="finish",
    )(
        y_s,
        cot_first,
        *near_first,
        *far_first,
        cot_second,
        *near_second,
        *far_second,
        down_full,
        down_full,
        down_full,
        down_full,
        grad_rows,
        pair[:, :hid],
        gate_logits,
        up_projected,
    )
    return (grad_gate, grad_up, new_moments_a, new_moments_b, step_a, step_b)


def solution(mesh):
    placed = (
        P("dp", "tensor"),
        P("dp", "tensor"),
        P("dp", "tensor"),
        P("tensor", "dp"),
        P("dp", None, "tensor"),
        P("dp", None, "tensor"),
        P(None, "dp", None, "tensor"),
        P(None, "dp", None, "tensor"),
        P("dp"),
        P(),
    )
    return jax.shard_map(
        shards,
        mesh=mesh,
        in_specs=placed,
        out_specs=(
            P("dp", "tensor"),
            P("dp", "tensor"),
            P(None, "dp", None, "tensor"),
            P(None, "dp", None, "tensor"),
            P("dp", None, "tensor"),
            P("dp", None, "tensor"),
        ),
        check_vma=False,
    )
```

```python
import functools

import jax
import jax.numpy as jnp
from jax import lax
from jax.experimental import pallas as pl
from jax.experimental.pallas import tpu as pltpu
from jax.sharding import PartitionSpec as P

ADAM_STEP = 10


ADAPTER_SCALE = 2.0
BETA_ONE = 0.9
BETA_TWO = 0.95
ADAM_EPS = 1e-08
X, Z_LO, CORES = 4, 4, 2
Y, Z_HI = 4, 4
COUNT_BASE = 32
LANES = 128
INFO_FIRST, INFO_LAST, INFO_CUT = 0, 1, 2

ALONG_X = [[(x * Z_LO + z) * CORES + c for x in range(X)] for z in range(Z_LO) for c in range(CORES)]
ALONG_Z_LO = [[(x * Z_LO + z) * CORES + c for z in range(Z_LO)] for x in range(X) for c in range(CORES)]
ALONG_Y = [[y * Z_HI + h for y in range(Y)] for h in range(Z_HI)]
ALONG_Z_HI = [[y * Z_HI + h for h in range(Z_HI)] for y in range(Y)]
OTHER_CORE = [(d, d ^ 1) for d in range(X * Z_LO * CORES)]
NEXT_Y = [(y * Z_HI + h, (y + 1) % Y * Z_HI + h) for y in range(Y) for h in range(Z_HI)]
LAST_Y = [(y * Z_HI + h, (y - 1) % Y * Z_HI + h) for y in range(Y) for h in range(Z_HI)]

VMEM = pl.BlockSpec(memory_space=pltpu.VMEM)
WHOLE = pl.BlockSpec()
SMEM = pl.BlockSpec(memory_space=pltpu.SMEM)


def params(mib=40):
    return pltpu.CompilerParams(vmem_limit_bytes=mib * 1024 * 1024)


def nt_dot(left, right):
    return lax.dot_general(
        left, right, (((1,), (1,)), ((), ())), preferred_element_type=jnp.float32
    )


def tn_dot(left, right):
    return lax.dot_general(
        left, right, (((0,), (0,)), ((), ())), preferred_element_type=jnp.float32
    )


def spread(copies, block):
    return jnp.broadcast_to(block[None], (copies,) + block.shape)


def prepare(tenants_s, owners_s, tenants_v, factor_a, factor_b, packed, info_v):
    tok = tenants_s.shape[0]
    rank, hid = factor_a.shape
    feat = factor_b.shape[1]
    first, last = tenants_s[0], tenants_s[tok - 1]
    slot_first, slot_last = owners_s[first], owners_s[last]
    cut = jnp.sum((tenants_v[...] == first).astype(jnp.int32))
    lane = lax.broadcasted_iota(jnp.int32, (rank, LANES), 1)
    row = lax.broadcasted_iota(jnp.int32, (rank, LANES), 0)
    counts = jnp.where(lane == slot_first, cut, 0) + jnp.where(lane == slot_last, tok - cut, 0)
    high = lax.shift_right_logical(counts, 5)
    digits = jnp.where(row == 0, high, jnp.where(row == 1, counts - COUNT_BASE * high, 0))
    digits = digits.astype(jnp.float32).astype(jnp.bfloat16)
    a = factor_a[...].astype(jnp.bfloat16)
    b = factor_b[...].astype(jnp.bfloat16)
    for copy in range(packed.shape[0]):
        packed[copy, :, :hid] = a
        packed[copy, :, hid : hid + feat] = b
        packed[copy, :, hid + feat :] = digits
    lane_i = lax.broadcasted_iota(jnp.int32, info_v.shape, 1)
    info_v[...] = jnp.where(
        lane_i == INFO_FIRST, slot_first, jnp.where(lane_i == INFO_LAST, slot_last, cut)
    )


def low_rank(info_s, core_s, own, other, hidden, cot, part, pair, totals):
    core = core_s[0]
    rank = own.shape[1]
    hid, feat = hidden.shape[1], cot.shape[1]
    for run, place in enumerate((INFO_FIRST, INFO_LAST)):
        slot = info_s[place]
        chip = lax.shift_right_logical(slot, 1)
        here = (slot & 1) == core
        rows = pl.ds(run * rank, rank)

        @pl.when(here)
        def _():
            pair[rows, :] = own[chip, :, : hid + feat]

        @pl.when(jnp.logical_not(here))
        def _():
            pair[rows, :] = other[chip, :, : hid + feat]

    tok = hidden.shape[0]
    in_first = lax.broadcasted_iota(jnp.int32, (rank, tok), 1) < info_s[INFO_CUT]
    proj = nt_dot(pair[:, :hid], hidden[...])
    grad = nt_dot(pair[:, hid:], cot[...])
    proj = jnp.where(in_first, proj[:rank], proj[rank:])
    grad = jnp.where(in_first, grad[:rank], grad[rank:])
    part[:rank, :] = proj
    part[rank:, :] = grad
    digits = own[:, :, hid + feat :].astype(jnp.float32)
    digits = digits + other[:, :, hid + feat :].astype(jnp.float32)
    totals[...] = jnp.sum(digits, axis=0)


def terms(info_s, sums, hidden, cot, grad_rows, term):
    rank = sums.shape[1] // 2
    hid = hidden.shape[1]
    tok = hidden.shape[0]
    rows = jnp.sum(sums[...], axis=0)
    in_first = lax.broadcasted_iota(jnp.int32, (rank, tok), 1) < info_s[INFO_CUT]
    proj = rows[:rank]
    grad = ADAPTER_SCALE * rows[rank:]
    zero = jnp.zeros_like(proj)

    def by_run(values):
        both = [jnp.where(in_first, values, zero), jnp.where(in_first, zero, values)]
        return jnp.concatenate(both, axis=0).astype(jnp.bfloat16)

    proj, grad = by_run(proj), by_run(grad)
    grad_rows[...] = grad
    term[:, :hid] = jnp.dot(grad, hidden[...], preferred_element_type=jnp.float32)
    wide = hid + cot.shape[1]
    term[:, hid:wide] = ADAPTER_SCALE * jnp.dot(
        proj, cot[...], preferred_element_type=jnp.float32
    )
    term[:rank, wide:] = jnp.full((rank, LANES), info_s[INFO_FIRST], jnp.int32).astype(jnp.float32)
    term[rank:, wide:] = jnp.full((rank, LANES), info_s[INFO_LAST], jnp.int32).astype(jnp.float32)


def dense(core_s, term, term_other, outgoing, total):
    core = core_s[0]
    rank, wide = outgoing.shape[1:]
    total[...] = jnp.zeros_like(total)
    for source in (term, term_other):
        for run in range(2):
            slot = jnp.max(source[run * rank : run * rank + 8, wide:]).astype(jnp.int32)
            chip = lax.shift_right_logical(slot, 1)

            @pl.when((slot & 1) == core)
            def _():
                total[chip] += source[run * rank : (run + 1) * rank, :wide]

    outgoing[...] = total[...].astype(jnp.bfloat16)


def adam(me_s, totals, incoming, moments_a, moments_b, new_a, new_b, step_a, step_b):
    lane = lax.broadcasted_iota(jnp.int32, (1, LANES), 1)
    digit = COUNT_BASE * totals[0:1, :] + totals[1:2, :]
    count = jnp.sum(jnp.where(lane == me_s[0], digit, 0.0))
    active = count > 0.5
    divisor = jnp.maximum(count, 1.0)
    corr_one = 1.0 - BETA_ONE**ADAM_STEP
    corr_two = 1.0 - BETA_TWO**ADAM_STEP
    sums = jnp.sum(incoming[...].astype(jnp.float32), axis=0)
    hid = moments_a.shape[-1]
    for part, moments, new, step in (
        (sums[:, :hid], moments_a, new_a, step_a),
        (sums[:, hid:], moments_b, new_b, step_b),
    ):
        grad = part / divisor
        old_one, old_two = moments[0, 0], moments[1, 0]
        first = jnp.where(active, BETA_ONE * old_one + (1.0 - BETA_ONE) * grad, old_one)
        second = jnp.where(active, BETA_TWO * old_two + (1.0 - BETA_TWO) * grad * grad, old_two)
        update = first / corr_one / (jnp.sqrt(second / corr_two) + ADAM_EPS)
        new[0, 0] = first
        new[1, 0] = second
        step[0] = jnp.where(active, update, 0.0)


def finish(
    place_s, own, back, ahead, far_low, far_high, down_own, down_back, down_ahead, down_far,
    grad_rows, pair_a, gate, up, out_gate, out_up, total, far
):
    place = pl.program_id(0)

    @pl.when(place == 0)
    def _():
        total[...] = tn_dot(grad_rows[...], pair_a[...])

    @pl.when(place < 2)
    def _():
        far[...] = far_low[0]

    @pl.when(place >= 2)
    def _():
        far[...] = far_high[0]

    total[...] += (
        nt_dot(own[0], down_own[...])
        + nt_dot(back[0], down_back[...])
        + nt_dot(ahead[0], down_ahead[...])
        + nt_dot(far[...], down_far[...])
    )

    @pl.when(place == pl.num_programs(0) - 1)
    def _():
        gate_f = gate[...].astype(jnp.float32)
        up_f = up[...].astype(jnp.float32)
        sigmoid_gate = jax.nn.sigmoid(gate_f)
        grad = total[...]
        out_gate[...] = (
            grad * up_f * sigmoid_gate * (1.0 + gate_f * (1.0 - sigmoid_gate))
        ).astype(jnp.bfloat16)
        out_up[...] = (grad * (gate_f * sigmoid_gate)).astype(jnp.bfloat16)


def shards(
    gate_logits,
    up_projected,
    output_gradient,
    down_matrix,
    adapter_input_factors,
    adapter_output_factors,
    input_moments,
    output_moments,
    batch_tenants,
    tenant_owner_slots,
):
    me = lax.axis_index("dp").astype(jnp.int32)
    core_s = (me & (CORES - 1)).reshape(1)
    y_s = lax.shift_right_logical(lax.axis_index("tensor").astype(jnp.int32), 2).reshape(1)
    rank, hid = adapter_input_factors.shape[1:]
    feat = adapter_output_factors.shape[2]
    tok = gate_logits.shape[0]
    wide = hid + feat
    bf16, f32 = jnp.bfloat16, jnp.float32
    shape = jax.ShapeDtypeStruct

    down_full = lax.all_gather(down_matrix, "dp", axis=1, tiled=True)

    packed, info_v = pl.pallas_call(
        prepare,
        out_shape=(shape((Z_LO, rank, wide + LANES), bf16), shape((8, LANES), jnp.int32)),
        in_specs=[SMEM, SMEM, WHOLE, WHOLE, WHOLE],
        out_specs=(WHOLE, WHOLE),
        compiler_params=params(56),
        name="prepare",
    )(
        batch_tenants,
        tenant_owner_slots,
        batch_tenants.reshape(-1, LANES),
        adapter_input_factors[0],
        adapter_output_factors[0],
    )
    column = lax.all_to_all(packed, "dp", 0, 0, axis_index_groups=ALONG_Z_LO)
    column, cot_copies = lax.optimization_barrier((column, spread(Z_HI, output_gradient)))
    cot_z = lax.all_to_all(cot_copies, "tensor", 0, 0, axis_index_groups=ALONG_Z_HI)
    info_s = info_v[0, :8]
    hidden = (
        jax.nn.silu(gate_logits.astype(f32)) * up_projected.astype(f32)
    ).astype(bf16)
    plane = lax.all_gather(column, "dp", axis_index_groups=ALONG_X)
    own = plane.reshape(X * Z_LO, rank, wide + LANES)
    other = lax.ppermute(own, "dp", OTHER_CORE)

    part, pair, totals = pl.pallas_call(
        low_rank,
        out_shape=(
            shape((2 * rank, tok), f32),
            shape((2 * rank, wide), bf16),
            shape((rank, LANES), f32),
        ),
        in_specs=[SMEM, SMEM, VMEM, VMEM, VMEM, VMEM],
        out_specs=(VMEM, VMEM, VMEM),
        compiler_params=params(),
        name="low_rank",
    )(info_s, core_s, own, other, hidden, output_gradient)

    sums = jnp.sum(lax.all_gather(part, "tensor", axis_index_groups=ALONG_Y), axis=0)
    sums = lax.all_gather(sums, "tensor", axis_index_groups=ALONG_Z_HI)
    cot_z, sums = lax.optimization_barrier((cot_z, sums))
    back = lax.ppermute(cot_z, "tensor", NEXT_Y)
    ahead = lax.ppermute(cot_z, "tensor", LAST_Y)

    grad_rows, term = pl.pallas_call(
        terms,
        out_shape=(shape((2 * rank, tok), bf16), shape((2 * rank, wide + LANES), f32)),
        in_specs=[SMEM, VMEM, VMEM, VMEM],
        out_specs=(VMEM, VMEM),
        compiler_params=params(),
        name="terms",
    )(info_s, sums, hidden, output_gradient)

    term_other = lax.ppermute(term, "dp", OTHER_CORE)
    outgoing = pl.pallas_call(
        dense,
        out_shape=shape((X * Z_LO, rank, wide), bf16),
        in_specs=[SMEM, VMEM, VMEM],
        out_specs=VMEM,
        scratch_shapes=[pltpu.VMEM((X * Z_LO, rank, wide), f32)],
        compiler_params=params(),
        name="dense",
    )(core_s, term, term_other)
    outgoing = outgoing.reshape(X, Z_LO, rank, wide)
    by_x = lax.all_to_all(outgoing, "dp", 0, 0, axis_index_groups=ALONG_X)
    by_x = jnp.sum(by_x.astype(f32), axis=0).astype(bf16)
    back, ahead, by_x = lax.optimization_barrier((back, ahead, by_x))
    half = Z_HI // 2
    far_low = lax.ppermute(back[:half], "tensor", NEXT_Y)
    far_high = lax.ppermute(ahead[half:], "tensor", LAST_Y)
    incoming = lax.all_to_all(by_x, "dp", 0, 0, axis_index_groups=ALONG_Z_LO)

    new_moments_a, new_moments_b, step_a, step_b = pl.pallas_call(
        adam,
        out_shape=(
            shape(input_moments.shape, f32),
            shape(output_moments.shape, f32),
            shape(adapter_input_factors.shape, f32),
            shape(adapter_output_factors.shape, f32),
        ),
        in_specs=[SMEM, WHOLE, WHOLE, WHOLE, WHOLE],
        out_specs=(WHOLE,) * 4,
        compiler_params=params(56),
        name="adam",
    )(me.reshape(1), totals, incoming, input_moments, output_moments)

    def down_block(ahead_by):
        return pl.BlockSpec(
            (hid, feat),
            lambda place, y_ref: (0, lax.rem(y_ref[0] + ahead_by, Y) * Z_HI + place),
        )

    def by_place(index):
        return pl.BlockSpec((1, tok, feat), lambda place, y_ref: (index(place), 0, 0))

    def whole_of(rows, columns):
        return pl.BlockSpec((rows, columns), lambda place, y_ref: (0, 0))

    grad_gate, grad_up = pl.pallas_call(
        finish,
        out_shape=(shape((tok, hid), bf16), shape((tok, hid), bf16)),
        grid_spec=pltpu.PrefetchScalarGridSpec(
            num_scalar_prefetch=1,
            grid=(Z_HI,),
            in_specs=[
                by_place(lambda place: place),
                by_place(lambda place: place),
                by_place(lambda place: place),
                by_place(lambda place: jnp.minimum(place, half - 1)),
                by_place(lambda place: jnp.maximum(place - half, 0)),
                down_block(0),
                down_block(Y - 1),
                down_block(1),
                down_block(2),
                whole_of(2 * rank, tok),
                whole_of(2 * rank, hid),
                whole_of(tok, hid),
                whole_of(tok, hid),
            ],
            out_specs=[whole_of(tok, hid), whole_of(tok, hid)],
            scratch_shapes=[pltpu.VMEM((tok, hid), f32), pltpu.VMEM((tok, feat), bf16)],
        ),
        compiler_params=params(56),
        name="finish",
    )(
        y_s,
        cot_z,
        back,
        ahead,
        far_low,
        far_high,
        down_full,
        down_full,
        down_full,
        down_full,
        grad_rows,
        pair[:, :hid],
        gate_logits,
        up_projected,
    )
    return (grad_gate, grad_up, new_moments_a, new_moments_b, step_a, step_b)


def solution(mesh):
    placed = (
        P("dp", "tensor"),
        P("dp", "tensor"),
        P("dp", "tensor"),
        P("tensor", "dp"),
        P("dp", None, "tensor"),
        P("dp", None, "tensor"),
        P(None, "dp", None, "tensor"),
        P(None, "dp", None, "tensor"),
        P("dp"),
        P(),
    )
    return jax.shard_map(
        shards,
        mesh=mesh,
        in_specs=placed,
        out_specs=(
            P("dp", "tensor"),
            P("dp", "tensor"),
            P(None, "dp", None, "tensor"),
            P(None, "dp", None, "tensor"),
            P("dp", None, "tensor"),
            P("dp", None, "tensor"),
        ),
        check_vma=False,
    )
```

```python
import functools

import jax
import jax.numpy as jnp
from jax import lax
from jax.experimental import pallas as pl
from jax.experimental.pallas import tpu as pltpu
from jax.sharding import PartitionSpec as P

ADAM_STEP = 10


ADAPTER_SCALE = 2.0
BETA_ONE = 0.9
BETA_TWO = 0.95
ADAM_EPS = 1e-08
X, Z_LO, CORES = 4, 4, 2
Y, Z_HI = 4, 4
COUNT_BASE = 32
LANES = 128
INFO_FIRST, INFO_LAST, INFO_CUT = 0, 1, 2

ALONG_X = [[(x * Z_LO + z) * CORES + c for x in range(X)] for z in range(Z_LO) for c in range(CORES)]
ALONG_Z_LO = [[(x * Z_LO + z) * CORES + c for z in range(Z_LO)] for x in range(X) for c in range(CORES)]
ALONG_Y = [[y * Z_HI + h for y in range(Y)] for h in range(Z_HI)]
ALONG_Z_HI = [[y * Z_HI + h for h in range(Z_HI)] for y in range(Y)]
OTHER_CORE = [(d, d ^ 1) for d in range(X * Z_LO * CORES)]
NEXT_Y = [(y * Z_HI + h, (y + 1) % Y * Z_HI + h) for y in range(Y) for h in range(Z_HI)]
LAST_Y = [(y * Z_HI + h, (y - 1) % Y * Z_HI + h) for y in range(Y) for h in range(Z_HI)]

VMEM = pl.BlockSpec(memory_space=pltpu.VMEM)
WHOLE = pl.BlockSpec()
SMEM = pl.BlockSpec(memory_space=pltpu.SMEM)


def params(mib=40):
    return pltpu.CompilerParams(vmem_limit_bytes=mib * 1024 * 1024)


def nt_dot(left, right):
    return lax.dot_general(
        left, right, (((1,), (1,)), ((), ())), preferred_element_type=jnp.float32
    )


def tn_dot(left, right):
    return lax.dot_general(
        left, right, (((0,), (0,)), ((), ())), preferred_element_type=jnp.float32
    )


def spread(copies, block):
    return jnp.broadcast_to(block[None], (copies,) + block.shape)


def prepare(tenants_s, owners_s, tenants_v, factor_a, factor_b, packed, info_v):
    tok = tenants_s.shape[0]
    rank, hid = factor_a.shape
    feat = factor_b.shape[1]
    first, last = tenants_s[0], tenants_s[tok - 1]
    slot_first, slot_last = owners_s[first], owners_s[last]
    cut = jnp.sum((tenants_v[...] == first).astype(jnp.int32))
    lane = lax.broadcasted_iota(jnp.int32, (rank, LANES), 1)
    row = lax.broadcasted_iota(jnp.int32, (rank, LANES), 0)
    counts = jnp.where(lane == slot_first, cut, 0) + jnp.where(lane == slot_last, tok - cut, 0)
    high = lax.shift_right_logical(counts, 5)
    digits = jnp.where(row == 0, high, jnp.where(row == 1, counts - COUNT_BASE * high, 0))
    digits = digits.astype(jnp.float32).astype(jnp.bfloat16)
    a = factor_a[...].astype(jnp.bfloat16)
    b = factor_b[...].astype(jnp.bfloat16)
    for copy in range(packed.shape[0]):
        packed[copy, :, :hid] = a
        packed[copy, :, hid : hid + feat] = b
        packed[copy, :, hid + feat :] = digits
    lane_i = lax.broadcasted_iota(jnp.int32, info_v.shape, 1)
    info_v[...] = jnp.where(
        lane_i == INFO_FIRST, slot_first, jnp.where(lane_i == INFO_LAST, slot_last, cut)
    )


def low_rank(info_s, core_s, own, other, hidden, cot, part, pair, totals):
    core = core_s[0]
    rank = own.shape[1]
    hid, feat = hidden.shape[1], cot.shape[1]
    for run, place in enumerate((INFO_FIRST, INFO_LAST)):
        slot = info_s[place]
        chip = lax.shift_right_logical(slot, 1)
        here = (slot & 1) == core
        rows = pl.ds(run * rank, rank)

        @pl.when(here)
        def _():
            pair[rows, :] = own[chip, :, : hid + feat]

        @pl.when(jnp.logical_not(here))
        def _():
            pair[rows, :] = other[chip, :, : hid + feat]

    tok = hidden.shape[0]
    in_first = lax.broadcasted_iota(jnp.int32, (rank, tok), 1) < info_s[INFO_CUT]
    proj = nt_dot(pair[:, :hid], hidden[...])
    grad = nt_dot(pair[:, hid:], cot[...])
    proj = jnp.where(in_first, proj[:rank], proj[rank:])
    grad = jnp.where(in_first, grad[:rank], grad[rank:])
    part[:rank, :] = proj
    part[rank:, :] = grad
    digits = own[:, :, hid + feat :].astype(jnp.float32)
    digits = digits + other[:, :, hid + feat :].astype(jnp.float32)
    totals[...] = jnp.sum(digits, axis=0)


def terms(info_s, sums, hidden, cot, grad_rows, term):
    rank = sums.shape[1] // 2
    hid = hidden.shape[1]
    tok = hidden.shape[0]
    rows = jnp.sum(sums[...], axis=0)
    in_first = lax.broadcasted_iota(jnp.int32, (rank, tok), 1) < info_s[INFO_CUT]
    proj = rows[:rank]
    grad = ADAPTER_SCALE * rows[rank:]
    zero = jnp.zeros_like(proj)

    def by_run(values):
        both = [jnp.where(in_first, values, zero), jnp.where(in_first, zero, values)]
        return jnp.concatenate(both, axis=0).astype(jnp.bfloat16)

    proj, grad = by_run(proj), by_run(grad)
    grad_rows[...] = grad
    term[:, :hid] = jnp.dot(grad, hidden[...], preferred_element_type=jnp.float32)
    wide = hid + cot.shape[1]
    term[:, hid:wide] = ADAPTER_SCALE * jnp.dot(
        proj, cot[...], preferred_element_type=jnp.float32
    )
    term[:rank, wide:] = jnp.full((rank, LANES), info_s[INFO_FIRST], jnp.int32).astype(jnp.float32)
    term[rank:, wide:] = jnp.full((rank, LANES), info_s[INFO_LAST], jnp.int32).astype(jnp.float32)


def dense(core_s, term, term_other, outgoing, total):
    core = core_s[0]
    rank, wide = outgoing.shape[1:]
    total[...] = jnp.zeros_like(total)
    for source in (term, term_other):
        for run in range(2):
            slot = jnp.max(source[run * rank : run * rank + 8, wide:]).astype(jnp.int32)
            chip = lax.shift_right_logical(slot, 1)

            @pl.when((slot & 1) == core)
            def _():
                total[chip] += source[run * rank : (run + 1) * rank, :wide]

    outgoing[...] = total[...].astype(jnp.bfloat16)


def adam(me_s, totals, incoming, moments_a, moments_b, new_a, new_b, step_a, step_b):
    lane = lax.broadcasted_iota(jnp.int32, (1, LANES), 1)
    digit = COUNT_BASE * totals[0:1, :] + totals[1:2, :]
    count = jnp.sum(jnp.where(lane == me_s[0], digit, 0.0))
    active = count > 0.5
    divisor = jnp.maximum(count, 1.0)
    corr_one = 1.0 - BETA_ONE**ADAM_STEP
    corr_two = 1.0 - BETA_TWO**ADAM_STEP
    sums = jnp.sum(incoming[...].astype(jnp.float32), axis=0)
    hid = moments_a.shape[-1]
    for part, moments, new, step in (
        (sums[:, :hid], moments_a, new_a, step_a),
        (sums[:, hid:], moments_b, new_b, step_b),
    ):
        grad = part / divisor
        old_one, old_two = moments[0, 0], moments[1, 0]
        first = jnp.where(active, BETA_ONE * old_one + (1.0 - BETA_ONE) * grad, old_one)
        second = jnp.where(active, BETA_TWO * old_two + (1.0 - BETA_TWO) * grad * grad, old_two)
        update = first / corr_one / (jnp.sqrt(second / corr_two) + ADAM_EPS)
        new[0, 0] = first
        new[1, 0] = second
        step[0] = jnp.where(active, update, 0.0)


def finish(
    place_s, own, back, ahead, far_low, far_high, down_own, down_back, down_ahead, down_far,
    grad_rows, pair_a, gate, up, out_gate, out_up, total, far
):
    place = pl.program_id(0)

    @pl.when(place == 0)
    def _():
        total[...] = tn_dot(grad_rows[...], pair_a[...])

    @pl.when(place < 2)
    def _():
        far[...] = far_low[0]

    @pl.when(place >= 2)
    def _():
        far[...] = far_high[0]

    total[...] += (
        nt_dot(own[0], down_own[...])
        + nt_dot(back[0], down_back[...])
        + nt_dot(ahead[0], down_ahead[...])
        + nt_dot(far[...], down_far[...])
    )

    @pl.when(place == pl.num_programs(0) - 1)
    def _():
        gate_f = gate[...].astype(jnp.float32)
        up_f = up[...].astype(jnp.float32)
        sigmoid_gate = jax.nn.sigmoid(gate_f)
        grad = total[...]
        out_gate[...] = (
            grad * up_f * sigmoid_gate * (1.0 + gate_f * (1.0 - sigmoid_gate))
        ).astype(jnp.bfloat16)
        out_up[...] = (grad * (gate_f * sigmoid_gate)).astype(jnp.bfloat16)


def shards(
    gate_logits,
    up_projected,
    output_gradient,
    down_matrix,
    adapter_input_factors,
    adapter_output_factors,
    input_moments,
    output_moments,
    batch_tenants,
    tenant_owner_slots,
):
    me = lax.axis_index("dp").astype(jnp.int32)
    core_s = (me & (CORES - 1)).reshape(1)
    y_s = lax.shift_right_logical(lax.axis_index("tensor").astype(jnp.int32), 2).reshape(1)
    rank, hid = adapter_input_factors.shape[1:]
    feat = adapter_output_factors.shape[2]
    tok = gate_logits.shape[0]
    wide = hid + feat
    bf16, f32 = jnp.bfloat16, jnp.float32
    shape = jax.ShapeDtypeStruct

    down_full = lax.all_gather(down_matrix, "dp", axis=1, tiled=True)

    packed, info_v = pl.pallas_call(
        prepare,
        out_shape=(shape((Z_LO, rank, wide + LANES), bf16), shape((8, LANES), jnp.int32)),
        in_specs=[SMEM, SMEM, WHOLE, WHOLE, WHOLE],
        out_specs=(WHOLE, WHOLE),
        compiler_params=params(56),
        name="prepare",
    )(
        batch_tenants,
        tenant_owner_slots,
        batch_tenants.reshape(-1, LANES),
        adapter_input_factors[0],
        adapter_output_factors[0],
    )
    column = lax.all_to_all(packed, "dp", 0, 0, axis_index_groups=ALONG_Z_LO)
    column, cot_copies = lax.optimization_barrier((column, spread(Z_HI, output_gradient)))
    cot_z = lax.all_to_all(cot_copies, "tensor", 0, 0, axis_index_groups=ALONG_Z_HI)
    info_s = info_v[0, :8]
    hidden = (
        jax.nn.silu(gate_logits.astype(f32)) * up_projected.astype(f32)
    ).astype(bf16)
    plane = lax.all_gather(column, "dp", axis_index_groups=ALONG_X)
    own = plane.reshape(X * Z_LO, rank, wide + LANES)
    other = lax.ppermute(own, "dp", OTHER_CORE)

    part, pair, totals = pl.pallas_call(
        low_rank,
        out_shape=(
            shape((2 * rank, tok), f32),
            shape((2 * rank, wide), bf16),
            shape((rank, LANES), f32),
        ),
        in_specs=[SMEM, SMEM, VMEM, VMEM, VMEM, VMEM],
        out_specs=(VMEM, VMEM, VMEM),
        compiler_params=params(),
        name="low_rank",
    )(info_s, core_s, own, other, hidden, output_gradient)

    sums = jnp.sum(lax.all_gather(part, "tensor", axis_index_groups=ALONG_Y), axis=0)
    sums = lax.all_gather(sums, "tensor", axis_index_groups=ALONG_Z_HI)
    cot_z, sums = lax.optimization_barrier((cot_z, sums))
    back = lax.ppermute(cot_z, "tensor", NEXT_Y)
    ahead = lax.ppermute(cot_z, "tensor", LAST_Y)
    half = Z_HI // 2
    far_low = lax.ppermute(back[:half], "tensor", NEXT_Y)
    far_high = lax.ppermute(ahead[half:], "tensor", LAST_Y)

    grad_rows, term = pl.pallas_call(
        terms,
        out_shape=(shape((2 * rank, tok), bf16), shape((2 * rank, wide + LANES), f32)),
        in_specs=[SMEM, VMEM, VMEM, VMEM],
        out_specs=(VMEM, VMEM),
        compiler_params=params(),
        name="terms",
    )(info_s, sums, hidden, output_gradient)

    term_other = lax.ppermute(term, "dp", OTHER_CORE)
    outgoing = pl.pallas_call(
        dense,
        out_shape=shape((X * Z_LO, rank, wide), bf16),
        in_specs=[SMEM, VMEM, VMEM],
        out_specs=VMEM,
        scratch_shapes=[pltpu.VMEM((X * Z_LO, rank, wide), f32)],
        compiler_params=params(),
        name="dense",
    )(core_s, term, term_other)
    outgoing = outgoing.reshape(X, Z_LO, rank, wide)
    by_x = lax.all_to_all(outgoing, "dp", 0, 0, axis_index_groups=ALONG_X)
    by_x = jnp.sum(by_x.astype(f32), axis=0).astype(bf16)
    incoming = lax.all_to_all(by_x, "dp", 0, 0, axis_index_groups=ALONG_Z_LO)

    new_moments_a, new_moments_b, step_a, step_b = pl.pallas_call(
        adam,
        out_shape=(
            shape(input_moments.shape, f32),
            shape(output_moments.shape, f32),
            shape(adapter_input_factors.shape, f32),
            shape(adapter_output_factors.shape, f32),
        ),
        in_specs=[SMEM, WHOLE, WHOLE, WHOLE, WHOLE],
        out_specs=(WHOLE,) * 4,
        compiler_params=params(56),
        name="adam",
    )(me.reshape(1), totals, incoming, input_moments, output_moments)

    def down_block(ahead_by):
        return pl.BlockSpec(
            (hid, feat),
            lambda place, y_ref: (0, lax.rem(y_ref[0] + ahead_by, Y) * Z_HI + place),
        )

    def by_place(index):
        return pl.BlockSpec((1, tok, feat), lambda place, y_ref: (index(place), 0, 0))

    def whole_of(rows, columns):
        return pl.BlockSpec((rows, columns), lambda place, y_ref: (0, 0))

    grad_gate, grad_up = pl.pallas_call(
        finish,
        out_shape=(shape((tok, hid), bf16), shape((tok, hid), bf16)),
        grid_spec=pltpu.PrefetchScalarGridSpec(
            num_scalar_prefetch=1,
            grid=(Z_HI,),
            in_specs=[
                by_place(lambda place: place),
                by_place(lambda place: place),
                by_place(lambda place: place),
                by_place(lambda place: jnp.minimum(place, half - 1)),
                by_place(lambda place: jnp.maximum(place - half, 0)),
                down_block(0),
                down_block(Y - 1),
                down_block(1),
                down_block(2),
                whole_of(2 * rank, tok),
                whole_of(2 * rank, hid),
                whole_of(tok, hid),
                whole_of(tok, hid),
            ],
            out_specs=[whole_of(tok, hid), whole_of(tok, hid)],
            scratch_shapes=[pltpu.VMEM((tok, hid), f32), pltpu.VMEM((tok, feat), bf16)],
        ),
        compiler_params=params(56),
        name="finish",
    )(
        y_s,
        cot_z,
        back,
        ahead,
        far_low,
        far_high,
        down_full,
        down_full,
        down_full,
        down_full,
        grad_rows,
        pair,
        gate_logits,
        up_projected,
    )
    return (grad_gate, grad_up, new_moments_a, new_moments_b, step_a, step_b)


def solution(mesh):
    placed = (
        P("dp", "tensor"),
        P("dp", "tensor"),
        P("dp", "tensor"),
        P("tensor", "dp"),
        P("dp", None, "tensor"),
        P("dp", None, "tensor"),
        P(None, "dp", None, "tensor"),
        P(None, "dp", None, "tensor"),
        P("dp"),
        P(),
    )
    return jax.shard_map(
        shards,
        mesh=mesh,
        in_specs=placed,
        out_specs=(
            P("dp", "tensor"),
            P("dp", "tensor"),
            P(None, "dp", None, "tensor"),
            P(None, "dp", None, "tensor"),
            P("dp", None, "tensor"),
            P("dp", None, "tensor"),
        ),
        check_vma=False,
    )
```

```python
import functools

import jax
import jax.numpy as jnp
from jax import lax
from jax.experimental import pallas as pl
from jax.experimental.pallas import tpu as pltpu
from jax.sharding import PartitionSpec as P

ADAM_STEP = 10


ADAPTER_SCALE = 2.0
BETA_ONE = 0.9
BETA_TWO = 0.95
ADAM_EPS = 1e-08
X, Z_LO, CORES = 4, 4, 2
Y, Z_HI = 4, 4
COUNT_BASE = 32
LANES = 128
INFO_FIRST, INFO_LAST, INFO_CUT = 0, 1, 2

ALONG_X = [[(x * Z_LO + z) * CORES + c for x in range(X)] for z in range(Z_LO) for c in range(CORES)]
ALONG_Z_LO = [[(x * Z_LO + z) * CORES + c for z in range(Z_LO)] for x in range(X) for c in range(CORES)]
ALONG_Y = [[y * Z_HI + h for y in range(Y)] for h in range(Z_HI)]
ALONG_Z_HI = [[y * Z_HI + h for h in range(Z_HI)] for y in range(Y)]
SAME_CORE = [
    [(x * Z_LO + z) * CORES + c for x in range(X) for z in range(Z_LO)] for c in range(CORES)
]
OTHER_CORE = [(d, d ^ 1) for d in range(X * Z_LO * CORES)]
NEXT_Y = [(y * Z_HI + h, (y + 1) % Y * Z_HI + h) for y in range(Y) for h in range(Z_HI)]
LAST_Y = [(y * Z_HI + h, (y - 1) % Y * Z_HI + h) for y in range(Y) for h in range(Z_HI)]

VMEM = pl.BlockSpec(memory_space=pltpu.VMEM)
WHOLE = pl.BlockSpec()
SMEM = pl.BlockSpec(memory_space=pltpu.SMEM)


def params(mib=40):
    return pltpu.CompilerParams(vmem_limit_bytes=mib * 1024 * 1024)


def nt_dot(left, right):
    return lax.dot_general(
        left, right, (((1,), (1,)), ((), ())), preferred_element_type=jnp.float32
    )


def tn_dot(left, right):
    return lax.dot_general(
        left, right, (((0,), (0,)), ((), ())), preferred_element_type=jnp.float32
    )


def spread(copies, block):
    return jnp.broadcast_to(block[None], (copies,) + block.shape)


def prepare(tenants_s, owners_s, tenants_v, factor_a, factor_b, packed, info_v):
    tok = tenants_s.shape[0]
    rank, hid = factor_a.shape
    feat = factor_b.shape[1]
    first, last = tenants_s[0], tenants_s[tok - 1]
    slot_first, slot_last = owners_s[first], owners_s[last]
    cut = jnp.sum((tenants_v[...] == first).astype(jnp.int32))
    lane = lax.broadcasted_iota(jnp.int32, (rank, LANES), 1)
    row = lax.broadcasted_iota(jnp.int32, (rank, LANES), 0)
    counts = jnp.where(lane == slot_first, cut, 0) + jnp.where(lane == slot_last, tok - cut, 0)
    high = lax.shift_right_logical(counts, 5)
    digits = jnp.where(row == 0, high, jnp.where(row == 1, counts - COUNT_BASE * high, 0))
    digits = digits.astype(jnp.float32).astype(jnp.bfloat16)
    a = factor_a[...].astype(jnp.bfloat16)
    b = factor_b[...].astype(jnp.bfloat16)
    for copy in range(packed.shape[0]):
        packed[copy, :, :hid] = a
        packed[copy, :, hid : hid + feat] = b
        packed[copy, :, hid + feat :] = digits
    lane_i = lax.broadcasted_iota(jnp.int32, info_v.shape, 1)
    info_v[...] = jnp.where(
        lane_i == INFO_FIRST, slot_first, jnp.where(lane_i == INFO_LAST, slot_last, cut)
    )


def low_rank(info_s, core_s, own, other, hidden, cot, part, pair, totals):
    core = core_s[0]
    rank = own.shape[1]
    hid, feat = hidden.shape[1], cot.shape[1]
    for run, place in enumerate((INFO_FIRST, INFO_LAST)):
        slot = info_s[place]
        chip = lax.shift_right_logical(slot, 1)
        here = (slot & 1) == core
        rows = pl.ds(run * rank, rank)

        @pl.when(here)
        def _():
            pair[rows, :] = own[chip, :, : hid + feat]

        @pl.when(jnp.logical_not(here))
        def _():
            pair[rows, :] = other[chip, :, : hid + feat]

    tok = hidden.shape[0]
    in_first = lax.broadcasted_iota(jnp.int32, (rank, tok), 1) < info_s[INFO_CUT]
    proj = nt_dot(pair[:, :hid], hidden[...])
    grad = nt_dot(pair[:, hid:], cot[...])
    proj = jnp.where(in_first, proj[:rank], proj[rank:])
    grad = jnp.where(in_first, grad[:rank], grad[rank:])
    part[:rank, :] = proj
    part[rank:, :] = grad
    digits = own[:, :, hid + feat :].astype(jnp.float32)
    digits = digits + other[:, :, hid + feat :].astype(jnp.float32)
    totals[...] = jnp.sum(digits, axis=0)


def terms(info_s, sums, hidden, cot, grad_rows, term):
    rank = sums.shape[1] // 2
    hid = hidden.shape[1]
    tok = hidden.shape[0]
    rows = jnp.sum(sums[...], axis=0)
    in_first = lax.broadcasted_iota(jnp.int32, (rank, tok), 1) < info_s[INFO_CUT]
    proj = rows[:rank]
    grad = ADAPTER_SCALE * rows[rank:]
    zero = jnp.zeros_like(proj)

    def by_run(values):
        both = [jnp.where(in_first, values, zero), jnp.where(in_first, zero, values)]
        return jnp.concatenate(both, axis=0).astype(jnp.bfloat16)

    proj, grad = by_run(proj), by_run(grad)
    grad_rows[...] = grad
    term[:, :hid] = jnp.dot(grad, hidden[...], preferred_element_type=jnp.float32)
    wide = hid + cot.shape[1]
    term[:, hid:wide] = ADAPTER_SCALE * jnp.dot(
        proj, cot[...], preferred_element_type=jnp.float32
    )
    term[:rank, wide:] = jnp.full((rank, LANES), info_s[INFO_FIRST], jnp.int32).astype(jnp.float32)
    term[rank:, wide:] = jnp.full((rank, LANES), info_s[INFO_LAST], jnp.int32).astype(jnp.float32)


def dense(core_s, term, term_other, outgoing, total):
    core = core_s[0]
    rank, wide = outgoing.shape[1:]
    total[...] = jnp.zeros_like(total)
    for source in (term, term_other):
        for run in range(2):
            slot = jnp.max(source[run * rank : run * rank + 8, wide:]).astype(jnp.int32)
            chip = lax.shift_right_logical(slot, 1)

            @pl.when((slot & 1) == core)
            def _():
                total[chip] += source[run * rank : (run + 1) * rank, :wide]

    outgoing[...] = total[...].astype(jnp.bfloat16)


def adam(me_s, totals, incoming, moments_a, moments_b, new_a, new_b, step_a, step_b):
    lane = lax.broadcasted_iota(jnp.int32, (1, LANES), 1)
    digit = COUNT_BASE * totals[0:1, :] + totals[1:2, :]
    count = jnp.sum(jnp.where(lane == me_s[0], digit, 0.0))
    active = count > 0.5
    divisor = jnp.maximum(count, 1.0)
    corr_one = 1.0 - BETA_ONE**ADAM_STEP
    corr_two = 1.0 - BETA_TWO**ADAM_STEP
    sums = jnp.sum(incoming[...].astype(jnp.float32), axis=0)
    hid = moments_a.shape[-1]
    for part, moments, new, step in (
        (sums[:, :hid], moments_a, new_a, step_a),
        (sums[:, hid:], moments_b, new_b, step_b),
    ):
        grad = part / divisor
        old_one, old_two = moments[0, 0], moments[1, 0]
        first = jnp.where(active, BETA_ONE * old_one + (1.0 - BETA_ONE) * grad, old_one)
        second = jnp.where(active, BETA_TWO * old_two + (1.0 - BETA_TWO) * grad * grad, old_two)
        update = first / corr_one / (jnp.sqrt(second / corr_two) + ADAM_EPS)
        new[0, 0] = first
        new[1, 0] = second
        step[0] = jnp.where(active, update, 0.0)


def near(place_s, own, back, ahead, down_own, down_back, down_ahead, grad_rows, pair_a, total):
    @pl.when(pl.program_id(0) == 0)
    def _():
        total[...] = tn_dot(grad_rows[...], pair_a[...])

    total[...] += (
        nt_dot(own[0], down_own[...])
        + nt_dot(back[0], down_back[...])
        + nt_dot(ahead[0], down_ahead[...])
    )


def finish(place_s, far_low, far_high, down_far, total, gate, up, out_gate, out_up):
    feat = far_low.shape[2]
    blocks = [far_low[0], far_low[1], far_high[0], far_high[1]]
    grad = total[...]
    for place, block in enumerate(blocks):
        grad += nt_dot(block, down_far[:, place * feat : (place + 1) * feat])
    gate_f = gate[...].astype(jnp.float32)
    up_f = up[...].astype(jnp.float32)
    sigmoid_gate = jax.nn.sigmoid(gate_f)
    out_gate[...] = (
        grad * up_f * sigmoid_gate * (1.0 + gate_f * (1.0 - sigmoid_gate))
    ).astype(jnp.bfloat16)
    out_up[...] = (grad * (gate_f * sigmoid_gate)).astype(jnp.bfloat16)


def shards(
    gate_logits,
    up_projected,
    output_gradient,
    down_matrix,
    adapter_input_factors,
    adapter_output_factors,
    input_moments,
    output_moments,
    batch_tenants,
    tenant_owner_slots,
):
    me = lax.axis_index("dp").astype(jnp.int32)
    core_s = (me & (CORES - 1)).reshape(1)
    y_s = lax.shift_right_logical(lax.axis_index("tensor").astype(jnp.int32), 2).reshape(1)
    rank, hid = adapter_input_factors.shape[1:]
    feat = adapter_output_factors.shape[2]
    tok = gate_logits.shape[0]
    wide = hid + feat
    bf16, f32 = jnp.bfloat16, jnp.float32
    shape = jax.ShapeDtypeStruct

    down_full = lax.all_gather(down_matrix, "dp", axis=1, tiled=True)

    packed, info_v = pl.pallas_call(
        prepare,
        out_shape=(shape((Z_LO, rank, wide + LANES), bf16), shape((8, LANES), jnp.int32)),
        in_specs=[SMEM, SMEM, WHOLE, WHOLE, WHOLE],
        out_specs=(WHOLE, WHOLE),
        compiler_params=params(56),
        name="prepare",
    )(
        batch_tenants,
        tenant_owner_slots,
        batch_tenants.reshape(-1, LANES),
        adapter_input_factors[0],
        adapter_output_factors[0],
    )
    column = lax.all_to_all(packed, "dp", 0, 0, axis_index_groups=ALONG_Z_LO)
    column, cot_copies = lax.optimization_barrier((column, spread(Z_HI, output_gradient)))
    cot_z = lax.all_to_all(cot_copies, "tensor", 0, 0, axis_index_groups=ALONG_Z_HI)
    info_s = info_v[0, :8]
    hidden = (
        jax.nn.silu(gate_logits.astype(f32)) * up_projected.astype(f32)
    ).astype(bf16)
    plane = lax.all_gather(column, "dp", axis_index_groups=ALONG_X)
    own = plane.reshape(X * Z_LO, rank, wide + LANES)
    other = lax.ppermute(own, "dp", OTHER_CORE)

    part, pair, totals = pl.pallas_call(
        low_rank,
        out_shape=(
            shape((2 * rank, tok), f32),
            shape((2 * rank, wide), bf16),
            shape((rank, LANES), f32),
        ),
        in_specs=[SMEM, SMEM, VMEM, VMEM, VMEM, VMEM],
        out_specs=(VMEM, VMEM, VMEM),
        compiler_params=params(),
        name="low_rank",
    )(info_s, core_s, own, other, hidden, output_gradient)

    sums = jnp.sum(lax.all_gather(part, "tensor", axis_index_groups=ALONG_Y), axis=0)
    cot_z, sums = lax.optimization_barrier((cot_z, sums))
    back = lax.ppermute(cot_z, "tensor", NEXT_Y)
    ahead = lax.ppermute(cot_z, "tensor", LAST_Y)
    sums = lax.all_gather(sums, "tensor", axis_index_groups=ALONG_Z_HI)
    back, ahead, sums = lax.optimization_barrier((back, ahead, sums))
    half = Z_HI // 2
    far_low = lax.ppermute(back[:half], "tensor", NEXT_Y)
    far_high = lax.ppermute(ahead[half:], "tensor", LAST_Y)

    grad_rows, term = pl.pallas_call(
        terms,
        out_shape=(shape((2 * rank, tok), bf16), shape((2 * rank, wide + LANES), f32)),
        in_specs=[SMEM, VMEM, VMEM, VMEM],
        out_specs=(VMEM, VMEM),
        compiler_params=params(),
        name="terms",
    )(info_s, sums, hidden, output_gradient)

    term_other = lax.ppermute(term, "dp", OTHER_CORE)
    outgoing = pl.pallas_call(
        dense,
        out_shape=shape((X * Z_LO, rank, wide), bf16),
        in_specs=[SMEM, VMEM, VMEM],
        out_specs=VMEM,
        scratch_shapes=[pltpu.VMEM((X * Z_LO, rank, wide), f32)],
        compiler_params=params(),
        name="dense",
    )(core_s, term, term_other)
    incoming = lax.all_to_all(outgoing, "dp", 0, 0, axis_index_groups=SAME_CORE)

    def down_block(ahead_by):
        return pl.BlockSpec(
            (hid, feat),
            lambda place, y_ref: (0, lax.rem(y_ref[0] + ahead_by, Y) * Z_HI + place),
        )

    def fixed(*block):
        return pl.BlockSpec(block, lambda step, y_ref: (0,) * len(block))

    by_place = pl.BlockSpec((1, tok, feat), lambda place, y_ref: (place, 0, 0))
    total = pl.pallas_call(
        near,
        out_shape=shape((tok, hid), f32),
        grid_spec=pltpu.PrefetchScalarGridSpec(
            num_scalar_prefetch=1,
            grid=(Z_HI,),
            in_specs=[
                by_place,
                by_place,
                by_place,
                down_block(0),
                down_block(Y - 1),
                down_block(1),
                fixed(2 * rank, tok),
                fixed(2 * rank, hid),
            ],
            out_specs=fixed(tok, hid),
        ),
        compiler_params=params(56),
        name="near",
    )(y_s, cot_z, back, ahead, down_full, down_full, down_full, grad_rows, pair)
    total, incoming = lax.optimization_barrier((total, incoming))
    new_moments_a, new_moments_b, step_a, step_b = pl.pallas_call(
        adam,
        out_shape=(
            shape(input_moments.shape, f32),
            shape(output_moments.shape, f32),
            shape(adapter_input_factors.shape, f32),
            shape(adapter_output_factors.shape, f32),
        ),
        in_specs=[SMEM, WHOLE, WHOLE, WHOLE, WHOLE],
        out_specs=(WHOLE,) * 4,
        compiler_params=params(56),
        name="adam",
    )(me.reshape(1), totals, incoming, input_moments, output_moments)

    rows = tok // 4
    far_rows = pl.BlockSpec((half, rows, feat), lambda step, y_ref: (0, step, 0))
    wide_rows = pl.BlockSpec((rows, hid), lambda step, y_ref: (step, 0))
    grad_gate, grad_up = pl.pallas_call(
        finish,
        out_shape=(shape((tok, hid), bf16), shape((tok, hid), bf16)),
        grid_spec=pltpu.PrefetchScalarGridSpec(
            num_scalar_prefetch=1,
            grid=(tok // rows,),
            in_specs=[
                far_rows,
                far_rows,
                pl.BlockSpec(
                    (hid, Z_HI * feat), lambda step, y_ref: (0, lax.rem(y_ref[0] + 2, Y))
                ),
                wide_rows,
                wide_rows,
                wide_rows,
            ],
            out_specs=[wide_rows, wide_rows],
        ),
        compiler_params=params(56),
        name="finish",
    )(y_s, far_low, far_high, down_full, total, gate_logits, up_projected)
    return (grad_gate, grad_up, new_moments_a, new_moments_b, step_a, step_b)


def solution(mesh):
    placed = (
        P("dp", "tensor"),
        P("dp", "tensor"),
        P("dp", "tensor"),
        P("tensor", "dp"),
        P("dp", None, "tensor"),
        P("dp", None, "tensor"),
        P(None, "dp", None, "tensor"),
        P(None, "dp", None, "tensor"),
        P("dp"),
        P(),
    )
    return jax.shard_map(
        shards,
        mesh=mesh,
        in_specs=placed,
        out_specs=(
            P("dp", "tensor"),
            P("dp", "tensor"),
            P(None, "dp", None, "tensor"),
            P(None, "dp", None, "tensor"),
            P("dp", None, "tensor"),
            P("dp", None, "tensor"),
        ),
        check_vma=False,
    )
```

```python
import functools

import jax
import jax.numpy as jnp
from jax import lax
from jax.experimental import pallas as pl
from jax.experimental.pallas import tpu as pltpu
from jax.sharding import PartitionSpec as P

ADAM_STEP = 10


ADAPTER_SCALE = 2.0
BETA_ONE = 0.9
BETA_TWO = 0.95
ADAM_EPS = 1e-08
X, Z_LO, CORES = 4, 4, 2
Y, Z_HI = 4, 4
COUNT_BASE = 32
LANES = 128
INFO_FIRST, INFO_LAST, INFO_CUT = 0, 1, 2

ALONG_X = [[(x * Z_LO + z) * CORES + c for x in range(X)] for z in range(Z_LO) for c in range(CORES)]
ALONG_Z_LO = [[(x * Z_LO + z) * CORES + c for z in range(Z_LO)] for x in range(X) for c in range(CORES)]
ALONG_Y = [[y * Z_HI + h for y in range(Y)] for h in range(Z_HI)]
ALONG_Z_HI = [[y * Z_HI + h for h in range(Z_HI)] for y in range(Y)]
OTHER_CORE = [(d, d ^ 1) for d in range(X * Z_LO * CORES)]


def shift_z_hi(by):
    return [(y * Z_HI + h, y * Z_HI + (h + by) % Z_HI) for y in range(Y) for h in range(Z_HI)]


NEXT_Y = [(y * Z_HI + h, (y + 1) % Y * Z_HI + h) for y in range(Y) for h in range(Z_HI)]
LAST_Y = [(y * Z_HI + h, (y - 1) % Y * Z_HI + h) for y in range(Y) for h in range(Z_HI)]

VMEM = pl.BlockSpec(memory_space=pltpu.VMEM)
WHOLE = pl.BlockSpec()
SMEM = pl.BlockSpec(memory_space=pltpu.SMEM)


def params(mib=40):
    return pltpu.CompilerParams(vmem_limit_bytes=mib * 1024 * 1024)


def nt_dot(left, right):
    return lax.dot_general(
        left, right, (((1,), (1,)), ((), ())), preferred_element_type=jnp.float32
    )


def tn_dot(left, right):
    return lax.dot_general(
        left, right, (((0,), (0,)), ((), ())), preferred_element_type=jnp.float32
    )


def spread(copies, block):
    return jnp.broadcast_to(block[None], (copies,) + block.shape)


def prepare(tenants_s, owners_s, tenants_v, factor_a, factor_b, cot, packed, info_v, cot_copies):
    for copy in range(cot_copies.shape[0]):
        cot_copies[copy] = cot[...]
    tok = tenants_s.shape[0]
    rank, hid = factor_a.shape
    feat = factor_b.shape[1]
    first, last = tenants_s[0], tenants_s[tok - 1]
    slot_first, slot_last = owners_s[first], owners_s[last]
    cut = jnp.sum((tenants_v[...] == first).astype(jnp.int32))
    lane = lax.broadcasted_iota(jnp.int32, (rank, LANES), 1)
    row = lax.broadcasted_iota(jnp.int32, (rank, LANES), 0)
    counts = jnp.where(lane == slot_first, cut, 0) + jnp.where(lane == slot_last, tok - cut, 0)
    high = lax.shift_right_logical(counts, 5)
    digits = jnp.where(row == 0, high, jnp.where(row == 1, counts - COUNT_BASE * high, 0))
    digits = digits.astype(jnp.float32).astype(jnp.bfloat16)
    a = factor_a[...].astype(jnp.bfloat16)
    b = factor_b[...].astype(jnp.bfloat16)
    for copy in range(packed.shape[0]):
        packed[copy, :, :hid] = a
        packed[copy, :, hid : hid + feat] = b
        packed[copy, :, hid + feat :] = digits
    lane_i = lax.broadcasted_iota(jnp.int32, info_v.shape, 1)
    info_v[...] = jnp.where(
        lane_i == INFO_FIRST, slot_first, jnp.where(lane_i == INFO_LAST, slot_last, cut)
    )


def low_rank(info_s, core_s, own, other, hidden, cot, part, pair, totals):
    core = core_s[0]
    rank = own.shape[1]
    hid, feat = hidden.shape[1], cot.shape[1]
    for run, place in enumerate((INFO_FIRST, INFO_LAST)):
        slot = info_s[place]
        chip = lax.shift_right_logical(slot, 1)
        here = (slot & 1) == core
        rows = pl.ds(run * rank, rank)

        @pl.when(here)
        def _():
            pair[rows, :] = own[chip, :, : hid + feat]

        @pl.when(jnp.logical_not(here))
        def _():
            pair[rows, :] = other[chip, :, : hid + feat]

    tok = hidden.shape[0]
    in_first = lax.broadcasted_iota(jnp.int32, (rank, tok), 1) < info_s[INFO_CUT]
    proj = nt_dot(pair[:, :hid], hidden[...])
    grad = nt_dot(pair[:, hid:], cot[...])
    proj = jnp.where(in_first, proj[:rank], proj[rank:])
    grad = jnp.where(in_first, grad[:rank], grad[rank:])
    part[:rank, :] = proj
    part[rank:, :] = grad
    digits = own[:, :, hid + feat :].astype(jnp.float32)
    digits = digits + other[:, :, hid + feat :].astype(jnp.float32)
    totals[...] = jnp.sum(digits, axis=0)


def terms(info_s, sums, one, two, three, hidden, cot, grad_rows, term):
    rank = sums.shape[0] // 2
    hid = hidden.shape[1]
    tok = hidden.shape[0]
    rows = sums[...] + one[...] + two[...] + three[...]
    in_first = lax.broadcasted_iota(jnp.int32, (rank, tok), 1) < info_s[INFO_CUT]
    proj = rows[:rank]
    grad = ADAPTER_SCALE * rows[rank:]
    zero = jnp.zeros_like(proj)

    def by_run(values):
        both = [jnp.where(in_first, values, zero), jnp.where(in_first, zero, values)]
        return jnp.concatenate(both, axis=0).astype(jnp.bfloat16)

    proj, grad = by_run(proj), by_run(grad)
    grad_rows[...] = grad
    term[:, :hid] = jnp.dot(grad, hidden[...], preferred_element_type=jnp.float32)
    wide = hid + cot.shape[1]
    term[:, hid:wide] = ADAPTER_SCALE * jnp.dot(
        proj, cot[...], preferred_element_type=jnp.float32
    )
    term[:rank, wide:] = jnp.full((rank, LANES), info_s[INFO_FIRST], jnp.int32).astype(jnp.float32)
    term[rank:, wide:] = jnp.full((rank, LANES), info_s[INFO_LAST], jnp.int32).astype(jnp.float32)


def dense(core_s, term, term_other, outgoing, total):
    core = core_s[0]
    rank, wide = outgoing.shape[1:]
    total[...] = jnp.zeros_like(total)
    for source in (term, term_other):
        for run in range(2):
            slot = jnp.max(source[run * rank : run * rank + 8, wide:]).astype(jnp.int32)
            chip = lax.shift_right_logical(slot, 1)

            @pl.when((slot & 1) == core)
            def _():
                total[chip] += source[run * rank : (run + 1) * rank, :wide]

    outgoing[...] = total[...].astype(jnp.bfloat16)


def adam(me_s, totals, incoming, moments_a, moments_b, new_a, new_b, step_a, step_b):
    lane = lax.broadcasted_iota(jnp.int32, (1, LANES), 1)
    digit = COUNT_BASE * totals[0:1, :] + totals[1:2, :]
    count = jnp.sum(jnp.where(lane == me_s[0], digit, 0.0))
    active = count > 0.5
    divisor = jnp.maximum(count, 1.0)
    corr_one = 1.0 - BETA_ONE**ADAM_STEP
    corr_two = 1.0 - BETA_TWO**ADAM_STEP
    sums = jnp.sum(incoming[...].astype(jnp.float32), axis=0)
    hid = moments_a.shape[-1]
    for part, moments, new, step in (
        (sums[:, :hid], moments_a, new_a, step_a),
        (sums[:, hid:], moments_b, new_b, step_b),
    ):
        grad = part / divisor
        old_one, old_two = moments[0, 0], moments[1, 0]
        first = jnp.where(active, BETA_ONE * old_one + (1.0 - BETA_ONE) * grad, old_one)
        second = jnp.where(active, BETA_TWO * old_two + (1.0 - BETA_TWO) * grad * grad, old_two)
        update = first / corr_one / (jnp.sqrt(second / corr_two) + ADAM_EPS)
        new[0, 0] = first
        new[1, 0] = second
        step[0] = jnp.where(active, update, 0.0)


def finish(
    place_s, own, back, ahead, far_low, far_high, down_own, down_back, down_ahead, down_far,
    grad_rows, pair_a, gate, up, out_gate, out_up, total, far
):
    place = pl.program_id(0)

    @pl.when(place == 0)
    def _():
        total[...] = tn_dot(grad_rows[...], pair_a[...])

    @pl.when(place < 2)
    def _():
        far[...] = far_low[0]

    @pl.when(place >= 2)
    def _():
        far[...] = far_high[0]

    total[...] += (
        nt_dot(own[0], down_own[...])
        + nt_dot(back[0], down_back[...])
        + nt_dot(ahead[0], down_ahead[...])
        + nt_dot(far[...], down_far[...])
    )

    @pl.when(place == pl.num_programs(0) - 1)
    def _():
        gate_f = gate[...].astype(jnp.float32)
        up_f = up[...].astype(jnp.float32)
        sigmoid_gate = jax.nn.sigmoid(gate_f)
        grad = total[...]
        out_gate[...] = (
            grad * up_f * sigmoid_gate * (1.0 + gate_f * (1.0 - sigmoid_gate))
        ).astype(jnp.bfloat16)
        out_up[...] = (grad * (gate_f * sigmoid_gate)).astype(jnp.bfloat16)


def shards(
    gate_logits,
    up_projected,
    output_gradient,
    down_matrix,
    adapter_input_factors,
    adapter_output_factors,
    input_moments,
    output_moments,
    batch_tenants,
    tenant_owner_slots,
):
    me = lax.axis_index("dp").astype(jnp.int32)
    core_s = (me & (CORES - 1)).reshape(1)
    y_s = lax.shift_right_logical(lax.axis_index("tensor").astype(jnp.int32), 2).reshape(1)
    rank, hid = adapter_input_factors.shape[1:]
    feat = adapter_output_factors.shape[2]
    tok = gate_logits.shape[0]
    wide = hid + feat
    bf16, f32 = jnp.bfloat16, jnp.float32
    shape = jax.ShapeDtypeStruct

    down_full = lax.all_gather(down_matrix, "dp", axis=1, tiled=True)

    packed, info_v, cot_copies = pl.pallas_call(
        prepare,
        out_shape=(
            shape((Z_LO, rank, wide + LANES), bf16),
            shape((8, LANES), jnp.int32),
            shape((Z_HI, tok, feat), bf16),
        ),
        in_specs=[SMEM, SMEM, WHOLE, WHOLE, WHOLE, WHOLE],
        out_specs=(WHOLE, WHOLE, WHOLE),
        compiler_params=params(56),
        name="prepare",
    )(
        batch_tenants,
        tenant_owner_slots,
        batch_tenants.reshape(-1, LANES),
        adapter_input_factors[0],
        adapter_output_factors[0],
        output_gradient,
    )
    column = lax.all_to_all(packed, "dp", 0, 0, axis_index_groups=ALONG_Z_LO)
    column, cot_copies = lax.optimization_barrier((column, cot_copies))
    cot_z = lax.all_to_all(cot_copies, "tensor", 0, 0, axis_index_groups=ALONG_Z_HI)
    info_s = info_v[0, :8]
    hidden = (
        jax.nn.silu(gate_logits.astype(f32)) * up_projected.astype(f32)
    ).astype(bf16)
    plane = lax.all_gather(column, "dp", axis_index_groups=ALONG_X)
    own = plane.reshape(X * Z_LO, rank, wide + LANES)
    other = lax.ppermute(own, "dp", OTHER_CORE)

    part, pair, totals = pl.pallas_call(
        low_rank,
        out_shape=(
            shape((2 * rank, tok), f32),
            shape((2 * rank, wide), bf16),
            shape((rank, LANES), f32),
        ),
        in_specs=[SMEM, SMEM, VMEM, VMEM, VMEM, VMEM],
        out_specs=(VMEM, VMEM, VMEM),
        compiler_params=params(),
        name="low_rank",
    )(info_s, core_s, own, other, hidden, output_gradient)

    sums = jnp.sum(lax.all_gather(part, "tensor", axis_index_groups=ALONG_Y), axis=0)
    others = [lax.ppermute(sums, "tensor", shift_z_hi(by)) for by in (1, 3, 2)]
    cot_z, sums, others = lax.optimization_barrier((cot_z, sums, others))
    back = lax.ppermute(cot_z, "tensor", NEXT_Y)
    ahead = lax.ppermute(cot_z, "tensor", LAST_Y)
    half = Z_HI // 2
    far_low = lax.ppermute(back[:half], "tensor", NEXT_Y)
    far_high = lax.ppermute(ahead[half:], "tensor", LAST_Y)

    grad_rows, term = pl.pallas_call(
        terms,
        out_shape=(shape((2 * rank, tok), bf16), shape((2 * rank, wide + LANES), f32)),
        in_specs=[SMEM] + [VMEM] * 6,
        out_specs=(VMEM, VMEM),
        compiler_params=params(),
        name="terms",
    )(info_s, sums, *others, hidden, output_gradient)

    term_other = lax.ppermute(term, "dp", OTHER_CORE)
    outgoing = pl.pallas_call(
        dense,
        out_shape=shape((X * Z_LO, rank, wide), bf16),
        in_specs=[SMEM, VMEM, VMEM],
        out_specs=VMEM,
        scratch_shapes=[pltpu.VMEM((X * Z_LO, rank, wide), f32)],
        compiler_params=params(),
        name="dense",
    )(core_s, term, term_other)
    outgoing = outgoing.reshape(X, Z_LO, rank, wide)
    by_x = lax.all_to_all(outgoing, "dp", 0, 0, axis_index_groups=ALONG_X)
    by_x = jnp.sum(by_x.astype(f32), axis=0).astype(bf16)
    incoming = lax.all_to_all(by_x, "dp", 0, 0, axis_index_groups=ALONG_Z_LO)

    new_moments_a, new_moments_b, step_a, step_b = pl.pallas_call(
        adam,
        out_shape=(
            shape(input_moments.shape, f32),
            shape(output_moments.shape, f32),
            shape(adapter_input_factors.shape, f32),
            shape(adapter_output_factors.shape, f32),
        ),
        in_specs=[SMEM, WHOLE, WHOLE, WHOLE, WHOLE],
        out_specs=(WHOLE,) * 4,
        compiler_params=params(56),
        name="adam",
    )(me.reshape(1), totals, incoming, input_moments, output_moments)

    def down_block(ahead_by):
        return pl.BlockSpec(
            (hid, feat),
            lambda place, y_ref: (0, lax.rem(y_ref[0] + ahead_by, Y) * Z_HI + place),
        )

    def by_place(index):
        return pl.BlockSpec((1, tok, feat), lambda place, y_ref: (index(place), 0, 0))

    def whole_of(rows, columns):
        return pl.BlockSpec((rows, columns), lambda place, y_ref: (0, 0))

    grad_gate, grad_up = pl.pallas_call(
        finish,
        out_shape=(shape((tok, hid), bf16), shape((tok, hid), bf16)),
        grid_spec=pltpu.PrefetchScalarGridSpec(
            num_scalar_prefetch=1,
            grid=(Z_HI,),
            in_specs=[
                by_place(lambda place: place),
                by_place(lambda place: place),
                by_place(lambda place: place),
                by_place(lambda place: jnp.minimum(place, half - 1)),
                by_place(lambda place: jnp.maximum(place - half, 0)),
                down_block(0),
                down_block(Y - 1),
                down_block(1),
                down_block(2),
                whole_of(2 * rank, tok),
                whole_of(2 * rank, hid),
                whole_of(tok, hid),
                whole_of(tok, hid),
            ],
            out_specs=[whole_of(tok, hid), whole_of(tok, hid)],
            scratch_shapes=[pltpu.VMEM((tok, hid), f32), pltpu.VMEM((tok, feat), bf16)],
        ),
        compiler_params=params(56),
        name="finish",
    )(
        y_s,
        cot_z,
        back,
        ahead,
        far_low,
        far_high,
        down_full,
        down_full,
        down_full,
        down_full,
        grad_rows,
        pair,
        gate_logits,
        up_projected,
    )
    return (grad_gate, grad_up, new_moments_a, new_moments_b, step_a, step_b)


def solution(mesh):
    placed = (
        P("dp", "tensor"),
        P("dp", "tensor"),
        P("dp", "tensor"),
        P("tensor", "dp"),
        P("dp", None, "tensor"),
        P("dp", None, "tensor"),
        P(None, "dp", None, "tensor"),
        P(None, "dp", None, "tensor"),
        P("dp"),
        P(),
    )
    return jax.shard_map(
        shards,
        mesh=mesh,
        in_specs=placed,
        out_specs=(
            P("dp", "tensor"),
            P("dp", "tensor"),
            P(None, "dp", None, "tensor"),
            P(None, "dp", None, "tensor"),
            P("dp", None, "tensor"),
            P("dp", None, "tensor"),
        ),
        check_vma=False,
    )
```

```python
import functools

import jax
import jax.numpy as jnp
from jax import lax
from jax.experimental import pallas as pl
from jax.experimental.pallas import tpu as pltpu
from jax.sharding import PartitionSpec as P

ADAM_STEP = 10


ADAPTER_SCALE = 2.0
BETA_ONE = 0.9
BETA_TWO = 0.95
ADAM_EPS = 1e-08
X, Z_LO, CORES = 4, 4, 2
Y, Z_HI = 4, 4
COUNT_BASE = 32
LANES = 128
INFO_FIRST, INFO_LAST, INFO_CUT = 0, 1, 2

ALONG_X = [[(x * Z_LO + z) * CORES + c for x in range(X)] for z in range(Z_LO) for c in range(CORES)]
ALONG_Z_LO = [[(x * Z_LO + z) * CORES + c for z in range(Z_LO)] for x in range(X) for c in range(CORES)]
ALONG_Y = [[y * Z_HI + h for y in range(Y)] for h in range(Z_HI)]
ALONG_Z_HI = [[y * Z_HI + h for h in range(Z_HI)] for y in range(Y)]
SAME_CORE = [
    [(x * Z_LO + z) * CORES + c for x in range(X) for z in range(Z_LO)] for c in range(CORES)
]
OTHER_CORE = [(d, d ^ 1) for d in range(X * Z_LO * CORES)]
NEXT_Y = [(y * Z_HI + h, (y + 1) % Y * Z_HI + h) for y in range(Y) for h in range(Z_HI)]
LAST_Y = [(y * Z_HI + h, (y - 1) % Y * Z_HI + h) for y in range(Y) for h in range(Z_HI)]

VMEM = pl.BlockSpec(memory_space=pltpu.VMEM)
WHOLE = pl.BlockSpec()
SMEM = pl.BlockSpec(memory_space=pltpu.SMEM)


def params(mib=40):
    return pltpu.CompilerParams(vmem_limit_bytes=mib * 1024 * 1024)


def nt_dot(left, right):
    return lax.dot_general(
        left, right, (((1,), (1,)), ((), ())), preferred_element_type=jnp.float32
    )


def tn_dot(left, right):
    return lax.dot_general(
        left, right, (((0,), (0,)), ((), ())), preferred_element_type=jnp.float32
    )


def prepare(tenants_s, owners_s, tenants_v, factor_a, factor_b, cot, packed, info_v, cot_copies):
    for copy in range(cot_copies.shape[0]):
        cot_copies[copy] = cot[...]
    tok = tenants_s.shape[0]
    rank, hid = factor_a.shape
    feat = factor_b.shape[1]
    first, last = tenants_s[0], tenants_s[tok - 1]
    slot_first, slot_last = owners_s[first], owners_s[last]
    cut = jnp.sum((tenants_v[...] == first).astype(jnp.int32))
    lane = lax.broadcasted_iota(jnp.int32, (rank, LANES), 1)
    row = lax.broadcasted_iota(jnp.int32, (rank, LANES), 0)
    counts = jnp.where(lane == slot_first, cut, 0) + jnp.where(lane == slot_last, tok - cut, 0)
    high = lax.shift_right_logical(counts, 5)
    digits = jnp.where(row == 0, high, jnp.where(row == 1, counts - COUNT_BASE * high, 0))
    digits = digits.astype(jnp.float32).astype(jnp.bfloat16)
    a = factor_a[...].astype(jnp.bfloat16)
    b = factor_b[...].astype(jnp.bfloat16)
    for copy in range(packed.shape[0]):
        packed[copy, :, :hid] = a
        packed[copy, :, hid : hid + feat] = b
        packed[copy, :, hid + feat :] = digits
    lane_i = lax.broadcasted_iota(jnp.int32, info_v.shape, 1)
    info_v[...] = jnp.where(
        lane_i == INFO_FIRST, slot_first, jnp.where(lane_i == INFO_LAST, slot_last, cut)
    )


def low_rank(info_s, core_s, own, other, hidden, cot, part, pair, totals):
    core = core_s[0]
    rank = own.shape[1]
    hid, feat = hidden.shape[1], cot.shape[1]
    for run, place in enumerate((INFO_FIRST, INFO_LAST)):
        slot = info_s[place]
        chip = lax.shift_right_logical(slot, 1)
        here = (slot & 1) == core
        rows = pl.ds(run * rank, rank)

        @pl.when(here)
        def _():
            pair[rows, :] = own[chip, :, : hid + feat]

        @pl.when(jnp.logical_not(here))
        def _():
            pair[rows, :] = other[chip, :, : hid + feat]

    tok = hidden.shape[0]
    in_first = lax.broadcasted_iota(jnp.int32, (rank, tok), 1) < info_s[INFO_CUT]
    proj = nt_dot(pair[:, :hid], hidden[...])
    grad = nt_dot(pair[:, hid:], cot[...])
    proj = jnp.where(in_first, proj[:rank], proj[rank:])
    grad = jnp.where(in_first, grad[:rank], grad[rank:])
    part[:rank, :] = proj
    part[rank:, :] = grad
    digits = own[:, :, hid + feat :].astype(jnp.float32)
    digits = digits + other[:, :, hid + feat :].astype(jnp.float32)
    totals[...] = jnp.sum(digits, axis=0)


def terms(info_s, sums, hidden, cot, grad_rows, term):
    rank = sums.shape[1] // 2
    hid = hidden.shape[1]
    tok = hidden.shape[0]
    rows = jnp.sum(sums[...], axis=0)
    in_first = lax.broadcasted_iota(jnp.int32, (rank, tok), 1) < info_s[INFO_CUT]
    proj = rows[:rank]
    grad = ADAPTER_SCALE * rows[rank:]
    zero = jnp.zeros_like(proj)

    def by_run(values):
        both = [jnp.where(in_first, values, zero), jnp.where(in_first, zero, values)]
        return jnp.concatenate(both, axis=0).astype(jnp.bfloat16)

    proj, grad = by_run(proj), by_run(grad)
    grad_rows[...] = grad
    term[:, :hid] = jnp.dot(grad, hidden[...], preferred_element_type=jnp.float32)
    wide = hid + cot.shape[1]
    term[:, hid:wide] = ADAPTER_SCALE * jnp.dot(
        proj, cot[...], preferred_element_type=jnp.float32
    )
    term[:rank, wide:] = jnp.full((rank, LANES), info_s[INFO_FIRST], jnp.int32).astype(jnp.float32)
    term[rank:, wide:] = jnp.full((rank, LANES), info_s[INFO_LAST], jnp.int32).astype(jnp.float32)


def dense(core_s, term, term_other, outgoing, total):
    core = core_s[0]
    rank, wide = outgoing.shape[1:]
    total[...] = jnp.zeros_like(total)
    for source in (term, term_other):
        for run in range(2):
            slot = jnp.max(source[run * rank : run * rank + 8, wide:]).astype(jnp.int32)
            chip = lax.shift_right_logical(slot, 1)

            @pl.when((slot & 1) == core)
            def _():
                total[chip] += source[run * rank : (run + 1) * rank, :wide]

    outgoing[...] = total[...].astype(jnp.bfloat16)


def adam(me_s, totals, incoming, moments_a, moments_b, new_a, new_b, step_a, step_b):
    lane = lax.broadcasted_iota(jnp.int32, (1, LANES), 1)
    digit = COUNT_BASE * totals[0:1, :] + totals[1:2, :]
    count = jnp.sum(jnp.where(lane == me_s[0], digit, 0.0))
    active = count > 0.5
    divisor = jnp.maximum(count, 1.0)
    corr_one = 1.0 - BETA_ONE**ADAM_STEP
    corr_two = 1.0 - BETA_TWO**ADAM_STEP
    sums = jnp.sum(incoming[...].astype(jnp.float32), axis=0)
    hid = moments_a.shape[-1]
    for part, moments, new, step in (
        (sums[:, :hid], moments_a, new_a, step_a),
        (sums[:, hid:], moments_b, new_b, step_b),
    ):
        grad = part / divisor
        old_one, old_two = moments[0, 0], moments[1, 0]
        first = jnp.where(active, BETA_ONE * old_one + (1.0 - BETA_ONE) * grad, old_one)
        second = jnp.where(active, BETA_TWO * old_two + (1.0 - BETA_TWO) * grad * grad, old_two)
        update = first / corr_one / (jnp.sqrt(second / corr_two) + ADAM_EPS)
        new[0, 0] = first
        new[1, 0] = second
        step[0] = jnp.where(active, update, 0.0)


def near(place_s, own, back, ahead, down_own, down_back, down_ahead, grad_rows, pair_a, total):
    @pl.when(pl.program_id(0) == 0)
    def _():
        total[...] = tn_dot(grad_rows[...], pair_a[...])

    total[...] += (
        nt_dot(own[0], down_own[...])
        + nt_dot(back[0], down_back[...])
        + nt_dot(ahead[0], down_ahead[...])
    )


def finish(place_s, far_low, far_high, down_far, total, gate, up, out_gate, out_up):
    feat = far_low.shape[2]
    blocks = [far_low[0], far_low[1], far_high[0], far_high[1]]
    grad = total[...]
    for place, block in enumerate(blocks):
        grad += nt_dot(block, down_far[:, place * feat : (place + 1) * feat])
    gate_f = gate[...].astype(jnp.float32)
    up_f = up[...].astype(jnp.float32)
    sigmoid_gate = jax.nn.sigmoid(gate_f)
    out_gate[...] = (
        grad * up_f * sigmoid_gate * (1.0 + gate_f * (1.0 - sigmoid_gate))
    ).astype(jnp.bfloat16)
    out_up[...] = (grad * (gate_f * sigmoid_gate)).astype(jnp.bfloat16)


def shards(
    gate_logits,
    up_projected,
    output_gradient,
    down_matrix,
    adapter_input_factors,
    adapter_output_factors,
    input_moments,
    output_moments,
    batch_tenants,
    tenant_owner_slots,
):
    me = lax.axis_index("dp").astype(jnp.int32)
    core_s = (me & (CORES - 1)).reshape(1)
    y_s = lax.shift_right_logical(lax.axis_index("tensor").astype(jnp.int32), 2).reshape(1)
    rank, hid = adapter_input_factors.shape[1:]
    feat = adapter_output_factors.shape[2]
    tok = gate_logits.shape[0]
    wide = hid + feat
    bf16, f32 = jnp.bfloat16, jnp.float32
    shape = jax.ShapeDtypeStruct

    down_full = lax.all_gather(down_matrix, "dp", axis=1, tiled=True)

    packed, info_v, cot_copies = pl.pallas_call(
        prepare,
        out_shape=(
            shape((Z_LO, rank, wide + LANES), bf16),
            shape((8, LANES), jnp.int32),
            shape((Z_HI, tok, feat), bf16),
        ),
        in_specs=[SMEM, SMEM, WHOLE, WHOLE, WHOLE, WHOLE],
        out_specs=(WHOLE, WHOLE, WHOLE),
        compiler_params=params(56),
        name="prepare",
    )(
        batch_tenants,
        tenant_owner_slots,
        batch_tenants.reshape(-1, LANES),
        adapter_input_factors[0],
        adapter_output_factors[0],
        output_gradient,
    )
    column = lax.all_to_all(packed, "dp", 0, 0, axis_index_groups=ALONG_Z_LO)
    column, cot_copies = lax.optimization_barrier((column, cot_copies))
    cot_z = lax.all_to_all(cot_copies, "tensor", 0, 0, axis_index_groups=ALONG_Z_HI)
    info_s = info_v[0, :8]
    hidden = (
        jax.nn.silu(gate_logits.astype(f32)) * up_projected.astype(f32)
    ).astype(bf16)
    plane = lax.all_gather(column, "dp", axis_index_groups=ALONG_X)
    own = plane.reshape(X * Z_LO, rank, wide + LANES)
    other = lax.ppermute(own, "dp", OTHER_CORE)

    part, pair, totals = pl.pallas_call(
        low_rank,
        out_shape=(
            shape((2 * rank, tok), f32),
            shape((2 * rank, wide), bf16),
            shape((rank, LANES), f32),
        ),
        in_specs=[SMEM, SMEM, VMEM, VMEM, VMEM, VMEM],
        out_specs=(VMEM, VMEM, VMEM),
        compiler_params=params(),
        name="low_rank",
    )(info_s, core_s, own, other, hidden, output_gradient)

    sums = jnp.sum(lax.all_gather(part, "tensor", axis_index_groups=ALONG_Y), axis=0)
    cot_z, sums = lax.optimization_barrier((cot_z, sums))
    back = lax.ppermute(cot_z, "tensor", NEXT_Y)
    ahead = lax.ppermute(cot_z, "tensor", LAST_Y)
    sums = lax.all_gather(sums, "tensor", axis_index_groups=ALONG_Z_HI)
    back, ahead, sums = lax.optimization_barrier((back, ahead, sums))
    half = Z_HI // 2
    far_low = lax.ppermute(back[:half], "tensor", NEXT_Y)
    far_high = lax.ppermute(ahead[half:], "tensor", LAST_Y)

    grad_rows, term = pl.pallas_call(
        terms,
        out_shape=(shape((2 * rank, tok), bf16), shape((2 * rank, wide + LANES), f32)),
        in_specs=[SMEM, VMEM, VMEM, VMEM],
        out_specs=(VMEM, VMEM),
        compiler_params=params(),
        name="terms",
    )(info_s, sums, hidden, output_gradient)

    term_other = lax.ppermute(term, "dp", OTHER_CORE)
    outgoing = pl.pallas_call(
        dense,
        out_shape=shape((X * Z_LO, rank, wide), bf16),
        in_specs=[SMEM, VMEM, VMEM],
        out_specs=VMEM,
        scratch_shapes=[pltpu.VMEM((X * Z_LO, rank, wide), f32)],
        compiler_params=params(),
        name="dense",
    )(core_s, term, term_other)
    incoming = lax.all_to_all(outgoing, "dp", 0, 0, axis_index_groups=SAME_CORE)

    def down_block(ahead_by):
        return pl.BlockSpec(
            (hid, feat),
            lambda place, y_ref: (0, lax.rem(y_ref[0] + ahead_by, Y) * Z_HI + place),
        )

    def fixed(*block):
        return pl.BlockSpec(block, lambda step, y_ref: (0,) * len(block))

    by_place = pl.BlockSpec((1, tok, feat), lambda place, y_ref: (place, 0, 0))
    total = pl.pallas_call(
        near,
        out_shape=shape((tok, hid), f32),
        grid_spec=pltpu.PrefetchScalarGridSpec(
            num_scalar_prefetch=1,
            grid=(Z_HI,),
            in_specs=[
                by_place,
                by_place,
                by_place,
                down_block(0),
                down_block(Y - 1),
                down_block(1),
                fixed(2 * rank, tok),
                fixed(2 * rank, hid),
            ],
            out_specs=fixed(tok, hid),
        ),
        compiler_params=params(56),
        name="near",
    )(y_s, cot_z, back, ahead, down_full, down_full, down_full, grad_rows, pair)
    total, incoming = lax.optimization_barrier((total, incoming))
    new_moments_a, new_moments_b, step_a, step_b = pl.pallas_call(
        adam,
        out_shape=(
            shape(input_moments.shape, f32),
            shape(output_moments.shape, f32),
            shape(adapter_input_factors.shape, f32),
            shape(adapter_output_factors.shape, f32),
        ),
        in_specs=[SMEM, WHOLE, WHOLE, WHOLE, WHOLE],
        out_specs=(WHOLE,) * 4,
        compiler_params=params(24),
        name="adam",
    )(me.reshape(1), totals, incoming, input_moments, output_moments)

    rows = tok // 4
    far_rows = pl.BlockSpec((half, rows, feat), lambda step, y_ref: (0, step, 0))
    wide_rows = pl.BlockSpec((rows, hid), lambda step, y_ref: (step, 0))
    grad_gate, grad_up = pl.pallas_call(
        finish,
        out_shape=(shape((tok, hid), bf16), shape((tok, hid), bf16)),
        grid_spec=pltpu.PrefetchScalarGridSpec(
            num_scalar_prefetch=1,
            grid=(tok // rows,),
            in_specs=[
                far_rows,
                far_rows,
                pl.BlockSpec(
                    (hid, Z_HI * feat), lambda step, y_ref: (0, lax.rem(y_ref[0] + 2, Y))
                ),
                wide_rows,
                wide_rows,
                wide_rows,
            ],
            out_specs=[wide_rows, wide_rows],
        ),
        compiler_params=params(56),
        name="finish",
    )(y_s, far_low, far_high, down_full, total, gate_logits, up_projected)
    return (grad_gate, grad_up, new_moments_a, new_moments_b, step_a, step_b)


def solution(mesh):
    placed = (
        P("dp", "tensor"),
        P("dp", "tensor"),
        P("dp", "tensor"),
        P("tensor", "dp"),
        P("dp", None, "tensor"),
        P("dp", None, "tensor"),
        P(None, "dp", None, "tensor"),
        P(None, "dp", None, "tensor"),
        P("dp"),
        P(),
    )
    return jax.shard_map(
        shards,
        mesh=mesh,
        in_specs=placed,
        out_specs=(
            P("dp", "tensor"),
            P("dp", "tensor"),
            P(None, "dp", None, "tensor"),
            P(None, "dp", None, "tensor"),
            P("dp", None, "tensor"),
            P("dp", None, "tensor"),
        ),
        check_vma=False,
    )
```

```python
import functools

import jax
import jax.numpy as jnp
from jax import lax
from jax.experimental import pallas as pl
from jax.experimental.pallas import tpu as pltpu
from jax.sharding import PartitionSpec as P

ADAM_STEP = 10


ADAPTER_SCALE = 2.0
BETA_ONE = 0.9
BETA_TWO = 0.95
ADAM_EPS = 1e-08
X, Z_LO, CORES = 4, 4, 2
Y, Z_HI = 4, 4
COUNT_BASE = 32
LANES = 128
INFO_FIRST, INFO_LAST, INFO_CUT = 0, 1, 2

ALONG_X = [[(x * Z_LO + z) * CORES + c for x in range(X)] for z in range(Z_LO) for c in range(CORES)]
ALONG_Z_LO = [[(x * Z_LO + z) * CORES + c for z in range(Z_LO)] for x in range(X) for c in range(CORES)]
ALONG_Y = [[y * Z_HI + h for y in range(Y)] for h in range(Z_HI)]
ALONG_Z_HI = [[y * Z_HI + h for h in range(Z_HI)] for y in range(Y)]
SAME_CORE = [
    [(x * Z_LO + z) * CORES + c for x in range(X) for z in range(Z_LO)] for c in range(CORES)
]
OTHER_CORE = [(d, d ^ 1) for d in range(X * Z_LO * CORES)]
NEXT_Y = [(y * Z_HI + h, (y + 1) % Y * Z_HI + h) for y in range(Y) for h in range(Z_HI)]
LAST_Y = [(y * Z_HI + h, (y - 1) % Y * Z_HI + h) for y in range(Y) for h in range(Z_HI)]

VMEM = pl.BlockSpec(memory_space=pltpu.VMEM)
WHOLE = pl.BlockSpec()
SMEM = pl.BlockSpec(memory_space=pltpu.SMEM)


def params(mib=40):
    return pltpu.CompilerParams(vmem_limit_bytes=mib * 1024 * 1024)


def nt_dot(left, right):
    return lax.dot_general(
        left, right, (((1,), (1,)), ((), ())), preferred_element_type=jnp.float32
    )


def tn_dot(left, right):
    return lax.dot_general(
        left, right, (((0,), (0,)), ((), ())), preferred_element_type=jnp.float32
    )


def prepare(tenants_s, owners_s, tenants_v, factor_a, factor_b, cot, packed, info_v, cot_copies):
    for copy in range(cot_copies.shape[0]):
        cot_copies[copy] = cot[...]
    tok = tenants_s.shape[0]
    rank, hid = factor_a.shape
    feat = factor_b.shape[1]
    first, last = tenants_s[0], tenants_s[tok - 1]
    slot_first, slot_last = owners_s[first], owners_s[last]
    cut = jnp.sum((tenants_v[...] == first).astype(jnp.int32))
    lane = lax.broadcasted_iota(jnp.int32, (rank, LANES), 1)
    row = lax.broadcasted_iota(jnp.int32, (rank, LANES), 0)
    counts = jnp.where(lane == slot_first, cut, 0) + jnp.where(lane == slot_last, tok - cut, 0)
    high = lax.shift_right_logical(counts, 5)
    digits = jnp.where(row == 0, high, jnp.where(row == 1, counts - COUNT_BASE * high, 0))
    digits = digits.astype(jnp.float32).astype(jnp.bfloat16)
    a = factor_a[...].astype(jnp.bfloat16)
    b = factor_b[...].astype(jnp.bfloat16)
    for copy in range(packed.shape[0]):
        packed[copy, :, :hid] = a
        packed[copy, :, hid : hid + feat] = b
        packed[copy, :, hid + feat :] = digits
    lane_i = lax.broadcasted_iota(jnp.int32, info_v.shape, 1)
    info_v[...] = jnp.where(
        lane_i == INFO_FIRST, slot_first, jnp.where(lane_i == INFO_LAST, slot_last, cut)
    )


def low_rank(info_s, core_s, own, other, hidden, cot, part, pair, totals):
    core = core_s[0]
    rank = own.shape[1]
    hid, feat = hidden.shape[1], cot.shape[1]
    for run, place in enumerate((INFO_FIRST, INFO_LAST)):
        slot = info_s[place]
        chip = lax.shift_right_logical(slot, 1)
        here = (slot & 1) == core
        rows = pl.ds(run * rank, rank)

        @pl.when(here)
        def _():
            pair[rows, :] = own[chip, :, : hid + feat]

        @pl.when(jnp.logical_not(here))
        def _():
            pair[rows, :] = other[chip, :, : hid + feat]

    tok = hidden.shape[0]
    in_first = lax.broadcasted_iota(jnp.int32, (rank, tok), 1) < info_s[INFO_CUT]
    proj = nt_dot(pair[:, :hid], hidden[...])
    grad = nt_dot(pair[:, hid:], cot[...])
    proj = jnp.where(in_first, proj[:rank], proj[rank:])
    grad = jnp.where(in_first, grad[:rank], grad[rank:])
    part[:rank, :] = proj
    part[rank:, :] = grad
    digits = own[:, :, hid + feat :].astype(jnp.float32)
    digits = digits + other[:, :, hid + feat :].astype(jnp.float32)
    totals[...] = jnp.sum(digits, axis=0)


def terms(info_s, sums, hidden, cot, grad_rows, term):
    rank = sums.shape[1] // 2
    hid = hidden.shape[1]
    tok = hidden.shape[0]
    rows = jnp.sum(sums[...], axis=0)
    in_first = lax.broadcasted_iota(jnp.int32, (rank, tok), 1) < info_s[INFO_CUT]
    proj = rows[:rank]
    grad = ADAPTER_SCALE * rows[rank:]
    zero = jnp.zeros_like(proj)

    def by_run(values):
        both = [jnp.where(in_first, values, zero), jnp.where(in_first, zero, values)]
        return jnp.concatenate(both, axis=0).astype(jnp.bfloat16)

    proj, grad = by_run(proj), by_run(grad)
    grad_rows[...] = grad
    term[:, :hid] = jnp.dot(grad, hidden[...], preferred_element_type=jnp.float32)
    wide = hid + cot.shape[1]
    term[:, hid:wide] = ADAPTER_SCALE * jnp.dot(
        proj, cot[...], preferred_element_type=jnp.float32
    )
    term[:rank, wide:] = jnp.full((rank, LANES), info_s[INFO_FIRST], jnp.int32).astype(jnp.float32)
    term[rank:, wide:] = jnp.full((rank, LANES), info_s[INFO_LAST], jnp.int32).astype(jnp.float32)


def dense(core_s, term, term_other, outgoing, total):
    core = core_s[0]
    rank, wide = outgoing.shape[1:]
    total[...] = jnp.zeros_like(total)
    for source in (term, term_other):
        for run in range(2):
            slot = jnp.max(source[run * rank : run * rank + 8, wide:]).astype(jnp.int32)
            chip = lax.shift_right_logical(slot, 1)

            @pl.when((slot & 1) == core)
            def _():
                total[chip] += source[run * rank : (run + 1) * rank, :wide]

    outgoing[...] = total[...].astype(jnp.bfloat16)


def adam(me_s, totals, incoming, moments_a, moments_b, new_a, new_b, step_a, step_b):
    lane = lax.broadcasted_iota(jnp.int32, (1, LANES), 1)
    digit = COUNT_BASE * totals[0:1, :] + totals[1:2, :]
    count = jnp.sum(jnp.where(lane == me_s[0], digit, 0.0))
    active = count > 0.5
    divisor = jnp.maximum(count, 1.0)
    corr_one = 1.0 - BETA_ONE**ADAM_STEP
    corr_two = 1.0 - BETA_TWO**ADAM_STEP
    sums = jnp.sum(incoming[...].astype(jnp.float32), axis=0)
    hid = moments_a.shape[-1]
    for part, moments, new, step in (
        (sums[:, :hid], moments_a, new_a, step_a),
        (sums[:, hid:], moments_b, new_b, step_b),
    ):
        grad = part / divisor
        old_one, old_two = moments[0, 0], moments[1, 0]
        first = jnp.where(active, BETA_ONE * old_one + (1.0 - BETA_ONE) * grad, old_one)
        second = jnp.where(active, BETA_TWO * old_two + (1.0 - BETA_TWO) * grad * grad, old_two)
        update = first / corr_one / (jnp.sqrt(second / corr_two) + ADAM_EPS)
        new[0, 0] = first
        new[1, 0] = second
        step[0] = jnp.where(active, update, 0.0)


def near(place_s, own, back, ahead, down_own, down_back, down_ahead, grad_rows, pair_a, total):
    @pl.when(pl.program_id(0) == 0)
    def _():
        total[...] = tn_dot(grad_rows[...], pair_a[...])

    blocks = jnp.concatenate([own[0], back[0], ahead[0]], axis=1)
    weights = jnp.concatenate([down_own[...], down_back[...], down_ahead[...]], axis=1)
    total[...] += nt_dot(blocks, weights)


def finish(place_s, far_low, far_high, down_far, total, gate, up, out_gate, out_up):
    blocks = jnp.concatenate([far_low[0], far_low[1], far_high[0], far_high[1]], axis=1)
    grad = total[...] + nt_dot(blocks, down_far[...])
    gate_f = gate[...].astype(jnp.float32)
    up_f = up[...].astype(jnp.float32)
    sigmoid_gate = jax.nn.sigmoid(gate_f)
    out_gate[...] = (
        grad * up_f * sigmoid_gate * (1.0 + gate_f * (1.0 - sigmoid_gate))
    ).astype(jnp.bfloat16)
    out_up[...] = (grad * (gate_f * sigmoid_gate)).astype(jnp.bfloat16)


def shards(
    gate_logits,
    up_projected,
    output_gradient,
    down_matrix,
    adapter_input_factors,
    adapter_output_factors,
    input_moments,
    output_moments,
    batch_tenants,
    tenant_owner_slots,
):
    me = lax.axis_index("dp").astype(jnp.int32)
    core_s = (me & (CORES - 1)).reshape(1)
    y_s = lax.shift_right_logical(lax.axis_index("tensor").astype(jnp.int32), 2).reshape(1)
    rank, hid = adapter_input_factors.shape[1:]
    feat = adapter_output_factors.shape[2]
    tok = gate_logits.shape[0]
    wide = hid + feat
    bf16, f32 = jnp.bfloat16, jnp.float32
    shape = jax.ShapeDtypeStruct

    down_full = lax.all_gather(down_matrix, "dp", axis=1, tiled=True)

    packed, info_v, cot_copies = pl.pallas_call(
        prepare,
        out_shape=(
            shape((Z_LO, rank, wide + LANES), bf16),
            shape((8, LANES), jnp.int32),
            shape((Z_HI, tok, feat), bf16),
        ),
        in_specs=[SMEM, SMEM, WHOLE, WHOLE, WHOLE, WHOLE],
        out_specs=(WHOLE, WHOLE, WHOLE),
        compiler_params=params(56),
        name="prepare",
    )(
        batch_tenants,
        tenant_owner_slots,
        batch_tenants.reshape(-1, LANES),
        adapter_input_factors[0],
        adapter_output_factors[0],
        output_gradient,
    )
    column = lax.all_to_all(packed, "dp", 0, 0, axis_index_groups=ALONG_Z_LO)
    column, cot_copies = lax.optimization_barrier((column, cot_copies))
    cot_z = lax.all_to_all(cot_copies, "tensor", 0, 0, axis_index_groups=ALONG_Z_HI)
    info_s = info_v[0, :8]
    hidden = (
        jax.nn.silu(gate_logits.astype(f32)) * up_projected.astype(f32)
    ).astype(bf16)
    plane = lax.all_gather(column, "dp", axis_index_groups=ALONG_X)
    own = plane.reshape(X * Z_LO, rank, wide + LANES)
    other = lax.ppermute(own, "dp", OTHER_CORE)

    part, pair, totals = pl.pallas_call(
        low_rank,
        out_shape=(
            shape((2 * rank, tok), f32),
            shape((2 * rank, wide), bf16),
            shape((rank, LANES), f32),
        ),
        in_specs=[SMEM, SMEM, VMEM, VMEM, VMEM, VMEM],
        out_specs=(VMEM, VMEM, VMEM),
        compiler_params=params(),
        name="low_rank",
    )(info_s, core_s, own, other, hidden, output_gradient)

    sums = jnp.sum(lax.all_gather(part, "tensor", axis_index_groups=ALONG_Y), axis=0)
    cot_z, sums = lax.optimization_barrier((cot_z, sums))
    back = lax.ppermute(cot_z, "tensor", NEXT_Y)
    ahead = lax.ppermute(cot_z, "tensor", LAST_Y)
    sums = lax.all_gather(sums, "tensor", axis_index_groups=ALONG_Z_HI)
    back, ahead, sums = lax.optimization_barrier((back, ahead, sums))
    half = Z_HI // 2
    far_low = lax.ppermute(back[:half], "tensor", NEXT_Y)
    far_high = lax.ppermute(ahead[half:], "tensor", LAST_Y)

    grad_rows, term = pl.pallas_call(
        terms,
        out_shape=(shape((2 * rank, tok), bf16), shape((2 * rank, wide + LANES), f32)),
        in_specs=[SMEM, VMEM, VMEM, VMEM],
        out_specs=(VMEM, VMEM),
        compiler_params=params(),
        name="terms",
    )(info_s, sums, hidden, output_gradient)

    term_other = lax.ppermute(term, "dp", OTHER_CORE)
    outgoing = pl.pallas_call(
        dense,
        out_shape=shape((X * Z_LO, rank, wide), bf16),
        in_specs=[SMEM, VMEM, VMEM],
        out_specs=VMEM,
        scratch_shapes=[pltpu.VMEM((X * Z_LO, rank, wide), f32)],
        compiler_params=params(),
        name="dense",
    )(core_s, term, term_other)
    incoming = lax.all_to_all(outgoing, "dp", 0, 0, axis_index_groups=SAME_CORE)

    def down_block(ahead_by):
        return pl.BlockSpec(
            (hid, feat),
            lambda place, y_ref: (0, lax.rem(y_ref[0] + ahead_by, Y) * Z_HI + place),
        )

    def fixed(*block):
        return pl.BlockSpec(block, lambda step, y_ref: (0,) * len(block))

    by_place = pl.BlockSpec((1, tok, feat), lambda place, y_ref: (place, 0, 0))
    total = pl.pallas_call(
        near,
        out_shape=shape((tok, hid), f32),
        grid_spec=pltpu.PrefetchScalarGridSpec(
            num_scalar_prefetch=1,
            grid=(Z_HI,),
            in_specs=[
                by_place,
                by_place,
                by_place,
                down_block(0),
                down_block(Y - 1),
                down_block(1),
                fixed(2 * rank, tok),
                fixed(2 * rank, hid),
            ],
            out_specs=fixed(tok, hid),
        ),
        compiler_params=params(56),
        name="near",
    )(y_s, cot_z, back, ahead, down_full, down_full, down_full, grad_rows, pair)
    total, incoming = lax.optimization_barrier((total, incoming))
    new_moments_a, new_moments_b, step_a, step_b = pl.pallas_call(
        adam,
        out_shape=(
            shape(input_moments.shape, f32),
            shape(output_moments.shape, f32),
            shape(adapter_input_factors.shape, f32),
            shape(adapter_output_factors.shape, f32),
        ),
        in_specs=[SMEM, WHOLE, WHOLE, WHOLE, WHOLE],
        out_specs=(WHOLE,) * 4,
        compiler_params=params(24),
        name="adam",
    )(me.reshape(1), totals, incoming, input_moments, output_moments)

    rows = tok // 2
    far_rows = pl.BlockSpec((half, rows, feat), lambda step, y_ref: (0, step, 0))
    wide_rows = pl.BlockSpec((rows, hid), lambda step, y_ref: (step, 0))
    grad_gate, grad_up = pl.pallas_call(
        finish,
        out_shape=(shape((tok, hid), bf16), shape((tok, hid), bf16)),
        grid_spec=pltpu.PrefetchScalarGridSpec(
            num_scalar_prefetch=1,
            grid=(tok // rows,),
            in_specs=[
                far_rows,
                far_rows,
                pl.BlockSpec(
                    (hid, Z_HI * feat), lambda step, y_ref: (0, lax.rem(y_ref[0] + 2, Y))
                ),
                wide_rows,
                wide_rows,
                wide_rows,
            ],
            out_specs=[wide_rows, wide_rows],
        ),
        compiler_params=params(56),
        name="finish",
    )(y_s, far_low, far_high, down_full, total, gate_logits, up_projected)
    return (grad_gate, grad_up, new_moments_a, new_moments_b, step_a, step_b)


def solution(mesh):
    placed = (
        P("dp", "tensor"),
        P("dp", "tensor"),
        P("dp", "tensor"),
        P("tensor", "dp"),
        P("dp", None, "tensor"),
        P("dp", None, "tensor"),
        P(None, "dp", None, "tensor"),
        P(None, "dp", None, "tensor"),
        P("dp"),
        P(),
    )
    return jax.shard_map(
        shards,
        mesh=mesh,
        in_specs=placed,
        out_specs=(
            P("dp", "tensor"),
            P("dp", "tensor"),
            P(None, "dp", None, "tensor"),
            P(None, "dp", None, "tensor"),
            P("dp", None, "tensor"),
            P("dp", None, "tensor"),
        ),
        check_vma=False,
    )
```

```python
import functools

import jax
import jax.numpy as jnp
from jax import lax
from jax.experimental import pallas as pl
from jax.experimental.pallas import tpu as pltpu
from jax.sharding import PartitionSpec as P

ADAM_STEP = 10


ADAPTER_SCALE = 2.0
BETA_ONE = 0.9
BETA_TWO = 0.95
ADAM_EPS = 1e-08
X, Z_LO, CORES = 4, 4, 2
Y, Z_HI = 4, 4
COUNT_BASE = 32
LANES = 128
INFO_FIRST, INFO_LAST, INFO_CUT = 0, 1, 2

ALONG_X = [[(x * Z_LO + z) * CORES + c for x in range(X)] for z in range(Z_LO) for c in range(CORES)]
ALONG_Z_LO = [[(x * Z_LO + z) * CORES + c for z in range(Z_LO)] for x in range(X) for c in range(CORES)]
ALONG_Y = [[y * Z_HI + h for y in range(Y)] for h in range(Z_HI)]
ALONG_Z_HI = [[y * Z_HI + h for h in range(Z_HI)] for y in range(Y)]
SAME_CORE = [
    [(x * Z_LO + z) * CORES + c for x in range(X) for z in range(Z_LO)] for c in range(CORES)
]
OTHER_CORE = [(d, d ^ 1) for d in range(X * Z_LO * CORES)]
NEXT_Y = [(y * Z_HI + h, (y + 1) % Y * Z_HI + h) for y in range(Y) for h in range(Z_HI)]
LAST_Y = [(y * Z_HI + h, (y - 1) % Y * Z_HI + h) for y in range(Y) for h in range(Z_HI)]

VMEM = pl.BlockSpec(memory_space=pltpu.VMEM)
WHOLE = pl.BlockSpec()
SMEM = pl.BlockSpec(memory_space=pltpu.SMEM)


def params(mib=40):
    return pltpu.CompilerParams(vmem_limit_bytes=mib * 1024 * 1024)


def nt_dot(left, right):
    return lax.dot_general(
        left, right, (((1,), (1,)), ((), ())), preferred_element_type=jnp.float32
    )


def tn_dot(left, right):
    return lax.dot_general(
        left, right, (((0,), (0,)), ((), ())), preferred_element_type=jnp.float32
    )


def prepare(tenants_s, owners_s, tenants_v, factor_a, factor_b, cot, packed, info_v, cot_copies):
    for copy in range(cot_copies.shape[0]):
        cot_copies[copy] = cot[...]
    tok = tenants_s.shape[0]
    rank, hid = factor_a.shape
    feat = factor_b.shape[1]
    first, last = tenants_s[0], tenants_s[tok - 1]
    slot_first, slot_last = owners_s[first], owners_s[last]
    cut = jnp.sum((tenants_v[...] == first).astype(jnp.int32))
    lane = lax.broadcasted_iota(jnp.int32, (rank, LANES), 1)
    row = lax.broadcasted_iota(jnp.int32, (rank, LANES), 0)
    counts = jnp.where(lane == slot_first, cut, 0) + jnp.where(lane == slot_last, tok - cut, 0)
    high = lax.shift_right_logical(counts, 5)
    digits = jnp.where(row == 0, high, jnp.where(row == 1, counts - COUNT_BASE * high, 0))
    digits = digits.astype(jnp.float32).astype(jnp.bfloat16)
    a = factor_a[...].astype(jnp.bfloat16)
    b = factor_b[...].astype(jnp.bfloat16)
    for copy in range(packed.shape[0]):
        packed[copy, :, :hid] = a
        packed[copy, :, hid : hid + feat] = b
        packed[copy, :, hid + feat :] = digits
    lane_i = lax.broadcasted_iota(jnp.int32, info_v.shape, 1)
    info_v[...] = jnp.where(
        lane_i == INFO_FIRST, slot_first, jnp.where(lane_i == INFO_LAST, slot_last, cut)
    )


def low_rank(info_s, core_s, own, other, hidden, cot, part, pair, totals):
    core = core_s[0]
    rank = own.shape[1]
    hid, feat = hidden.shape[1], cot.shape[1]
    for run, place in enumerate((INFO_FIRST, INFO_LAST)):
        slot = info_s[place]
        chip = lax.shift_right_logical(slot, 1)
        here = (slot & 1) == core
        rows = pl.ds(run * rank, rank)

        @pl.when(here)
        def _():
            pair[rows, :] = own[chip, :, : hid + feat]

        @pl.when(jnp.logical_not(here))
        def _():
            pair[rows, :] = other[chip, :, : hid + feat]

    tok = hidden.shape[0]
    in_first = lax.broadcasted_iota(jnp.int32, (rank, tok), 1) < info_s[INFO_CUT]
    proj = nt_dot(pair[:, :hid], hidden[...])
    grad = nt_dot(pair[:, hid:], cot[...])
    proj = jnp.where(in_first, proj[:rank], proj[rank:])
    grad = jnp.where(in_first, grad[:rank], grad[rank:])
    part[:rank, :] = proj
    part[rank:, :] = grad
    digits = own[:, :, hid + feat :].astype(jnp.float32)
    digits = digits + other[:, :, hid + feat :].astype(jnp.float32)
    totals[...] = jnp.sum(digits, axis=0)


def terms(info_s, sums, hidden, cot, grad_rows, term):
    rank = sums.shape[1] // 2
    hid = hidden.shape[1]
    tok = hidden.shape[0]
    rows = jnp.sum(sums[...], axis=0)
    in_first = lax.broadcasted_iota(jnp.int32, (rank, tok), 1) < info_s[INFO_CUT]
    proj = rows[:rank]
    grad = ADAPTER_SCALE * rows[rank:]
    zero = jnp.zeros_like(proj)

    def by_run(values):
        both = [jnp.where(in_first, values, zero), jnp.where(in_first, zero, values)]
        return jnp.concatenate(both, axis=0).astype(jnp.bfloat16)

    proj, grad = by_run(proj), by_run(grad)
    grad_rows[...] = grad
    term[:, :hid] = jnp.dot(grad, hidden[...], preferred_element_type=jnp.float32)
    wide = hid + cot.shape[1]
    term[:, hid:wide] = ADAPTER_SCALE * jnp.dot(
        proj, cot[...], preferred_element_type=jnp.float32
    )
    term[:rank, wide:] = jnp.full((rank, LANES), info_s[INFO_FIRST], jnp.int32).astype(jnp.float32)
    term[rank:, wide:] = jnp.full((rank, LANES), info_s[INFO_LAST], jnp.int32).astype(jnp.float32)


def dense(core_s, term, term_other, outgoing, total):
    core = core_s[0]
    rank, wide = outgoing.shape[1:]
    total[...] = jnp.zeros_like(total)
    for source in (term, term_other):
        for run in range(2):
            slot = jnp.max(source[run * rank : run * rank + 8, wide:]).astype(jnp.int32)
            chip = lax.shift_right_logical(slot, 1)

            @pl.when((slot & 1) == core)
            def _():
                total[chip] += source[run * rank : (run + 1) * rank, :wide]

    outgoing[...] = total[...].astype(jnp.bfloat16)


def adam(me_s, totals, incoming, moments_a, moments_b, new_a, new_b, step_a, step_b):
    lane = lax.broadcasted_iota(jnp.int32, (1, LANES), 1)
    digit = COUNT_BASE * totals[0:1, :] + totals[1:2, :]
    count = jnp.sum(jnp.where(lane == me_s[0], digit, 0.0))
    active = count > 0.5
    divisor = jnp.maximum(count, 1.0)
    corr_one = 1.0 - BETA_ONE**ADAM_STEP
    corr_two = 1.0 - BETA_TWO**ADAM_STEP
    sums = jnp.sum(incoming[...].astype(jnp.float32), axis=0)
    hid = moments_a.shape[-1]
    for part, moments, new, step in (
        (sums[:, :hid], moments_a, new_a, step_a),
        (sums[:, hid:], moments_b, new_b, step_b),
    ):
        grad = part / divisor
        old_one, old_two = moments[0, 0], moments[1, 0]
        first = jnp.where(active, BETA_ONE * old_one + (1.0 - BETA_ONE) * grad, old_one)
        second = jnp.where(active, BETA_TWO * old_two + (1.0 - BETA_TWO) * grad * grad, old_two)
        update = first / corr_one / (jnp.sqrt(second / corr_two) + ADAM_EPS)
        new[0, 0] = first
        new[1, 0] = second
        step[0] = jnp.where(active, update, 0.0)


def near(place_s, own, back, ahead, down_own, down_back, down_ahead, grad_rows, pair_a, total):
    @pl.when(pl.program_id(0) == 0)
    def _():
        total[...] = tn_dot(grad_rows[...], pair_a[...])

    blocks = jnp.concatenate([own[0], back[0], ahead[0]], axis=1)
    weights = jnp.concatenate([down_own[...], down_back[...], down_ahead[...]], axis=1)
    total[...] += nt_dot(blocks, weights)


def finish(place_s, far_low, far_high, down_far, total, gate, up, out_gate, out_up, joined):
    rows, cut = total.shape[0], far_low.shape[1]
    places = range(far_low.shape[0])

    @pl.when(pl.program_id(0) == 0)
    def _():
        for place in places:
            joined[place] = far_low[place, :rows]

    @pl.when(pl.program_id(0) == 1)
    def _():
        for place in places:
            joined[place, : cut - rows] = far_low[place, rows:]
            joined[place, cut - rows :] = far_high[place]

    blocks = jnp.concatenate([joined[place] for place in places], axis=1)
    grad = total[...] + nt_dot(blocks, down_far[...])
    gate_f = gate[...].astype(jnp.float32)
    up_f = up[...].astype(jnp.float32)
    sigmoid_gate = jax.nn.sigmoid(gate_f)
    out_gate[...] = (
        grad * up_f * sigmoid_gate * (1.0 + gate_f * (1.0 - sigmoid_gate))
    ).astype(jnp.bfloat16)
    out_up[...] = (grad * (gate_f * sigmoid_gate)).astype(jnp.bfloat16)


def shards(
    gate_logits,
    up_projected,
    output_gradient,
    down_matrix,
    adapter_input_factors,
    adapter_output_factors,
    input_moments,
    output_moments,
    batch_tenants,
    tenant_owner_slots,
):
    me = lax.axis_index("dp").astype(jnp.int32)
    core_s = (me & (CORES - 1)).reshape(1)
    y_s = lax.shift_right_logical(lax.axis_index("tensor").astype(jnp.int32), 2).reshape(1)
    rank, hid = adapter_input_factors.shape[1:]
    feat = adapter_output_factors.shape[2]
    tok = gate_logits.shape[0]
    wide = hid + feat
    bf16, f32 = jnp.bfloat16, jnp.float32
    shape = jax.ShapeDtypeStruct

    down_full = lax.all_gather(down_matrix, "dp", axis=1, tiled=True)

    packed, info_v, cot_copies = pl.pallas_call(
        prepare,
        out_shape=(
            shape((Z_LO, rank, wide + LANES), bf16),
            shape((8, LANES), jnp.int32),
            shape((Z_HI, tok, feat), bf16),
        ),
        in_specs=[SMEM, SMEM, WHOLE, WHOLE, WHOLE, WHOLE],
        out_specs=(WHOLE, WHOLE, WHOLE),
        compiler_params=params(56),
        name="prepare",
    )(
        batch_tenants,
        tenant_owner_slots,
        batch_tenants.reshape(-1, LANES),
        adapter_input_factors[0],
        adapter_output_factors[0],
        output_gradient,
    )
    column = lax.all_to_all(packed, "dp", 0, 0, axis_index_groups=ALONG_Z_LO)
    column, cot_copies = lax.optimization_barrier((column, cot_copies))
    cot_z = lax.all_to_all(cot_copies, "tensor", 0, 0, axis_index_groups=ALONG_Z_HI)
    info_s = info_v[0, :8]
    hidden = (
        jax.nn.silu(gate_logits.astype(f32)) * up_projected.astype(f32)
    ).astype(bf16)
    plane = lax.all_gather(column, "dp", axis_index_groups=ALONG_X)
    own = plane.reshape(X * Z_LO, rank, wide + LANES)
    other = lax.ppermute(own, "dp", OTHER_CORE)

    part, pair, totals = pl.pallas_call(
        low_rank,
        out_shape=(
            shape((2 * rank, tok), f32),
            shape((2 * rank, wide), bf16),
            shape((rank, LANES), f32),
        ),
        in_specs=[SMEM, SMEM, VMEM, VMEM, VMEM, VMEM],
        out_specs=(VMEM, VMEM, VMEM),
        compiler_params=params(),
        name="low_rank",
    )(info_s, core_s, own, other, hidden, output_gradient)

    sums = jnp.sum(lax.all_gather(part, "tensor", axis_index_groups=ALONG_Y), axis=0)
    cot_z, sums = lax.optimization_barrier((cot_z, sums))
    back = lax.ppermute(cot_z, "tensor", NEXT_Y)
    ahead = lax.ppermute(cot_z, "tensor", LAST_Y)
    sums = lax.all_gather(sums, "tensor", axis_index_groups=ALONG_Z_HI)
    back, ahead, sums = lax.optimization_barrier((back, ahead, sums))
    cut = tok * 5 // 8
    far_low = lax.ppermute(back[:, :cut], "tensor", NEXT_Y)
    far_high = lax.ppermute(ahead[:, cut:], "tensor", LAST_Y)

    grad_rows, term = pl.pallas_call(
        terms,
        out_shape=(shape((2 * rank, tok), bf16), shape((2 * rank, wide + LANES), f32)),
        in_specs=[SMEM, VMEM, VMEM, VMEM],
        out_specs=(VMEM, VMEM),
        compiler_params=params(),
        name="terms",
    )(info_s, sums, hidden, output_gradient)

    term_other = lax.ppermute(term, "dp", OTHER_CORE)
    outgoing = pl.pallas_call(
        dense,
        out_shape=shape((X * Z_LO, rank, wide), bf16),
        in_specs=[SMEM, VMEM, VMEM],
        out_specs=VMEM,
        scratch_shapes=[pltpu.VMEM((X * Z_LO, rank, wide), f32)],
        compiler_params=params(),
        name="dense",
    )(core_s, term, term_other)
    incoming = lax.all_to_all(outgoing, "dp", 0, 0, axis_index_groups=SAME_CORE)

    def down_block(ahead_by):
        return pl.BlockSpec(
            (hid, feat),
            lambda place, y_ref: (0, lax.rem(y_ref[0] + ahead_by, Y) * Z_HI + place),
        )

    def fixed(*block):
        return pl.BlockSpec(block, lambda step, y_ref: (0,) * len(block))

    by_place = pl.BlockSpec((1, tok, feat), lambda place, y_ref: (place, 0, 0))
    total = pl.pallas_call(
        near,
        out_shape=shape((tok, hid), f32),
        grid_spec=pltpu.PrefetchScalarGridSpec(
            num_scalar_prefetch=1,
            grid=(Z_HI,),
            in_specs=[
                by_place,
                by_place,
                by_place,
                down_block(0),
                down_block(Y - 1),
                down_block(1),
                fixed(2 * rank, tok),
                fixed(2 * rank, hid),
            ],
            out_specs=fixed(tok, hid),
        ),
        compiler_params=params(56),
        name="near",
    )(y_s, cot_z, back, ahead, down_full, down_full, down_full, grad_rows, pair)
    total, incoming = lax.optimization_barrier((total, incoming))
    new_moments_a, new_moments_b, step_a, step_b = pl.pallas_call(
        adam,
        out_shape=(
            shape(input_moments.shape, f32),
            shape(output_moments.shape, f32),
            shape(adapter_input_factors.shape, f32),
            shape(adapter_output_factors.shape, f32),
        ),
        in_specs=[SMEM, WHOLE, WHOLE, WHOLE, WHOLE],
        out_specs=(WHOLE,) * 4,
        compiler_params=params(24),
        name="adam",
    )(me.reshape(1), totals, incoming, input_moments, output_moments)

    rows = tok // 2
    wide_rows = pl.BlockSpec((rows, hid), lambda step, y_ref: (step, 0))
    grad_gate, grad_up = pl.pallas_call(
        finish,
        out_shape=(shape((tok, hid), bf16), shape((tok, hid), bf16)),
        grid_spec=pltpu.PrefetchScalarGridSpec(
            num_scalar_prefetch=1,
            grid=(tok // rows,),
            in_specs=[
                fixed(Z_HI, cut, feat),
                fixed(Z_HI, tok - cut, feat),
                pl.BlockSpec(
                    (hid, Z_HI * feat), lambda step, y_ref: (0, lax.rem(y_ref[0] + 2, Y))
                ),
                wide_rows,
                wide_rows,
                wide_rows,
            ],
            out_specs=[wide_rows, wide_rows],
            scratch_shapes=[pltpu.VMEM((Z_HI, rows, feat), bf16)],
        ),
        compiler_params=params(56),
        name="finish",
    )(y_s, far_low, far_high, down_full, total, gate_logits, up_projected)
    return (grad_gate, grad_up, new_moments_a, new_moments_b, step_a, step_b)


def solution(mesh):
    placed = (
        P("dp", "tensor"),
        P("dp", "tensor"),
        P("dp", "tensor"),
        P("tensor", "dp"),
        P("dp", None, "tensor"),
        P("dp", None, "tensor"),
        P(None, "dp", None, "tensor"),
        P(None, "dp", None, "tensor"),
        P("dp"),
        P(),
    )
    return jax.shard_map(
        shards,
        mesh=mesh,
        in_specs=placed,
        out_specs=(
            P("dp", "tensor"),
            P("dp", "tensor"),
            P(None, "dp", None, "tensor"),
            P(None, "dp", None, "tensor"),
            P("dp", None, "tensor"),
            P("dp", None, "tensor"),
        ),
        check_vma=False,
    )
```
